32 devices in a mesh: rep: 2 (over x), shard: 16 (over z, y, core).
Axes of the slice: x: 2, y: 2, z: 4, core: 2. Of those that a mesh axis runs over, the one named last changes fastest.
Arguments:
- tokens: bfloat16 [2, 32, 256, 960], P(None, ('rep', 'shard')), may hold values from -6 to 6
- cotangent: bfloat16 [2, 32, 256, 960], P(None, ('rep', 'shard')), may hold values from -6 to 6
- attn_gain: bfloat16 [960], P('shard'), may hold values from 0.099609375 to 1.8984375
- w_query: bfloat16 [960, 960], P('shard'), may hold values from -0.1875 to 0.1875
- w_key: bfloat16 [960, 320], P('shard'), may hold values from -0.1875 to 0.1875
- w_value: bfloat16 [960, 320], P('shard'), may hold values from -0.1875 to 0.1875
- w_out: bfloat16 [960, 960], P('shard'), may hold values from -0.75 to 0.75
- mlp_gain: bfloat16 [960], P('shard'), may hold values from 0.099609375 to 1.8984375
- w_gate: bfloat16 [960, 2560], P('shard'), may hold values from -0.1875 to 0.1875
- w_up: bfloat16 [960, 2560], P('shard'), may hold values from -0.1875 to 0.1875
- w_down: bfloat16 [2560, 960], P('shard'), may hold values from -0.125 to 0.125
Outputs:
- output: bfloat16 [2, 32, 256, 960], P(None, ('rep', 'shard'))
- grad_tokens: bfloat16 [2, 32, 256, 960], P(None, ('rep', 'shard'))
- grad_attn_gain: float32 [960], P('shard')
- grad_query: float32 [960, 960], P('shard')
- grad_key: float32 [960, 320], P('shard')
- grad_value: float32 [960, 320], P('shard')
- grad_out: float32 [960, 960], P('shard')
- grad_mlp_gain: float32 [960], P('shard')
- grad_gate: float32 [960, 2560], P('shard')
- grad_up: float32 [960, 2560], P('shard')
- grad_down: float32 [2560, 960], P('shard')
The draws below stay inside these ranges and needn't reach their ends.
All inputs are finite; a program needn't handle non-finite values.
Results may differ from the reference program's by a relative error of at most 0.015.
Values may be sent and summed in bfloat16 or wider, within the bound.
No kernel may reach another device: no remote copies, remote signals or barrier semaphores. Data moves between devices by JAX's collectives and lax.ppermute only.
A program may use at most 192 MiB of HBM per device.

```python
import math
import jax
import jax.numpy as jnp
from jax import lax

D = 960
HQ = 15
KV = 5
HD = 64
FF = 2560
SEQ = 256
MICRO = 2
SEQUENCES = 32


def with_spikes(drawn, rng, source, target, blocks, factor):
    def block_of(axis_at):
        return (jnp.arange(drawn.shape[axis_at]) // (drawn.shape[axis_at] // blocks)).reshape((-1,) + (1,) * (drawn.ndim - 1 - axis_at))

    first = jax.random.permutation(rng, blocks)[block_of(target)]
    other_side = (block_of(target) + blocks // 2) % blocks
    return jnp.where((block_of(source) == first) | (block_of(source) == other_side), factor * drawn, drawn)


def level_of(key, extent, split, low, largest):
    def one(position, blocks):
        steps = jax.random.uniform(jax.random.fold_in(jax.random.fold_in(key, 6), position), (blocks,), jnp.float32, low / len(split), largest / len(split))
        return jnp.repeat(jnp.exp(steps), extent[position] // blocks).reshape((-1,) + (1,) * (len(extent) - position - 1))

    level = one(*split[0])
    for cut in split[1:]:
        level = level * one(*cut)
    return level


def scatter_about(key, extent, spread, bound, cuts=(), dtype=jnp.bfloat16):
    values = spread * jax.random.normal(key, extent, jnp.float32)
    if cuts:
        values = values * level_of(key, extent, cuts, -0.22, 0.18)
    return jnp.clip(values, -bound, bound).astype(dtype)


def heavy_noise(rng, shape, width, reach, cuts, heavy, dtype=jnp.bfloat16):
    drawn = width * jax.random.normal(rng, shape, jnp.float32)
    if cuts:
        drawn = drawn * level_of(rng, shape, cuts, -0.22, 0.18)
    return jnp.clip(with_spikes(drawn, jax.random.fold_in(rng, 3), *heavy), -reach, reach).astype(dtype)


def setup_inputs(seed: int = 0) -> dict:
    seeds = jax.random.split(jax.random.key(seed), 12)
    return {
        "tokens": scatter_about(seeds[0], (MICRO, SEQUENCES, SEQ, D), 1.0, 6.0, ((1, 32),)),
        "cotangent": heavy_noise(seeds[1], (MICRO, SEQUENCES, SEQ, D), 1.0, 6.0, ((1, 32),), (1, 3, 32, 2.75)),
        "attn_gain": jnp.clip(1.0 + 0.18 * jax.random.normal(seeds[2], (D,), jnp.float32), 0.099609375, 1.8984375).astype(jnp.bfloat16),
        "w_query": scatter_about(seeds[3], (D, HQ * HD), D ** -0.5, 0.1875, ((0, 16),)),
        "w_key": scatter_about(seeds[4], (D, KV * HD), D ** -0.5, 0.1875, ((0, 16),)),
        "w_value": scatter_about(seeds[5], (D, KV * HD), D ** -0.5, 0.1875, ((0, 16),)),
        "w_out": scatter_about(seeds[6], (HQ * HD, D), (HQ * HD * 16 // SEQ) ** -0.5, 0.75, ((0, 16),)),
        "mlp_gain": jnp.clip(1.0 + 0.18 * jax.random.normal(seeds[7], (D,), jnp.float32), 0.099609375, 1.8984375).astype(jnp.bfloat16),
        "w_gate": scatter_about(seeds[8], (D, FF), D ** -0.5, 0.1875, ((0, 16),)),
        "w_up": scatter_about(seeds[9], (D, FF), D ** -0.5, 0.1875, ((0, 16),)),
        "w_down": scatter_about(seeds[10], (FF, D), FF ** -0.5, 0.125, ((0, 16),)),
    }


@jax.custom_vjp
def low(v):
    return lax.optimization_barrier(v.astype(jnp.bfloat16)).astype(jnp.float32)

@jax.custom_vjp
def low_back(v):
    return v

def low_keep(v):
    return (low(v), None)

def low_pass(kept, grad):
    return (grad,)

def back_keep(v):
    return (v, None)

def back_low(kept, grad):
    return (low(grad),)
low.defvjp(low_keep, low_pass)
low_back.defvjp(back_keep, back_low)
precise = lax.Precision.HIGHEST
EPSILON = 1e-05
THETA = 100000.0

def rms_scale(values, gain_row):
    return values * lax.rsqrt(lax.optimization_barrier(jnp.mean(values * values, axis=-1, keepdims=True)) + EPSILON) * gain_row

def rotation(length, head_width):
    positions = jnp.arange(length).astype(jnp.float32)
    frequency = THETA ** (-2.0 * jnp.arange(head_width // 2).astype(jnp.float32) / head_width)
    angles = positions[:, None] * frequency[None, :]
    return (jnp.cos(angles), jnp.sin(angles))

def rotate(vectors, cosine, sine_table):
    half_width = vectors.shape[-1] // 2
    first_half = vectors[..., :half_width]
    second = vectors[..., half_width:]
    cos_wide = cosine[None, :, None, :]
    sin_wide = sine_table[None, :, None, :]
    return jnp.concatenate([first_half * cos_wide - second * sin_wide, second * cos_wide + first_half * sin_wide], axis=-1)

def forward(inputs, attn_gain, w_query, w_key, w_value, w_out, mlp_gain, w_gate, w_up, w_down):
    batch_size, length, features = inputs.shape
    groups = HQ // KV
    cosine, sine_table = rotation(length, HD)
    normed = low(rms_scale(inputs, attn_gain))
    query_pre = low_back(jnp.einsum('bsd,de->bse', normed, w_query, precision=precise))
    key_pre = low_back(jnp.einsum('bsd,de->bse', normed, w_key, precision=precise))
    value_pre = low_back(jnp.einsum('bsd,de->bse', normed, w_value, precision=precise))
    queries = low(rotate(query_pre.reshape(batch_size, length, HQ, HD), cosine, sine_table))
    key_rows = low(rotate(key_pre.reshape(batch_size, length, KV, HD), cosine, sine_table))
    value_rows = low(value_pre.reshape(batch_size, length, KV, HD))
    queries = queries.reshape(batch_size, length, KV, groups, HD)
    raw_scores = low_back(jnp.einsum('bqgrd,bkgd->bgrqk', queries, key_rows, precision=precise))
    scores = raw_scores * (1.0 / math.sqrt(HD))
    causal = jnp.arange(length)[:, None] >= jnp.arange(length)[None, :]
    scores = jnp.where(causal, scores, -1e+30)
    row_max = lax.optimization_barrier(jnp.max(scores, axis=-1, keepdims=True))
    exponent = jnp.exp(scores - row_max)
    probability = exponent / lax.optimization_barrier(jnp.sum(exponent, axis=-1, keepdims=True))
    probs_low = low(probability)
    context = jnp.einsum('bgrqk,bkgd->bqgrd', probs_low, value_rows, precision=precise)
    context = low(low_back(context.reshape(batch_size, length, HQ * HD)))
    mixed_rows = inputs + low_back(jnp.einsum('bse,ed->bsd', context, w_out, precision=precise))
    normed_two = low(rms_scale(mixed_rows, mlp_gain))
    gate_pre = low_back(jnp.einsum('bsd,de->bse', normed_two, w_gate, precision=precise))
    up_pre = low_back(jnp.einsum('bsd,de->bse', normed_two, w_up, precision=precise))
    hidden = low(jax.nn.silu(gate_pre) * up_pre)
    return mixed_rows + low_back(jnp.einsum('bse,ed->bsd', hidden, w_down, precision=precise))

def reference(tokens, cotangent, attn_gain, w_query, w_key, w_value, w_out, mlp_gain, w_gate, w_up, w_down):
    seq_total = MICRO * SEQUENCES
    group_size = math.gcd(seq_total, max(1, 4096 // SEQ))
    step_count = seq_total // group_size
    flat_in = tokens.reshape(step_count, group_size, SEQ, D)
    flat_cot = cotangent.reshape(step_count, group_size, SEQ, D)
    weights = tuple((weight.astype(jnp.float32) for weight in (attn_gain, w_query, w_key, w_value, w_out, mlp_gain, w_gate, w_up, w_down)))

    def one_step(running, pieces):
        inputs, cot_piece = pieces
        result, pullback = jax.vjp(forward, inputs.astype(jnp.float32), *weights)
        gradients = pullback(cot_piece.astype(jnp.float32))
        updated = tuple((held_sum + addend for held_sum, addend in zip(running, gradients[1:])))
        return (updated, (result.astype(jnp.bfloat16), gradients[0].astype(jnp.bfloat16)))
    zero_sums = tuple((jnp.zeros(weight.shape, jnp.float32) for weight in weights))
    grad_sums, (outputs, grad_inputs) = lax.scan(one_step, zero_sums, (flat_in, flat_cot))
    return (outputs.reshape(tokens.shape), grad_inputs.reshape(tokens.shape), grad_sums[0], grad_sums[1], grad_sums[2], grad_sums[3], grad_sums[4], grad_sums[5], grad_sums[6], grad_sums[7], grad_sums[8])
```

```python
import math

import jax
import jax.numpy as jnp
import numpy as np
from jax import lax
from jax.sharding import PartitionSpec as P

HQ = 15
KV = 5
HD = 64
EPSILON = 1e-05
THETA = 100000.0
F32 = jnp.float32
BF16 = jnp.bfloat16


def rotation(length):
    positions = jnp.arange(length).astype(F32)
    frequency = THETA ** (-2.0 * jnp.arange(HD // 2).astype(F32) / HD)
    angles = positions[:, None] * frequency[None, :]
    return jnp.cos(angles), jnp.sin(angles)


def rotate(vectors, cosine, sine):
    half = vectors.shape[-1] // 2
    first, second = vectors[..., :half], vectors[..., half:]
    cos_wide, sin_wide = cosine[None, :, None, :], sine[None, :, None, :]
    return jnp.concatenate(
        [first * cos_wide - second * sin_wide, second * cos_wide + first * sin_wide], axis=-1
    )


def dot(a, b, contract):
    return lax.dot_general(a, b, (contract, ((), ())), preferred_element_type=F32)


NN = ((1,), (0,))
NT = ((1,), (1,))
TN = ((0,), (0,))


class Layout:
    def __init__(self, shards):
        self.shards = shards
        self.chips = shards // 2
        self.bits = self.chips.bit_length() - 1
        self.order = list(range(self.bits))[::-1]
        off = []
        for index in range(self.chips):
            off.append(sum(((index >> k) & 1) << b for k, b in enumerate(self.order)))
        self.off = np.array(off)

    def swap_bit(self, array, bit):
        pairs = [(s, s ^ (2 << bit)) for s in range(self.shards)]
        return lax.ppermute(array, "shard", pairs)

    def swap_core(self, array):
        return lax.ppermute(array, "shard", [(s, s ^ 1) for s in range(self.shards)])

    def gather(self, piece, axis):
        for bit in self.order:
            piece = jnp.concatenate([piece, self.swap_bit(piece, bit)], axis=axis)
        return piece

    def reduce(self, blocks, axis):
        for bit in self.order[::-1]:
            half = blocks.shape[axis] // 2
            keep = lax.slice_in_dim(blocks, 0, half, axis=axis)
            send = lax.slice_in_dim(blocks, half, 2 * half, axis=axis)
            got = self.swap_bit(send, bit)
            blocks = (keep.astype(F32) + got.astype(F32)).astype(BF16)
        other = lax.ppermute(blocks, "rep", [(0, 1), (1, 0)])
        return blocks.astype(F32) + other.astype(F32)


def on_device(
    tokens, cotangent, attn_gain, w_query, w_key, w_value, w_out, mlp_gain, w_gate, w_up, w_down
):
    shards = lax.axis_size("shard")
    lay = Layout(shards)
    chips = lay.chips
    me = lax.axis_index("shard")
    core, chip = me % 2, me // 2
    micro, batch, length, features = tokens.shape
    seqs = micro * batch
    rows = seqs * length
    dr = features // shards
    pr = -(-(dr + 1) // 16) * 16
    fr = w_down.shape[0]
    half_ff = chips * fr
    nq, nk = HQ * HD, KV * HD
    nqkv = nq + 2 * nk
    wide = -(-(nqkv + 2) // 128) * 128
    half_rows = chips * pr
    cosine, sine = rotation(length)
    groups = HQ // KV

    def grow(block):
        return jnp.pad(block, ((0, pr - dr), (0, 0)))

    gains = jnp.stack([attn_gain, mlp_gain], axis=1)
    attn_piece = grow(
        jnp.concatenate(
            [w_query, w_key, w_value, gains, jnp.zeros((dr, wide - nqkv - 2), BF16), w_out], axis=1
        )
    )

    def by_core(w):
        return w.reshape(dr, chips, 2, fr).transpose(2, 0, 1, 3).reshape(2, dr, half_ff)

    both = jnp.concatenate([by_core(w_gate), by_core(w_up)], axis=2)
    both = jnp.pad(both, ((0, 0), (0, pr - dr), (0, 0)))
    mine = lax.dynamic_index_in_dim(both, core, 0, keepdims=False)
    theirs = lax.dynamic_index_in_dim(both, 1 - core, 0, keepdims=False)
    gate_up_piece = jnp.stack([mine, lay.swap_core(theirs)])

    attn_own = lay.gather(attn_piece[None], 0)
    attn_all = jnp.concatenate([attn_own, lay.swap_core(attn_own)], axis=0)
    attn_all = attn_all.reshape(2 * half_rows, wide + features)
    w_qkv = attn_all[:, :nqkv]
    w_o = attn_all[:, wide:]
    w_gu = lay.gather(gate_up_piece[:, None], 1).reshape(2 * half_rows, 2 * half_ff)
    down_rel = lay.gather(w_down[None], 0)
    inverse = jnp.asarray(np.argsort(lay.off), jnp.int32)
    spots = inverse[jnp.arange(chips) ^ chip]
    w_d = jnp.concatenate(
        [lax.dynamic_index_in_dim(down_rel, spots[k], 0, keepdims=False) for k in range(chips)], 0
    )

    flip = np.concatenate([2 * lay.off, 2 * lay.off + 1])
    flip = jnp.asarray(np.repeat(flip, pr), jnp.int32)
    inside = jnp.asarray(np.tile(np.arange(pr), shards), jnp.int32)
    feat = jnp.where(inside < dr, (me ^ flip) * dr + inside, -1)
    spread = (jnp.arange(features)[:, None] == feat[None, :]).astype(BF16)

    gain_rows = dot(attn_all[:, nqkv : nqkv + 2], spread, ((0,), (1,)))
    gain_one, gain_two = gain_rows[0:1], gain_rows[1:2]

    def other_way(rel):
        return jnp.concatenate([rel[:, half_rows:], rel[:, :half_rows]], axis=1)

    x = tokens.reshape(rows, features).astype(F32)
    cot = cotangent.reshape(rows, features)
    cot_both = jnp.concatenate([cot, lay.swap_core(cot)], axis=0)
    r1 = lax.rsqrt(jnp.mean(x * x, axis=-1, keepdims=True) + EPSILON)
    normed = (x * r1 * gain_one).astype(BF16)
    normed_rel = dot(normed, spread, NN).astype(BF16)
    normed_other = lay.swap_core(normed_rel[:, half_rows:])
    qkv = dot(normed_rel, w_qkv, NN)
    queries = rotate(qkv[:, :nq].reshape(seqs, length, HQ, HD), cosine, sine).astype(BF16)
    queries = queries.reshape(seqs, length, KV, groups, HD)
    keys = rotate(qkv[:, nq : nq + nk].reshape(seqs, length, KV, HD), cosine, sine).astype(BF16)
    values = qkv[:, nq + nk :].astype(BF16).reshape(seqs, length, KV, HD)
    scores = jnp.einsum("bqgrd,bkgd->bgrqk", queries, keys, preferred_element_type=F32)
    causal = jnp.arange(length)[:, None] >= jnp.arange(length)[None, :]
    scores = jnp.where(causal, scores * (1.0 / math.sqrt(HD)), -1e30)
    exponent = jnp.exp(scores - jnp.max(scores, axis=-1, keepdims=True))
    probs = exponent / jnp.sum(exponent, axis=-1, keepdims=True)
    probs_low = probs.astype(BF16)
    context = jnp.einsum("bgrqk,bkgd->bqgrd", probs_low, values, preferred_element_type=F32)
    context = context.astype(BF16).reshape(rows, nq)
    context_rel = dot(context, spread, NN).astype(BF16)
    context_other = lay.swap_core(context_rel[:, half_rows:])
    mixed = x + dot(context_rel, w_o, NN)
    r2 = lax.rsqrt(jnp.mean(mixed * mixed, axis=-1, keepdims=True) + EPSILON)
    normed_two = (mixed * r2 * gain_two).astype(BF16)
    two_rel = dot(normed_two, spread, NN).astype(BF16)
    two_both = jnp.concatenate([two_rel, other_way(lay.swap_core(two_rel))], axis=0)
    gate_up = dot(two_both, w_gu, NN)
    gate, up = gate_up[:, :half_ff], gate_up[:, half_ff:]
    sg = jax.nn.sigmoid(gate)
    silu = gate * sg
    hidden = (silu * up).astype(BF16)
    out_part = dot(hidden, w_d, NN)
    out_other = lay.swap_core(out_part[rows:].astype(BF16))
    output = (mixed + out_part[:rows] + out_other.astype(F32)).astype(BF16)

    grad_down = dot(hidden, cot_both, TN).astype(BF16).reshape(chips, fr, features)
    places = chip ^ jnp.asarray(lay.off, jnp.int32)
    grad_down = jnp.stack(
        [lax.dynamic_index_in_dim(grad_down, places[k], 0, keepdims=False) for k in range(chips)]
    )
    grad_down = lay.reduce(grad_down, 0)[0]
    d_hidden = dot(cot_both, w_d, NT)
    d_gate = (d_hidden * up * sg * (1.0 + gate * (1.0 - sg))).astype(BF16)
    d_up = (d_hidden * silu).astype(BF16)
    d_gu = jnp.concatenate([d_gate, d_up], axis=1)
    grad_gu = dot(two_both, d_gu, TN).astype(BF16).reshape(2, chips, pr, 2 * half_ff)
    grad_gu = lay.reduce(grad_gu, 1)[:, 0, :dr]
    theirs = lay.swap_core(grad_gu[1].astype(BF16))
    mine = grad_gu[0]
    d_two_part = dot(d_gu, w_gu, NT)
    d_two_other = lay.swap_core(d_two_part[rows:].astype(BF16))
    d_two_rel = d_two_part[:rows] + other_way(d_two_other).astype(F32)
    d_two = dot(d_two_rel.astype(BF16), spread, NT)
    grad_gain_two = jnp.sum(d_two * mixed * r2, axis=0)
    e2 = d_two * gain_two
    d_mixed = cot.astype(F32) + r2 * (
        e2 - mixed * r2 * r2 * jnp.mean(e2 * mixed, axis=-1, keepdims=True)
    )
    d_attn = d_mixed.astype(BF16)

    attn_both = jnp.concatenate([d_attn, lay.swap_core(d_attn)], axis=0)
    context_both = jnp.concatenate([context_rel[:, :half_rows], context_other], axis=0)
    grad_out = dot(context_both, attn_both, TN).astype(BF16).reshape(chips, pr, features)
    grad_out = lay.reduce(grad_out, 0)[0, :dr]
    d_context = dot(dot(d_attn, w_o, NT).astype(BF16), spread, NT).astype(BF16)
    d_context = d_context.reshape(seqs, length, KV, groups, HD)
    d_probs = jnp.einsum("bqgrd,bkgd->bgrqk", d_context, values, preferred_element_type=F32)
    inner = jnp.sum(d_probs * probs, axis=-1, keepdims=True)
    d_scores = (probs * (d_probs - inner) * (1.0 / math.sqrt(HD))).astype(BF16)
    d_values = jnp.einsum("bgrqk,bqgrd->bkgd", probs_low, d_context, preferred_element_type=F32)
    d_queries = jnp.einsum("bgrqk,bkgd->bqgrd", d_scores, keys, preferred_element_type=F32)
    d_keys = jnp.einsum("bgrqk,bqgrd->bkgd", d_scores, queries, preferred_element_type=F32)
    d_queries = rotate(d_queries.reshape(seqs, length, HQ, HD), cosine, -sine)
    d_keys = rotate(d_keys, cosine, -sine)
    d_qkv = jnp.concatenate(
        [
            d_queries.astype(BF16).reshape(rows, nq),
            d_keys.astype(BF16).reshape(rows, nk),
            d_values.astype(BF16).reshape(rows, nk),
        ],
        axis=1,
    )
    d_normed_rel = dot(d_qkv, w_qkv, NT)
    d_normed = dot(d_normed_rel.astype(BF16), spread, NT)
    grad_gain_one = jnp.sum(d_normed * x * r1, axis=0)
    e1 = d_normed * gain_one
    grad_tokens = (
        d_mixed + r1 * (e1 - x * r1 * r1 * jnp.mean(e1 * x, axis=-1, keepdims=True))
    ).astype(BF16)

    qkv_both = jnp.concatenate([d_qkv, lay.swap_core(d_qkv)], axis=0)
    normed_both = jnp.concatenate([normed_rel[:, :half_rows], normed_other], axis=0)
    grad_gains = jnp.stack([grad_gain_one, grad_gain_two], axis=1).astype(BF16)
    grad_gains = dot(spread, grad_gains, TN)
    grad_gains = grad_gains[:half_rows] + lay.swap_core(grad_gains[half_rows:].astype(BF16))
    grad_attn = dot(normed_both, qkv_both, TN)
    grad_attn = jnp.concatenate(
        [grad_attn, grad_gains, jnp.zeros((half_rows, wide - nqkv - 2), F32)], axis=1
    )
    grad_attn = grad_attn.astype(BF16).reshape(chips, pr, wide)
    grad_attn = lay.reduce(grad_attn, 0)[0, :dr]

    pair = jnp.where(core == 0, jnp.stack([mine, theirs.astype(F32)]), jnp.stack([theirs.astype(F32), mine]))
    pair = pair.reshape(2, dr, 2, chips, fr).transpose(2, 1, 3, 0, 4).reshape(2, dr, 2 * half_ff)
    shape = tokens.shape
    return (
        output.reshape(shape),
        grad_tokens.reshape(shape),
        grad_attn[:, nqkv],
        grad_attn[:, :nq],
        grad_attn[:, nq : nq + nk],
        grad_attn[:, nq + nk : nqkv],
        grad_out,
        grad_attn[:, nqkv + 1],
        pair[0],
        pair[1],
        grad_down,
    )


def solution(mesh):
    data = P(None, ("rep", "shard"), None, None)
    vector, matrix = P("shard"), P("shard", None)
    weights = (vector, matrix, matrix, matrix, matrix, vector, matrix, matrix, matrix)
    return jax.shard_map(
        on_device,
        mesh=mesh,
        in_specs=(data, data) + weights,
        out_specs=(data, data) + weights,
        check_vma=False,
    )
```

```python
import functools
import math

import jax
import jax.numpy as jnp
import numpy as np
from jax import lax
from jax.experimental import pallas as pl
from jax.experimental.pallas import tpu as pltpu
from jax.sharding import PartitionSpec as P

HQ = 15
KV = 5
HD = 64
EPSILON = 1e-05
THETA = 100000.0
F32 = jnp.float32
BF16 = jnp.bfloat16
LANES = 128
COLS = 256
NN = ((1,), (0,))
NT = ((1,), (1,))
TN = ((0,), (0,))
VMEM = 56 << 20


def dot(a, b, contract=NN):
    return lax.dot_general(a, b, (contract, ((), ())), preferred_element_type=F32)


def params():
    return pltpu.CompilerParams(vmem_limit_bytes=VMEM)


def cost(flops, nbytes):
    return pl.CostEstimate(flops=int(flops), bytes_accessed=int(nbytes), transcendentals=0)


def shape(dims, dtype=BF16):
    return jax.ShapeDtypeStruct(dims, dtype)


def whole(*dims):
    return pl.BlockSpec(dims, lambda *_: (0,) * len(dims))


def once(*dims):
    return pl.BlockSpec(dims, lambda *_: (0,) * len(dims), pipeline_mode=pl.Buffered(1))


def tables(length):
    positions = jnp.arange(length).astype(F32)
    frequency = THETA ** (-2.0 * jnp.arange(HD // 2).astype(F32) / HD)
    angles = positions[:, None] * frequency[None, :]
    cosine, sine = jnp.cos(angles), jnp.sin(angles)
    return jnp.tile(cosine, (1, 4)), jnp.concatenate([-sine, sine, -sine, sine], axis=1)


def turn(tile, cosine, sine, low):
    other = jnp.where(low, pltpu.roll(tile, LANES - 32, 1), pltpu.roll(tile, 32, 1))
    return tile * cosine + other * sine


def placed(tile, half):
    lane = lax.broadcasted_iota(jnp.int32, tile.shape, 1)
    alone = jnp.where((lane >= HD) == (half == 1), tile, 0.0)
    moved = pltpu.roll(alone, HD, 1)
    pair = (moved, alone) if half else (alone, moved)
    return [one.astype(BF16) for one in pair]


def attention_forward(
    x_ref, own_ref, oth_ref, gain_ref, attn_order_ref, mlp_order_ref, cos_ref, sin_ref,
    two_ref, keep_ref, send_ref, qkv_ref, probs_ref, mixed_ref, *, wide
):
    length, features = x_ref.shape
    half = own_ref.shape[0]
    x = x_ref[...].astype(F32)
    r1 = lax.rsqrt(jnp.mean(x * x, axis=-1, keepdims=True) + EPSILON)
    normed = (x * r1 * gain_ref[0:1, :]).astype(BF16)
    to_order = attn_order_ref[:, :features]
    spread = dot(normed, to_order, NT).astype(BF16)
    left, right = spread[:, :half], spread[:, half:]
    spread = dot(to_order, normed, NT).astype(BF16)
    keep_ref[:half, :] = spread[:half]
    send_ref[2 * half : 3 * half, :] = spread[half:]
    lane = lax.broadcasted_iota(jnp.int32, (length, LANES), 1)
    low = lane % HD < HD // 2
    cosine, sine = cos_ref[...], sin_ref[...]
    tiles, heads = [], {}
    for t in range(wide // LANES):
        cols = slice(t * LANES, (t + 1) * LANES)
        tile = dot(left, own_ref[:, cols]) + dot(right, oth_ref[:, cols])
        if t * 2 < HQ + KV:
            tile = turn(tile, cosine, sine, low)
        if t == wide // LANES - 1:
            tile = jnp.where(lane < HD, tile, 0.0)
        short = tile.astype(BF16)
        qkv_ref[:, cols] = short
        tiles.append(short)
        for n in (2 * t, 2 * t + 1):
            if HQ <= n < HQ + 2 * KV:
                heads[n] = placed(tile, n % 2)
    causal = lax.broadcasted_iota(jnp.int32, (length, length), 0) >= lax.broadcasted_iota(
        jnp.int32, (length, length), 1
    )
    context = [None] * ((HQ + 1) // 2)
    for h in range(HQ):
        j, t, s = h // (HQ // KV), h // 2, h % 2
        scores = dot(tiles[t], heads[HQ + j][s], NT) * (1.0 / math.sqrt(HD))
        scores = jnp.where(causal, scores, -1e30)
        exponent = jnp.exp(scores - jnp.max(scores, axis=-1, keepdims=True))
        probs = exponent * (1.0 / jnp.sum(exponent, axis=-1, keepdims=True))
        probs = probs.astype(BF16)
        probs_ref[0, h] = probs
        part = dot(probs, heads[HQ + KV + j][s])
        context[t] = part if context[t] is None else context[t] + part
    context = jnp.concatenate([c.astype(BF16) for c in context], axis=1)
    spread = dot(context, attn_order_ref[...], NT).astype(BF16)
    mixed = x + dot(spread[:, :half], own_ref[:, wide:]) + dot(spread[:, half:], oth_ref[:, wide:])
    spread = dot(attn_order_ref[...], context, NT).astype(BF16)
    keep_ref[half:, :] = spread[:half]
    send_ref[3 * half :, :] = spread[half:]
    mixed_ref[...] = mixed
    r2 = lax.rsqrt(jnp.mean(mixed * mixed, axis=-1, keepdims=True) + EPSILON)
    two = (mixed * r2 * gain_ref[1:2, :]).astype(BF16)
    to_order = mlp_order_ref[:, :features]
    two_ref[...] = dot(two, to_order, NT).astype(BF16)
    send_ref[: 2 * half, :] = dot(to_order, two, NT).astype(BF16)


def attention_backward(
    d_attn_ref, own_ref, oth_ref, order_ref, qkv_ref, probs_ref, cos_ref, sin_ref, d_qkv_ref, *, wide
):
    length = d_attn_ref.shape[0]
    d_attn = d_attn_ref[...]
    d_context = jnp.concatenate(
        [
            dot(d_attn, own_ref[:, wide:], NT).astype(BF16),
            dot(d_attn, oth_ref[:, wide:], NT).astype(BF16),
        ],
        axis=1,
    )
    d_context = dot(d_context, order_ref[...]).astype(BF16)
    lane = lax.broadcasted_iota(jnp.int32, (length, LANES), 1)
    low = lane % HD < HD // 2
    cosine, sine = cos_ref[...], -sin_ref[...]

    def tile_of(n):
        t = n // 2
        return qkv_ref[:, t * LANES : (t + 1) * LANES]

    d_tiles = [None] * ((HQ + 2 * KV + 1) // 2)

    def add(t, part):
        d_tiles[t] = part if d_tiles[t] is None else d_tiles[t] + part

    groups = HQ // KV
    for j in range(KV):
        keys = placed(tile_of(HQ + j).astype(F32), (HQ + j) % 2)
        values = placed(tile_of(HQ + KV + j).astype(F32), (HQ + KV + j) % 2)
        d_key, d_value = [None, None], [None, None]
        for h in range(j * groups, (j + 1) * groups):
            t, s = h // 2, h % 2
            d_con = d_context[:, t * LANES : (t + 1) * LANES]
            probs = probs_ref[0, h]
            wide_probs = probs.astype(F32)
            d_probs = dot(d_con, values[s], NT)
            inner = jnp.sum(d_probs * wide_probs, axis=-1, keepdims=True)
            d_scores = (wide_probs * (d_probs - inner) * (1.0 / math.sqrt(HD))).astype(BF16)
            add(t, dot(d_scores, keys[s]))
            part = dot(d_scores, tile_of(h), TN)
            d_key[s] = part if d_key[s] is None else d_key[s] + part
            part = dot(probs, d_con, TN)
            d_value[s] = part if d_value[s] is None else d_value[s] + part
        for n, pair in ((HQ + j, d_key), (HQ + KV + j, d_value)):
            here = n % 2
            mask = (lane >= HD) == (here == 1)
            total = jnp.where(mask, pair[here] + pltpu.roll(pair[1 - here], HD, 1), 0.0)
            add(n // 2, total)
    for t, tile in enumerate(d_tiles):
        if t * 2 < HQ + KV:
            tile = turn(tile, cosine, sine, low)
        d_qkv_ref[:, t * LANES : (t + 1) * LANES] = tile.astype(BF16)


def flipped(array, axis, block):
    n = array.shape[axis] // block
    parts = [lax.slice_in_dim(array, i * block, (i + 1) * block, axis=axis) for i in range(n)]
    return jnp.concatenate([parts[i ^ 1] for i in range(n)], axis=axis)


def gate_up_kernel(own_ref, oth_ref, *refs):
    gates, ups = refs[:8], refs[8:16]
    hidden_ref, a_ref, b_ref = refs[16:]
    wg = jnp.concatenate([r[c].reshape(-1, COLS) for i in range(4) for c in (0, 1) for r in gates[2 * i : 2 * i + 2]], axis=0)
    wu = jnp.concatenate([r[c].reshape(-1, COLS) for i in range(4) for c in (0, 1) for r in ups[2 * i : 2 * i + 2]], axis=0)
    rows = own_ref.shape[0]
    block = wg.shape[0] // 8
    for at, acts in ((0, own_ref[...]), (rows, flipped(oth_ref[...], 1, block))):
        gate, up = dot(acts, wg), dot(acts, wu)
        sg = 1.0 / (1.0 + jnp.exp(-gate))
        silu = gate * sg
        hidden_ref[at : at + rows, :] = (silu * up).astype(BF16)
        a_ref[at : at + rows, :] = (up * sg * (1.0 + gate * (1.0 - sg))).astype(BF16)
        b_ref[at : at + rows, :] = silu.astype(BF16)


def d_gate_up_kernel(cot_ref, cot_oth_ref, w_ref, a_ref, b_ref, dg_ref, du_ref):
    rows = cot_ref.shape[0]
    for at, ref in ((0, cot_ref), (rows, cot_oth_ref)):
        d_hidden = dot(ref[...], w_ref[...], NT)
        dg_ref[at : at + rows, :] = (d_hidden * a_ref[at : at + rows, :].astype(F32)).astype(BF16)
        du_ref[at : at + rows, :] = (d_hidden * b_ref[at : at + rows, :].astype(F32)).astype(BF16)


def mlp_grad_kernel(own_ref, oth_ref, dg_ref, du_ref, *refs, count):
    alpha_ref, beta_ref = refs[-2:]
    rows, n = own_ref.shape[1], alpha_ref.shape[0]
    own, oth = own_ref[...], flipped(oth_ref[...], 0, n // 2)

    def put(ref):
        out = dot(own, ref[:rows, :]) + dot(oth, ref[rows:, :])
        alpha_ref[...] = out[:n].astype(BF16)
        beta_ref[...] = out[n:].astype(BF16)

    @pl.when(pl.program_id(0) < count)
    def _():
        put(dg_ref)

    @pl.when(pl.program_id(0) >= count)
    def _():
        put(du_ref)


def d_two_kernel(dg_ref, du_ref, *refs):
    gates, ups = refs[:8], refs[8:16]
    mine_ref, other_ref, total_ref = refs[-3:]
    wg = jnp.concatenate([r[c].reshape(-1, COLS) for i in range(4) for c in (0, 1) for r in gates[2 * i : 2 * i + 2]], axis=0)
    wu = jnp.concatenate([r[c].reshape(-1, COLS) for i in range(4) for c in (0, 1) for r in ups[2 * i : 2 * i + 2]], axis=0)
    part = dot(dg_ref[...], wg, NT) + dot(du_ref[...], wu, NT)
    step, rows = pl.program_id(0), mine_ref.shape[0]

    @pl.when(step == 0)
    def _():
        mine_ref[...] = part[:rows]
        total_ref[...] = part[rows:]

    @pl.when(step > 0)
    def _():
        mine_ref[...] += part[:rows]
        total_ref[...] += part[rows:]

    @pl.when(step == pl.num_programs(0) - 1)
    def _():
        other_ref[...] = flipped(total_ref[...].astype(BF16), 1, total_ref.shape[1] // 8)


def mixed_backward(mine_ref, other_ref, order_ref, mixed_ref, cot_ref, gain_ref, d_mixed_ref, d_attn_ref, grad_ref):
    features = mixed_ref.shape[1]
    total = (mine_ref[...] + other_ref[...].astype(F32)).astype(BF16)
    d_two = dot(total, order_ref[:, :features])
    mixed = mixed_ref[...]
    r2 = lax.rsqrt(jnp.mean(mixed * mixed, axis=-1, keepdims=True) + EPSILON)
    unit = mixed * r2
    e2 = d_two * gain_ref[1:2, :]
    d_mixed = cot_ref[...].astype(F32) + r2 * (e2 - unit * jnp.mean(e2 * unit, axis=-1, keepdims=True))
    d_mixed_ref[...] = d_mixed
    d_attn_ref[...] = d_mixed.astype(BF16)
    grad_ref[0] = jnp.sum(d_two * unit, axis=0, keepdims=True)


def token_backward(d_qkv_ref, own_ref, oth_ref, order_ref, x_ref, d_mixed_ref, gain_ref, out_ref, grad_ref, *, wide):
    features = x_ref.shape[1]
    d_qkv = d_qkv_ref[...]
    d_normed = jnp.concatenate(
        [
            dot(d_qkv, own_ref[:, :wide], NT).astype(BF16),
            dot(d_qkv, oth_ref[:, :wide], NT).astype(BF16),
        ],
        axis=1,
    )
    d_normed = dot(d_normed, order_ref[:, :features])
    x = x_ref[...].astype(F32)
    r1 = lax.rsqrt(jnp.mean(x * x, axis=-1, keepdims=True) + EPSILON)
    unit = x * r1
    e1 = d_normed * gain_ref[0:1, :]
    out = d_mixed_ref[...] + r1 * (e1 - unit * jnp.mean(e1 * unit, axis=-1, keepdims=True))
    out_ref[...] = out.astype(BF16)
    grad_ref[0] = jnp.sum(d_normed * unit, axis=0, keepdims=True)


def attn_grad_kernel(own_ref, oth_ref, rhs_ref, rhs_oth_ref, *refs, gain_at):
    out_refs = refs[-4:]
    out = dot(own_ref[...], rhs_ref[...]) + dot(oth_ref[...], rhs_oth_ref[...])
    if gain_at is not None:
        gains = dot(refs[1][...], refs[0][...], NT)
        lane = lax.broadcasted_iota(jnp.int32, out.shape, 1)
        out = out + jnp.where(lane == gain_at, gains[:, 0:1], 0.0)
        out = out + jnp.where(lane == gain_at + 1, gains[:, 1:2], 0.0)
    n = out_refs[0].shape[0]
    for i, ref in enumerate(out_refs):
        ref[...] = out[i * n : (i + 1) * n].astype(BF16)


def on_device(
    tokens, cotangent, attn_gain, w_query, w_key, w_value, w_out, mlp_gain, w_gate, w_up, w_down
):
    shards = lax.axis_size("shard")
    chips = shards // 2
    zs = chips // 2
    me, rep = lax.axis_index("shard"), lax.axis_index("rep")
    core = me % 2
    micro, batch, length, features = tokens.shape
    seqs = micro * batch
    rows = seqs * length
    dr = features // shards
    quarter = -(-dr // 4)
    qr = -(-quarter // 8) * 8
    width = shards * 4 * qr
    half = width // 2
    fr = w_down.shape[0]
    half_ff = chips * fr
    steps = half_ff // COLS
    nq, nk = HQ * HD, KV * HD
    nqkv = nq + 2 * nk
    wide = -(-(nqkv + 2) // LANES) * LANES
    cosine, sine = tables(length)

    def over(array, flip):
        return lax.ppermute(array, "shard", [(s, s ^ flip) for s in range(shards)])

    def over_core(array):
        return over(array, 1)

    def over_y(array):
        return over(array, 2)

    def over_rep(array):
        return lax.ppermute(array, "rep", [(0, 1), (1, 0)])

    def order(dims):
        sizes = {"core": 2, "split": 2, "f1": 2, "f2": 2, "z": zs, "row": qr}
        grid = np.meshgrid(*[np.arange(sizes[d]) for d in dims], indexing="ij")
        at = {d: g.reshape(-1) for d, g in zip(dims, grid)}
        x_flip = np.where(at["split"] == 0, at["f1"], at["f2"])
        y_flip = np.where(at["split"] == 0, at["f2"], at["f1"])
        shard = me ^ jnp.asarray(at["core"] + 2 * (y_flip + 2 * at["z"]), jnp.int32)
        part = 2 * (rep ^ jnp.asarray(x_flip, jnp.int32)) + jnp.asarray(at["split"], jnp.int32)
        inside = part * quarter + jnp.asarray(at["row"], jnp.int32)
        real = jnp.asarray(at["row"] < quarter) & (inside < dr)
        feat = jnp.where(real, shard * dr + inside, -1)
        columns = -(-features // LANES) * LANES
        return (feat[:, None] == jnp.arange(columns)[None, :]).astype(BF16)

    attn_order = order(("core", "f1", "split", "f2", "z", "row"))
    mlp_order = order(("f1", "split", "core", "f2", "z", "row"))

    def mine_of(w):
        pad = [(0, 0)] * (w.ndim - 2)
        w = jnp.pad(w, pad + [(0, 4 * quarter - dr), (0, 0)])
        w = w.reshape(w.shape[:-2] + (4, quarter, w.shape[-1]))
        w = lax.dynamic_slice_in_dim(w, 2 * rep, 2, axis=w.ndim - 3)
        return jnp.pad(w, pad + [(0, 0), (0, qr - quarter), (0, 0)])

    def gather(piece):
        parts = [piece] + [over(piece, 4 * z) for z in range(1, zs)]
        first, second = (jnp.stack([p[:, s] for p in parts], axis=1) for s in (0, 1))
        y_first, x_second = over_y(first), over_rep(second)
        x_first, y_second = over_rep(first), over_y(second)
        xy_first, xy_second = over_rep(y_first), over_y(x_second)
        return [first, y_first, second, x_second, x_first, xy_first, y_second, xy_second]

    gains = jnp.stack([attn_gain, mlp_gain], axis=1)
    blank = jnp.zeros((dr, wide - nqkv - 2), BF16)
    attn_piece = jnp.concatenate([w_query, w_key, w_value, gains, blank, w_out], axis=1)
    blocks = gather(mine_of(attn_piece[None]))
    attn_own = jnp.concatenate([b.reshape(half // 8, wide + features) for b in blocks], axis=0)
    attn_oth = over_core(attn_own)

    def by_core(w):
        return w.reshape(dr, chips, 2, fr).transpose(2, 0, 1, 3).reshape(2, dr, half_ff)

    both = mine_of(jnp.concatenate([by_core(w_gate), by_core(w_up)], axis=2))
    here = lax.dynamic_index_in_dim(both, core, 0, keepdims=False)
    there = lax.dynamic_index_in_dim(both, 1 - core, 0, keepdims=False)
    mlp = gather(jnp.stack([here, over_core(there)]))
    even = [[2 * k + c for k in range(chips)] for c in range(2)]
    w_d = lax.all_gather(w_down, "shard", axis=0, tiled=True, axis_index_groups=even)

    gain_cols = jnp.concatenate([attn_own[:, nqkv : nqkv + 2], attn_oth[:, nqkv : nqkv + 2]], axis=0)
    gain_rows = dot(gain_cols, attn_order[:, :features], TN)

    x = tokens.reshape(rows, features)
    cot = cotangent.reshape(rows, features)
    cot_oth = over_core(cot)
    by_rows = lambda cols: pl.BlockSpec((length, cols), lambda i: (i, 0))
    by_cols = lambda n: pl.BlockSpec((n, length), lambda i: (0, i))
    orders = whole(*attn_order.shape)
    two, keep_t, send_t, qkv, probs, mixed = pl.pallas_call(
        functools.partial(attention_forward, wide=wide),
        grid=(seqs,),
        in_specs=[
            by_rows(features), once(half, wide + features), once(half, wide + features),
            whole(2, features), once(*attn_order.shape), once(*attn_order.shape),
            whole(length, LANES), whole(length, LANES),
        ],
        out_specs=[
            by_rows(width), by_cols(width), by_cols(2 * width), by_rows(wide),
            pl.BlockSpec((1, HQ, length, length), lambda i: (i, 0, 0, 0)),
            by_rows(features),
        ],
        out_shape=[
            shape((rows, width)), shape((width, rows)), shape((2 * width, rows)), shape((rows, wide)),
            shape((seqs, HQ, length, length)), shape((rows, features), F32),
        ],
        compiler_params=params(),
        cost_estimate=cost(2 * rows * width * (wide + 6 * width), 30 << 20),
    )(x, attn_own, attn_oth, gain_rows, attn_order, mlp_order, cosine, sine)
    two_oth = over_core(two)
    got_t = over_core(send_t)

    def weights_at(first):
        return [pl.BlockSpec((2, zs, qr, COLS), lambda j: (0, 0, 0, first + j))] * 8

    cols = pl.BlockSpec((2 * rows, COLS), lambda j: (0, j))
    hidden, coef_a, coef_b = pl.pallas_call(
        gate_up_kernel,
        grid=(steps,),
        in_specs=[whole(rows, width)] * 2 + weights_at(0) + weights_at(steps),
        out_specs=[cols] * 3,
        out_shape=[shape((2 * rows, half_ff))] * 3,
        compiler_params=params(),
        cost_estimate=cost(8 * rows * width * half_ff, 16 << 20),
    )(two, two_oth, *mlp, *mlp)
    out_part = dot(hidden, w_d)
    out_oth = over_core(out_part[rows:].astype(BF16))
    output = (mixed + out_part[:rows] + out_oth.astype(F32)).astype(BF16)

    cot_both = jnp.concatenate([cot, cot_oth], axis=0)
    grad_down = dot(hidden, cot_both, TN).astype(BF16)
    grad_down = lax.psum_scatter(
        grad_down, "shard", scatter_dimension=0, tiled=True, axis_index_groups=even
    )
    d_gate, d_up = pl.pallas_call(
        d_gate_up_kernel,
        grid=(steps,),
        in_specs=[
            whole(rows, features), whole(rows, features),
            pl.BlockSpec((COLS, features), lambda j: (j, 0)), cols, cols,
        ],
        out_specs=[cols] * 2,
        out_shape=[shape((2 * rows, half_ff))] * 2,
        compiler_params=params(),
        cost_estimate=cost(4 * rows * features * half_ff, 14 << 20),
    )(cot, cot_oth, w_d, coef_a, coef_b)

    def mlp_grads(first, *after):
        spec = pl.BlockSpec((half, rows), lambda j: (first, 0))
        out = pl.BlockSpec((half // 2, COLS), lambda j: (0, j))
        made = pl.pallas_call(
            functools.partial(mlp_grad_kernel, count=steps),
            grid=(2 * steps,),
            in_specs=[
                spec, spec,
                pl.BlockSpec((2 * rows, COLS), lambda j: (0, jnp.minimum(j, steps - 1))),
                pl.BlockSpec((2 * rows, COLS), lambda j: (0, jnp.maximum(j - steps, 0))),
            ] + [pl.BlockSpec(memory_space=pl.ANY)] * len(after),
            out_specs=[out] * 2,
            out_shape=[shape((half // 2, 2 * half_ff))] * 2,
            compiler_params=params(),
            cost_estimate=cost(8 * rows * half * half_ff, 12 << 20),
        )(send_t, got_t, d_gate, d_up, *after)
        return [m.reshape(2, 2, zs, qr, 2 * half_ff) for m in made]

    alpha_send, beta_send = mlp_grads(1)
    alpha_keep, beta_keep = mlp_grads(0, alpha_send)

    def total(parts):
        return functools.reduce(jnp.add, [p.astype(F32) for p in parts])

    def second(alpha_parts, beta_parts):
        alpha_got = over_y(total([p[:, 1] for p in alpha_parts]).astype(BF16))
        beta_got = over_rep(total([p[:, 1] for p in beta_parts]).astype(BF16))
        return [p[:, 0] for p in alpha_parts] + [alpha_got], [p[:, 0] for p in beta_parts] + [beta_got]

    def finish(alpha_parts, beta_parts):
        parts = [jnp.stack(pair) for pair in zip(alpha_parts, beta_parts)]
        n = zs
        while n > 1:
            n //= 2
            sent = total([p[:, :, n:] for p in parts]).astype(BF16)
            parts = [p[:, :, :n] for p in parts] + [over(sent, 4 * n)]
        mine = total(parts)[:, :, 0].astype(BF16).transpose(1, 0, 2, 3)
        other = over_rep(mine)
        both = jnp.where(
            rep == 0, jnp.concatenate([mine, other], axis=1), jnp.concatenate([other, mine], axis=1)
        )
        both = both[:, :, :quarter].reshape(both.shape[0], 4 * quarter, both.shape[-1])
        return both[:, :dr].astype(F32)

    alpha_parts, beta_parts = second([alpha_keep, over_rep(alpha_send)], [beta_keep, over_y(beta_send)])
    grad_mlp = finish(alpha_parts, beta_parts)

    d_two_mine, d_two_other = pl.pallas_call(
        lambda dg, du, *refs: d_two_kernel(dg, du, *refs[:16], *refs[17:]),
        grid=(steps,),
        in_specs=[cols, cols] + weights_at(0) + weights_at(steps) + [pl.BlockSpec(memory_space=pl.ANY)],
        out_specs=[whole(rows, width)] * 2,
        out_shape=[shape((rows, width), F32), shape((rows, width))],
        scratch_shapes=[pltpu.VMEM((rows, width), F32)],
        compiler_params=params(),
        cost_estimate=cost(8 * rows * width * half_ff, 14 << 20),
    )(d_gate, d_up, *mlp, *mlp, alpha_keep)
    d_two_oth = over_core(d_two_other)
    gain_spec = pl.BlockSpec((1, 1, features), lambda i: (i, 0, 0))
    d_mixed, d_attn, grad_gain_two = pl.pallas_call(
        mixed_backward,
        grid=(seqs,),
        in_specs=[
            by_rows(width), by_rows(width), once(*mlp_order.shape), by_rows(features), by_rows(features),
            whole(2, features),
        ],
        out_specs=[by_rows(features), by_rows(features), gain_spec],
        out_shape=[shape((rows, features), F32), shape((rows, features)), shape((seqs, 1, features), F32)],
        compiler_params=params(),
        cost_estimate=cost(2 * rows * width * features, 10 << 20),
    )(d_two_mine, d_two_oth, mlp_order, mixed, cot, gain_rows)

    d_qkv = pl.pallas_call(
        functools.partial(attention_backward, wide=wide),
        grid=(seqs,),
        in_specs=[
            by_rows(features), once(half, wide + features), once(half, wide + features), once(*attn_order.shape),
            by_rows(wide), pl.BlockSpec((1, HQ, length, length), lambda i: (i, 0, 0, 0)),
            whole(length, LANES), whole(length, LANES),
        ],
        out_specs=by_rows(wide),
        out_shape=shape((rows, wide)),
        compiler_params=params(),
        cost_estimate=cost(10 * rows * width * width, 20 << 20),
    )(d_attn, attn_own, attn_oth, attn_order, qkv, probs, cosine, sine)
    grad_tokens, grad_gain_one = pl.pallas_call(
        functools.partial(token_backward, wide=wide),
        grid=(seqs,),
        in_specs=[
            by_rows(wide), once(half, wide + features), once(half, wide + features), once(*attn_order.shape),
            by_rows(features), by_rows(features), whole(2, features),
        ],
        out_specs=[by_rows(features), gain_spec],
        out_shape=[shape((rows, features)), shape((seqs, 1, features), F32)],
        compiler_params=params(),
        cost_estimate=cost(2 * rows * width * (wide + width), 14 << 20),
    )(d_qkv, attn_own, attn_oth, attn_order, x, d_mixed, gain_rows)

    def attn_grads(place, rhs, rhs_oth, extra=(), gain_at=None):
        n = rhs.shape[1]
        specs = [
            pl.BlockSpec((half, rows), lambda i: (place, 0)), pl.BlockSpec((half, rows), lambda i: (2 + place, 0)),
            whole(rows, n), whole(rows, n),
        ]
        if extra:
            specs += [whole(*extra[0].shape), whole(half, features)]
        made = pl.pallas_call(
            functools.partial(attn_grad_kernel, gain_at=gain_at),
            grid=(1,),
            in_specs=specs,
            out_specs=[whole(half // 4, n)] * 4,
            out_shape=[shape((half // 4, n))] * 4,
            compiler_params=params(),
            cost_estimate=cost(4 * half * rows * n, 4 << 20),
        )(keep_t, got_t, rhs, rhs_oth, *extra)
        return [m.reshape(1, 2, zs, qr, n) for m in made]

    a_keep, b_keep, a_send, b_send = attn_grads(1, d_attn, over_core(d_attn))
    out_alpha, out_beta = second([a_keep, over_rep(a_send)], [b_keep, over_y(b_send)])
    grad_out = finish(out_alpha, out_beta)[0]

    gain_pair = jnp.concatenate([jnp.sum(grad_gain_one, 0), jnp.sum(grad_gain_two, 0)], axis=0)
    gain_pair = (gain_pair + over_core(gain_pair)).astype(BF16)
    a_keep, b_keep, a_send, b_send = attn_grads(
        0, d_qkv, over_core(d_qkv), (gain_pair, attn_order[:half, :features]), nqkv
    )
    qkv_alpha, qkv_beta = second([a_keep, over_rep(a_send)], [b_keep, over_y(b_send)])
    grad_attn = finish(qkv_alpha, qkv_beta)[0]

    grad_down = grad_down.astype(F32) + over_rep(grad_down).astype(F32)
    mine, theirs = grad_mlp[0], over_core(grad_mlp[1].astype(BF16)).astype(F32)
    parts = jnp.stack([jnp.where(core == 0, mine, theirs), jnp.where(core == 0, theirs, mine)])
    parts = parts.reshape(2, dr, 2, chips, fr).transpose(2, 1, 3, 0, 4).reshape(2, dr, 2 * half_ff)
    dims = tokens.shape
    return (
        output.reshape(dims),
        grad_tokens.reshape(dims),
        grad_attn[:, nqkv],
        grad_attn[:, :nq],
        grad_attn[:, nq : nq + nk],
        grad_attn[:, nq + nk : nqkv],
        grad_out,
        grad_attn[:, nqkv + 1],
        parts[0],
        parts[1],
        grad_down,
    )


def solution(mesh):
    data = P(None, ("rep", "shard"), None, None)
    vector, matrix = P("shard"), P("shard", None)
    weights = (vector, matrix, matrix, matrix, matrix, vector, matrix, matrix, matrix)
    return jax.shard_map(
        on_device,
        mesh=mesh,
        in_specs=(data, data) + weights,
        out_specs=(data, data) + weights,
        check_vma=False,
    )
```

```python
import functools
import math

import jax
import jax.numpy as jnp
import numpy as np
from jax import lax
from jax.experimental import pallas as pl
from jax.experimental.pallas import tpu as pltpu
from jax.sharding import PartitionSpec as P

HQ = 15
KV = 5
HD = 64
EPSILON = 1e-05
THETA = 100000.0
F32 = jnp.float32
BF16 = jnp.bfloat16
LANES = 128
COLS = 256
NN = ((1,), (0,))
NT = ((1,), (1,))
TN = ((0,), (0,))
VMEM = 56 << 20


def dot(a, b, contract=NN):
    return lax.dot_general(a, b, (contract, ((), ())), preferred_element_type=F32)


def call(kernel, out_shape, *, vmem=VMEM, **how):
    return pl.pallas_call(
        kernel,
        out_shape=out_shape,
        compiler_params=pltpu.CompilerParams(vmem_limit_bytes=vmem),
        cost_estimate=pl.CostEstimate(flops=1 << 20, bytes_accessed=1 << 12, transcendentals=0),
        **how,
    )


def shape(dims, dtype=BF16):
    return jax.ShapeDtypeStruct(dims, dtype)


def whole(*dims):
    return pl.BlockSpec(dims, lambda *_: (0,) * len(dims))


def once(*dims):
    return pl.BlockSpec(dims, lambda *_: (0,) * len(dims), pipeline_mode=pl.Buffered(1))


def tables(length):
    frequency = THETA ** (-2.0 * np.arange(HD // 2, dtype=np.float32) / HD)
    angles = np.arange(length, dtype=np.float32)[:, None] * frequency.astype(np.float32)[None, :]
    cosine, sine = np.cos(angles), np.sin(angles)
    return np.tile(cosine, (1, 4)), np.concatenate([-sine, sine, -sine, sine], axis=1)


def turn(tile, cosine, sine, low):
    other = jnp.where(low, pltpu.roll(tile, LANES - 32, 1), pltpu.roll(tile, 32, 1))
    return tile * cosine + other * sine


def placed(tile, half):
    lane = lax.broadcasted_iota(jnp.int32, tile.shape, 1)
    alone = jnp.where((lane >= HD) == (half == 1), tile, 0.0)
    moved = pltpu.roll(alone, HD, 1)
    pair = (moved, alone) if half else (alone, moved)
    return [one.astype(BF16) for one in pair]


def attention_forward(
    x_ref, own_ref, oth_ref, attn_order_ref, mlp_order_ref, cos_ref, sin_ref, *refs, wide
):
    two_ref, two_t_ref, keep_ref, send_ref, qkv_ref, probs_ref, mixed_ref, gain_ref = refs[-8:]
    length, features = x_ref.shape
    half = own_ref.shape[0]
    to_order = attn_order_ref[:, :features]
    last = slice(wide - LANES, wide)
    gains = dot(own_ref[:, last], to_order[:half], TN) + dot(oth_ref[:, last], to_order[half:], TN)
    gain_one, gain_two = gains[HD : HD + 1], gains[HD + 1 : HD + 2]
    gain_ref[...] = gains[HD : HD + 8]
    x = x_ref[...].astype(F32)
    r1 = lax.rsqrt(jnp.mean(x * x, axis=-1, keepdims=True) + EPSILON)
    normed = (x * r1 * gain_one).astype(BF16)
    spread = dot(normed, to_order, NT).astype(BF16)
    left, right = spread[:, :half], spread[:, half:]
    spread = dot(to_order, normed, NT).astype(BF16)
    keep_ref[:half, :] = spread[:half]
    send_ref[:half, :] = spread[half:]
    lane = lax.broadcasted_iota(jnp.int32, (length, LANES), 1)
    low = lane % HD < HD // 2
    cosine, sine = cos_ref[...], sin_ref[...]
    tiles, heads = [], {}
    for t in range(wide // LANES):
        cols = slice(t * LANES, (t + 1) * LANES)
        tile = dot(left, own_ref[:, cols]) + dot(right, oth_ref[:, cols])
        if t * 2 < HQ + KV:
            tile = turn(tile, cosine, sine, low)
        if t == wide // LANES - 1:
            tile = jnp.where(lane < HD, tile, 0.0)
        short = tile.astype(BF16)
        qkv_ref[:, cols] = short
        tiles.append(short)
        for n in (2 * t, 2 * t + 1):
            if HQ <= n < HQ + 2 * KV:
                heads[n] = placed(tile, n % 2)
    causal = lax.broadcasted_iota(jnp.int32, (length, length), 0) >= lax.broadcasted_iota(
        jnp.int32, (length, length), 1
    )
    context = [None] * ((HQ + 1) // 2)
    for h in range(HQ):
        j, t, s = h // (HQ // KV), h // 2, h % 2
        scores = dot(tiles[t], heads[HQ + j][s], NT) * (1.0 / math.sqrt(HD))
        scores = jnp.where(causal, scores, -1e30)
        exponent = jnp.exp(scores - jnp.max(scores, axis=-1, keepdims=True))
        probs = exponent * (1.0 / jnp.sum(exponent, axis=-1, keepdims=True))
        probs = probs.astype(BF16)
        probs_ref[0, h] = probs
        part = dot(probs, heads[HQ + KV + j][s])
        context[t] = part if context[t] is None else context[t] + part
    context = jnp.concatenate([c.astype(BF16) for c in context], axis=1)
    spread = dot(context, attn_order_ref[...], NT).astype(BF16)
    mixed = x + dot(spread[:, :half], own_ref[:, wide : wide + features]) + dot(spread[:, half:], oth_ref[:, wide : wide + features])
    spread = dot(attn_order_ref[...], context, NT).astype(BF16)
    keep_ref[half:, :] = spread[:half]
    send_ref[half:, :] = spread[half:]
    mixed_ref[...] = mixed
    r2 = lax.rsqrt(jnp.mean(mixed * mixed, axis=-1, keepdims=True) + EPSILON)
    two = (mixed * r2 * gain_two).astype(BF16)
    to_order = mlp_order_ref[:, :features]
    two_ref[...] = dot(two, to_order, NT).astype(BF16)
    two_t_ref[...] = dot(to_order, two, NT).astype(BF16)


def attention_backward(
    mine_ref, other_ref, mlp_order_ref, mixed_ref, cot_ref, gain_ref, own_ref, oth_ref, order_ref, qkv_ref,
    probs_ref, cos_ref, sin_ref, x_ref, *refs, wide, first
):
    rhs_ref, d_attn_ref, out_ref, grad_ref = refs[-4:]
    length, features = mixed_ref.shape
    total = (mine_ref[...] + other_ref[...].astype(F32)).astype(BF16)
    d_two = dot(total, mlp_order_ref[:, :features])
    mixed = mixed_ref[...]
    r2 = lax.rsqrt(jnp.mean(mixed * mixed, axis=-1, keepdims=True) + EPSILON)
    unit = mixed * r2
    e2 = d_two * gain_ref[1:2, :]
    d_mixed = cot_ref[...].astype(F32) + r2 * (e2 - unit * jnp.mean(e2 * unit, axis=-1, keepdims=True))
    d_attn = d_mixed.astype(BF16)
    d_attn_ref[:, :features] = d_attn
    d_attn_ref[:, features:] = jnp.zeros((length, d_attn_ref.shape[1] - features), BF16)
    grad_gain_two = jnp.sum(d_two * unit, axis=0, keepdims=True)
    d_context = jnp.concatenate(
        [
            dot(d_attn, own_ref[:, wide : wide + features], NT).astype(BF16),
            dot(d_attn, oth_ref[:, wide : wide + features], NT).astype(BF16),
        ],
        axis=1,
    )
    d_context = dot(d_context, order_ref[...]).astype(BF16)
    lane = lax.broadcasted_iota(jnp.int32, (length, LANES), 1)
    low = lane % HD < HD // 2
    cosine, sine = cos_ref[...], -sin_ref[...]

    def tile_of(n):
        t = n // 2
        return qkv_ref[:, t * LANES : (t + 1) * LANES]

    d_tiles = [None] * ((HQ + 2 * KV + 1) // 2)

    def add(t, part):
        d_tiles[t] = part if d_tiles[t] is None else d_tiles[t] + part

    groups = HQ // KV
    for j in range(KV):
        keys = placed(tile_of(HQ + j).astype(F32), (HQ + j) % 2)
        values = placed(tile_of(HQ + KV + j).astype(F32), (HQ + KV + j) % 2)
        d_key, d_value = [None, None], [None, None]
        for h in range(j * groups, (j + 1) * groups):
            t, s = h // 2, h % 2
            d_con = d_context[:, t * LANES : (t + 1) * LANES]
            probs = probs_ref[0, h]
            wide_probs = probs.astype(F32)
            d_probs = dot(d_con, values[s], NT)
            inner = jnp.sum(d_probs * wide_probs, axis=-1, keepdims=True)
            d_scores = (wide_probs * (d_probs - inner) * (1.0 / math.sqrt(HD))).astype(BF16)
            add(t, dot(d_scores, keys[s]))
            part = dot(d_scores, tile_of(h), TN)
            d_key[s] = part if d_key[s] is None else d_key[s] + part
            part = dot(probs, d_con, TN)
            d_value[s] = part if d_value[s] is None else d_value[s] + part
        for n, pair in ((HQ + j, d_key), (HQ + KV + j, d_value)):
            here = n % 2
            mask = (lane >= HD) == (here == 1)
            total = jnp.where(mask, pair[here] + pltpu.roll(pair[1 - here], HD, 1), 0.0)
            add(n // 2, total)
    for t, tile in enumerate(d_tiles):
        if t * 2 < HQ + KV:
            tile = turn(tile, cosine, sine, low)
        rhs_ref[:, t * LANES : (t + 1) * LANES] = tile.astype(BF16)
    d_qkv = rhs_ref[...]
    d_normed = jnp.concatenate(
        [
            dot(d_qkv, own_ref[:, :wide], NT).astype(BF16),
            dot(d_qkv, oth_ref[:, :wide], NT).astype(BF16),
        ],
        axis=1,
    )
    d_normed = dot(d_normed, order_ref[:, :features])
    x = x_ref[...].astype(F32)
    r1 = lax.rsqrt(jnp.mean(x * x, axis=-1, keepdims=True) + EPSILON)
    unit = x * r1
    e1 = d_normed * gain_ref[0:1, :]
    out = d_mixed + r1 * (e1 - unit * jnp.mean(e1 * unit, axis=-1, keepdims=True))
    out_ref[...] = out.astype(BF16)
    grad_gain_one = jnp.sum(d_normed * unit, axis=0, keepdims=True)
    grads = jnp.concatenate([grad_gain_one, grad_gain_two, jnp.zeros((6, features), F32)], axis=0)

    grad_ref[...] = grads if first else grads + refs[0][...]


def flipped(array, axis, block):
    n = array.shape[axis] // block
    parts = [lax.slice_in_dim(array, i * block, (i + 1) * block, axis=axis) for i in range(n)]
    return jnp.concatenate([parts[i ^ 1] for i in range(n)], axis=axis)


def row_quarters(w, quarter, qr):
    dr, n = w.shape
    parts = []
    for q in range(4):
        part = w[min(q * quarter, dr) : min((q + 1) * quarter, dr), :]
        parts.append(jnp.concatenate([part, jnp.zeros((qr - part.shape[0], n), F32)], axis=0))
    return parts


def pieces_kernel(
    place_ref, wq_ref, wk_ref, wv_ref, wo_ref, g1_ref, g2_ref, wg_ref, wu_ref, attn_ref, here_ref, there_ref,
    *, quarter, qr, fr, wide
):
    core, rep = place_ref[0], place_ref[1]
    dr = wq_ref.shape[0]

    def store(ref, at, w):
        parts = row_quarters(w, quarter, qr)
        for s in range(2):
            ref[s, :, at : at + w.shape[1]] = jnp.where(rep == 0, parts[s], parts[2 + s]).astype(BF16)

    wide_of = lambda ref: ref[...].astype(F32)
    eye = (
        lax.broadcasted_iota(jnp.int32, (dr, dr), 0) == lax.broadcasted_iota(jnp.int32, (dr, dr), 1)
    ).astype(F32)
    columns = [jnp.sum(eye * wide_of(ref), axis=1, keepdims=True) for ref in (g1_ref, g2_ref)]
    blank = jnp.zeros((dr, wide - wq_ref.shape[1] - 2 * wk_ref.shape[1] - 2), F32)
    row = jnp.concatenate([wide_of(wq_ref), wide_of(wk_ref), wide_of(wv_ref)] + columns + [blank], axis=1)
    store(attn_ref, 0, row)
    w = wide_of(wo_ref)
    store(attn_ref, wide, jnp.concatenate([w, jnp.zeros((dr, attn_ref.shape[2] - wide - w.shape[1]), F32)], axis=1))
    half_ff = here_ref.shape[2] // 2
    for at, ref in ((0, wg_ref), (half_ff, wu_ref)):
        w = wide_of(ref)
        chunks = [w[:, i * fr : (i + 1) * fr] for i in range(w.shape[1] // fr)]
        first, second = (jnp.concatenate(chunks[c::2], axis=1) for c in (0, 1))
        store(here_ref, at, jnp.where(core == 0, first, second))
        store(there_ref, at, jnp.where(core == 0, second, first))


def join_kernel(*refs, count):
    rows = refs[0].shape[0]
    for i, ref in enumerate(refs[:count]):
        refs[-1][i * rows : (i + 1) * rows, :] = ref[...]


def tie_kernel(*refs):
    del refs


def add_kernel(*refs, picks, n_alpha, rows, form):
    totals = []
    for ref, (lead, f) in zip(refs, picks):
        at = (slice(None), slice(None), f, slice(rows, rows + refs[-1].shape[-2]))
        totals.append(ref[at if lead is None else (lead,) + at].astype(F32))
    alpha, beta = functools.reduce(jnp.add, totals[:n_alpha]), functools.reduce(jnp.add, totals[n_alpha:])
    if form == "apart":
        refs[-2][:, :, 0] = alpha.astype(BF16)
        refs[-1][:, :, 0] = beta.astype(BF16)
    elif form == "stack":
        refs[-1][0, :, :, 0] = alpha.astype(BF16)
        refs[-1][1, :, :, 0] = beta.astype(BF16)
    else:
        for c in range(alpha.shape[1]):
            refs[-1][c, :, 0] = alpha[:, c].astype(BF16)
            refs[-1][c, :, 1] = beta[:, c].astype(BF16)


def shards_kernel(place_ref, mine_ref, other_ref, got_ref, got_other_ref, gate_ref, up_ref, *, quarter, fr):
    core, rep = place_ref[0], place_ref[1]
    dr = gate_ref.shape[0]
    for at, out_ref in ((0, gate_ref), (1, up_ref)):
        sides = []
        for c, mine, other in ((0, mine_ref, other_ref), (1, got_ref, got_other_ref)):
            a, b = mine[c, at].astype(F32), other[c, at].astype(F32)
            low, high = jnp.where(rep == 0, a, b), jnp.where(rep == 0, b, a)
            rows = [half[s][:quarter] for half in (low, high) for s in range(2)]
            sides.append(jnp.concatenate(rows, axis=0)[:dr])
        even, odd = jnp.where(core == 0, sides[0], sides[1]), jnp.where(core == 0, sides[1], sides[0])
        chunks = []
        for k in range(even.shape[1] // fr):
            chunks += [even[:, k * fr : (k + 1) * fr], odd[:, k * fr : (k + 1) * fr]]
        out_ref[...] = jnp.concatenate(chunks, axis=1)


def attn_shards_kernel(place_ref, mine_ref, other_ref, query_ref, key_ref, value_ref, gains_ref, out_ref, *, quarter, wide):
    rep, dr = place_ref[1], out_ref.shape[0]
    a, b = mine_ref[0, 0].astype(F32), other_ref[0, 0].astype(F32)
    low, high = jnp.where(rep == 0, a, b), jnp.where(rep == 0, b, a)
    rows = jnp.concatenate([half[s][:quarter] for half in (low, high) for s in range(2)], axis=0)[:dr]
    at = 0
    for ref in (query_ref, key_ref, value_ref, gains_ref):
        ref[...] = rows[:, at : at + ref.shape[1]]
        at += ref.shape[1]
    out_ref[...] = rows[:, wide : wide + out_ref.shape[1]]


def order_kernel(*refs):
    for feat_ref, out_ref in zip(refs[:2], refs[-2:]):
        column = lax.broadcasted_iota(jnp.int32, out_ref.shape, 1)
        out_ref[...] = (feat_ref[...] == column).astype(F32).astype(BF16)


def copy_kernel(in_ref, *refs):
    out_ref, n = refs[-1], in_ref.shape[1]
    out_ref[:, :n] = in_ref[...]
    out_ref[:, n:] = jnp.zeros((out_ref.shape[0], out_ref.shape[1] - n), BF16)


def sum_kernel(*refs):
    n = refs[-1].shape[1]
    refs[-1][...] = functools.reduce(jnp.add, [r[:, :n].astype(F32) for r in (refs[:3] if len(refs) > 3 else refs[:-1])]).astype(refs[-1].dtype)


def pair_kernel(first_ref, second_ref, *refs):
    refs[-1][0] = first_ref[...]
    refs[-1][1] = second_ref[...]


def double_kernel(mine_ref, got_ref, out_ref):
    n = mine_ref.shape[2]
    out_ref[:, :, :n] = mine_ref[...]
    out_ref[:, :, n:] = got_ref[...]


def split_attn_kernel(*refs, count):
    ins, outs = refs[:count], refs[-2:]
    rows = ins[0].shape[1]
    for i, ref in enumerate(ins):
        for s in range(2):
            outs[s][i * rows : (i + 1) * rows, :] = ref[s]


def split_mlp_kernel(mine_ref, got_ref, *outs):
    n, rows = mine_ref.shape[2:4]
    for k, ref in enumerate((mine_ref, got_ref)):
        for s in range(2):
            for c in range(2):
                for i in range(n):
                    at = (k * n + i) * rows
                    outs[s][c, at : at + rows, :] = ref[c, s, i]


def attn_grad_kernel(*refs, seqs, wide, gain_at):
    keeps, gots, d_qkvs, d_attns = (refs[k * seqs : (k + 1) * seqs] for k in (0, 1, 2, 4))
    d_qkvs_oth, d_attns_oth = (refs[k * seqs : (k + 1) * seqs] for k in (3, 5))
    gains_ref, gains_oth_ref, order_ref = refs[6 * seqs : 6 * seqs + 3]
    out_refs = refs[-4:]
    half, features = keeps[0].shape[0] // 2, gains_ref.shape[1]

    def total(at, rights, rights_oth):
        pairs = list(zip(keeps + gots, rights + rights_oth))
        return functools.reduce(jnp.add, [dot(left[at, :], right[...]) for left, right in pairs])

    out = total(slice(0, half), d_qkvs, d_qkvs_oth)
    gains = (gains_ref[...] + gains_oth_ref[...]).astype(BF16)
    gains = dot(order_ref[:half, :features], gains, NT)
    lane = lax.broadcasted_iota(jnp.int32, (half, LANES), 1) + (wide - LANES)
    tile = jnp.where(lane == gain_at, gains[:, 0:1], 0.0) + jnp.where(lane == gain_at + 1, gains[:, 1:2], 0.0)
    out_two = total(slice(half, 2 * half), d_attns, d_attns_oth)
    n = out_refs[0].shape[0]
    for i, ref in enumerate(out_refs):
        at = slice(i * n, (i + 1) * n)
        ref[:, : wide - LANES] = out[at, : wide - LANES].astype(BF16)
        ref[:, wide - LANES : wide] = (out[at, wide - LANES :] + tile[at]).astype(BF16)
        ref[:, wide:] = out_two[at].astype(BF16)


def mlp_kernel(*refs, seqs):
    twos, ts, (cot_ref, cot_oth_ref, wd_ref) = refs[: 2 * seqs], refs[2 * seqs : 4 * seqs], refs[4 * seqs : 4 * seqs + 3]
    refs = refs[4 * seqs + 3 :]
    gates, ups = refs[:8], refs[8:16]
    alpha_send, beta_send, alpha_keep, beta_keep, down_ref = refs[16:21]
    out_ref, out_oth_ref, d_two_ref, d_two_oth_ref = refs[21:25]
    acts_ref, acts_t_ref, cots_ref, out_acc, d_two_acc = refs[25:]
    rows, width = d_two_ref.shape
    length = rows // seqs
    block, n = width // 8, width // 4
    step, last = pl.program_id(0), pl.num_programs(0) - 1

    @pl.when(step == 0)
    def _():
        for i in range(2 * seqs):
            at = slice(i * length, (i + 1) * length)
            two, t = twos[i][...], ts[i][...]
            acts_ref[at, :] = flipped(two, 1, block) if i >= seqs else two
            acts_t_ref[:, at] = flipped(t, 0, block) if i >= seqs else t
        cots_ref[:rows, :] = cot_ref[...]
        cots_ref[rows:, :] = cot_oth_ref[:, : cots_ref.shape[1]]
        for ref in (out_ref, d_two_ref, out_acc, d_two_acc):
            ref[...] = jnp.zeros(ref.shape, F32)

    def weight(refs):
        return jnp.concatenate(
            [r[c] for i in range(4) for c in (0, 1) for r in refs[2 * i : 2 * i + 2]], axis=0
        )

    wg, wu, wd = weight(gates), weight(ups), wd_ref[...]
    acts, cots = acts_ref[...], cots_ref[...]
    gate, up = dot(acts, wg), dot(acts, wu)
    sg = 1.0 / (1.0 + jnp.exp(-gate))
    silu = gate * sg
    hidden = (silu * up).astype(BF16)
    d_hidden = dot(cots, wd, NT)
    d_gate = (d_hidden * up * sg * (1.0 + gate * (1.0 - sg))).astype(BF16)
    d_up = (d_hidden * silu).astype(BF16)
    for i, d in ((0, d_gate), (1, d_up)):
        grad = dot(acts_t_ref[...], d).astype(BF16)
        for k, ref in enumerate((alpha_keep, beta_keep, alpha_send, beta_send)):
            ref[i] = grad[k * n : (k + 1) * n]
    down_ref[...] = dot(hidden, cots, TN).astype(BF16)
    out_ref[...] += dot(hidden[:rows], wd)
    out_acc[...] += dot(hidden[rows:], wd)
    d_two_ref[...] += dot(d_gate[:rows], wg, NT) + dot(d_up[:rows], wu, NT)
    d_two_acc[...] += dot(d_gate[rows:], wg, NT) + dot(d_up[rows:], wu, NT)

    @pl.when(step == last)
    def _():
        out_oth_ref[:, : out_acc.shape[1]] = out_acc[...].astype(BF16)
        out_oth_ref[:, out_acc.shape[1] :] = jnp.zeros((rows, out_oth_ref.shape[1] - out_acc.shape[1]), BF16)
        d_two_oth_ref[...] = flipped(d_two_acc[...].astype(BF16), 1, block)


def on_device(
    tokens, cotangent, attn_gain, w_query, w_key, w_value, w_out, mlp_gain, w_gate, w_up, w_down
):
    shards = lax.axis_size("shard")
    chips = shards // 2
    zs = chips // 2
    me, rep = lax.axis_index("shard"), lax.axis_index("rep")
    core = me % 2
    micro, batch, length, features = tokens.shape
    seqs = micro * batch
    rows = seqs * length
    dr = features // shards
    quarter = -(-dr // 4)
    qr = -(-quarter // 8) * 8
    width = shards * 4 * qr
    half = width // 2
    block = zs * qr
    fr = w_down.shape[0]
    half_ff = chips * fr
    steps = half_ff // COLS
    nq, nk = HQ * HD, KV * HD
    nqkv = nq + 2 * nk
    wide = -(-(nqkv + 2) // LANES) * LANES
    padded = -(-features // LANES) * LANES
    full = wide + padded
    cosine, sine = (jnp.asarray(t) for t in tables(length))
    place = jnp.stack([core, rep]).astype(jnp.int32)
    in_smem = pl.BlockSpec(memory_space=pltpu.SMEM)
    in_vmem = pl.BlockSpec(memory_space=pltpu.VMEM)
    anywhere = pl.BlockSpec(memory_space=pl.ANY)
    z_bits = zs.bit_length() - 1
    z_flip = np.array([sum(((i >> b) & 1) << (z_bits - 1 - b) for b in range(z_bits)) for i in range(zs)])

    def over(array, flip):
        return lax.ppermute(array, "shard", [(s, s ^ flip) for s in range(shards)])

    def over_core(array):
        return over(array, 1)

    def over_y(array):
        return over(array, 2)

    def over_rep(array):
        return lax.ppermute(array, "rep", [(0, 1), (1, 0)])

    def tie(arrays, *deps):
        return call(
            tie_kernel, [shape(a.shape, a.dtype) for a in arrays],
            in_specs=[anywhere] * (len(arrays) + len(deps)), out_specs=[anywhere] * len(arrays),
            input_output_aliases={i: i for i in range(len(arrays))},
        )(*arrays, *deps)

    def small(kernel, outs, arrays, deps=()):
        return call(
            kernel, outs, in_specs=[in_vmem] * len(arrays) + [anywhere] * len(deps), vmem=16 << 20
        )(*arrays, *deps)

    even = [[2 * k + c for k in range(chips)] for c in range(2)]
    w_d = lax.all_gather(w_down, "shard", axis=0, tiled=True, axis_index_groups=even)

    attn_piece, here, there = call(
        functools.partial(pieces_kernel, quarter=quarter, qr=qr, fr=fr, wide=wide),
        [shape((2, qr, full)), shape((2, qr, 2 * half_ff)), shape((2, qr, 2 * half_ff))],
        grid=(1,),
        in_specs=[in_smem] + [
            whole(*w.shape) for w in (w_query, w_key, w_value, w_out, attn_gain[None], mlp_gain[None], w_gate, w_up)
        ],
        out_specs=[in_vmem] * 3,
        vmem=24 << 20,
    )(place, w_query, w_key, w_value, w_out, attn_gain[None], mlp_gain[None], w_gate, w_up)
    parts = [attn_piece if z == 0 else over(attn_piece, 4 * z) for z in z_flip]
    x = tokens.reshape(rows, features)
    cot = cotangent.reshape(rows, features)
    cot_oth = over_core(small(copy_kernel, shape((rows, padded)), [cot], [attn_piece]))
    piece = small(pair_kernel, shape((2, 2, qr, 2 * half_ff)), [here, over_core(there)])
    attn_first, attn_second = small(
        functools.partial(split_attn_kernel, count=zs), [shape((block, full))] * 2, parts, [cot_oth, x, piece]
    )
    piece = piece.reshape(2, 2, 1, qr, 2 * half_ff)
    for bit in range(z_bits)[:0:-1]:
        got = over(piece, 4 << bit)
        piece = small(double_kernel, shape((2, 2, 2 * piece.shape[2]) + piece.shape[3:]), [piece, got])
    mlp_first, mlp_second = small(
        split_mlp_kernel, [shape((2, block, 2 * half_ff))] * 2, [piece, over(piece, 4)]
    )

    def feature_of(dims):
        sizes = {"core": 2, "split": 2, "f1": 2, "f2": 2, "z": zs, "row": qr}
        grid = np.meshgrid(*[np.arange(sizes[d]) for d in dims], indexing="ij")
        at = {d: g.reshape(-1) for d, g in zip(dims, grid)}
        x_flip = np.where(at["split"] == 0, at["f1"], at["f2"])
        y_flip = np.where(at["split"] == 0, at["f2"], at["f1"])
        shard = me ^ jnp.asarray(at["core"] + 2 * (y_flip + 2 * z_flip[at["z"]]), jnp.int32)
        part = 2 * (rep ^ jnp.asarray(x_flip, jnp.int32)) + jnp.asarray(at["split"], jnp.int32)
        inside = part * quarter + jnp.asarray(at["row"], jnp.int32)
        real = jnp.asarray(at["row"] < quarter) & (inside < dr)
        return jnp.where(real, shard * dr + inside, -1)[:, None]

    feats = [feature_of(("core", "f1", "split", "f2", "z", "row")), feature_of(("f1", "split", "core", "f2", "z", "row"))]
    attn_order, mlp_order = small(
        order_kernel, [shape((width, padded))] * 2, feats, [attn_first]
    )

    def start(first, second):
        return [over_y(first), over_rep(second)], [over_rep(first), over_y(second)]

    def finish(first, second, once_over, other_way, *deps):
        (y_first, x_second), (x_first, y_second) = once_over, other_way
        if deps:
            y_first, x_second = tie([y_first, x_second], *deps)
        xy_first, xy_second = over_rep(y_first), over_y(x_second)
        return [first, y_first, second, x_second, x_first, xy_first, y_second, xy_second]

    blocks = finish(attn_first, attn_second, *start(attn_first, attn_second), piece)
    attn_own = small(functools.partial(join_kernel, count=8), shape((half, full)), blocks, [mlp_first])
    attn_oth = over_core(attn_own)
    mlp_once, mlp_other_way = start(mlp_first, mlp_second)

    by_rows = lambda cols: pl.BlockSpec((length, cols), lambda i: (i, 0))
    rows_at = lambda i, cols: pl.BlockSpec((length, cols), lambda _: (i, 0))
    cols_at = lambda i, n: pl.BlockSpec((n, length), lambda _: (0, i))
    probs_at = lambda i: pl.BlockSpec((1, HQ, length, length), lambda _: (i, 0, 0, 0))
    by_once = lambda *arrays: [once(*a.shape) for a in arrays]
    saved = []
    for i in range(seqs):
        deps = [*mlp_once, *mlp_other_way, w_d] if i else [mlp_first]
        shared = (attn_own, attn_oth, attn_order, mlp_order, cosine, sine)
        outs = [
            shape((length, width)), shape((width, length)), shape((width, length)), shape((width, length)),
            shape((length, wide)), shape((1, HQ, length, length)), shape((length, features), F32),
            shape((8, features), F32),
        ]
        saved.append(call(
            functools.partial(attention_forward, wide=wide),
            outs,
            grid=(1,),
            in_specs=[rows_at(i, features)] + by_once(*shared) + [anywhere] * len(deps),
            out_specs=by_once(*outs),
            vmem=40 << 20,
        )(x, *shared, *deps))
        if i == 0:
            mlp_once = tie(mlp_once, saved[0][-1])
    two, two_t, keep_t, send_t, qkv, probs, mixed, gain_rows = zip(*saved)
    gain_rows = gain_rows[0]
    mlp = finish(mlp_first, mlp_second, mlp_once, mlp_other_way)
    across = lambda arrays: [over_core(a) for a in arrays]
    two_oth, two_t_oth = across(two), across(two_t)

    def weights_at(first):
        return [pl.BlockSpec((2, block, COLS), lambda j: (0, 0, first + j))] * 8

    grad_spec = pl.BlockSpec((2, width // 4, COLS), lambda j: (0, 0, j))
    (
        alpha_send, beta_send, alpha_keep, beta_keep, grad_down, out_part, out_other, d_two_mine, d_two_other
    ) = call(
        functools.partial(mlp_kernel, seqs=seqs),
        [shape((2, width // 4, half_ff))] * 4 + [shape((half_ff, features))]
        + [shape((rows, features), F32), shape((rows, padded)), shape((rows, width), F32), shape((rows, width))],
        grid=(steps,),
        in_specs=[once(length, width)] * (2 * seqs) + [once(width, length)] * (2 * seqs)
        + [once(rows, features), once(rows, padded)]
        + [pl.BlockSpec((COLS, features), lambda j: (j, 0))] + weights_at(0) + weights_at(steps),
        out_specs=[grad_spec] * 4 + [pl.BlockSpec((COLS, features), lambda j: (j, 0))]
        + [whole(rows, features), whole(rows, padded)] + [whole(rows, width)] * 2,
        scratch_shapes=[
            pltpu.VMEM((2 * rows, width), BF16), pltpu.VMEM((width, 2 * rows), BF16),
            pltpu.VMEM((2 * rows, features), BF16), pltpu.VMEM((rows, features), F32), pltpu.VMEM((rows, width), F32),
        ],
    )(*two, *two_oth, *two_t, *two_t_oth, cot, cot_oth, w_d, *mlp, *mlp)
    grad_down = lax.psum_scatter(
        grad_down, "shard", scatter_dimension=0, tiled=True, axis_index_groups=even
    )

    def add(alpha, beta, at, size, form, deps):
        arrays = [p[0] for p in alpha + beta]
        j, cores, _, _, n = arrays[0].shape
        one = shape((j, cores, 1, size, n))
        outs = {"apart": [one, one], "stack": shape((2,) + one.shape), "last": shape((cores, j, 2, size, n))}[form]
        body = functools.partial(add_kernel, picks=[p[1:] for p in alpha + beta], n_alpha=len(alpha), rows=at, form=form)
        return small(body, outs, arrays, deps)

    class Reduction:
        def __init__(self, alpha_keep, beta_keep, alpha_send, beta_send):
            self.early = [[alpha_keep, over_rep(alpha_send)], [beta_keep, over_y(beta_send)]]
            self.late = []
            self.both = []
            self.size = block

        def parts(self, f):
            return [
                [(a, None, f) for a in self.early[s]]
                + [(pair[s], None, 0) for pair in self.late] + [(a, s, 0) for a in self.both]
                for s in range(2)
            ]

        def second(self, *deps):
            alpha_sent, beta_sent = add(*self.parts(1), 0, block, "apart", deps)
            self.late.append((over_y(alpha_sent), over_rep(beta_sent)))
            return [alpha_sent, beta_sent]

        def z(self, *deps):
            self.size //= 2
            sent = add(*self.parts(0), self.size, self.size, "stack", deps)
            self.both.append(over(sent, 4 << (len(self.both))))
            return [sent]

        def last(self, *deps):
            mine = add(*self.parts(0), 0, qr, "last", deps)
            return mine, over_rep(mine)

    mlp_sum = Reduction(
        *[a.reshape(2, 2, 2, block, half_ff) for a in (alpha_keep, beta_keep, alpha_send, beta_send)]
    )

    d_two_oth = over_core(d_two_other)
    got_t = across(send_t)
    before, d_qkv, d_attn = [], [], []
    for i in range(seqs):
        arrays = (gain_rows, attn_own, attn_oth, attn_order, qkv[i], probs[i], cosine, sine)
        outs = [shape((length, wide)), shape((length, padded)), shape((rows, features)), shape((8, features), F32)]
        one, other, grad_tokens, grad_gains = call(
            functools.partial(attention_backward, wide=wide, first=not i),
            outs,
            grid=(1,),
            in_specs=[rows_at(i, width), rows_at(i, width)] + by_once(mlp_order, mixed[i]) + [rows_at(i, features)]
            + by_once(*arrays) + [rows_at(i, features)] + ([once(8, features), anywhere] if i else []),
            out_specs=by_once(*outs[:2]) + [rows_at(i, features)] + by_once(outs[3]),
            input_output_aliases={15: 2} if i else {},
            vmem=48 << 20,
        )(d_two_mine, d_two_oth, mlp_order, mixed[i], cot, *arrays, x, *before)
        before = [grad_gains, grad_tokens]
        d_qkv.append(one)
        d_attn.append(other)
    sent = mlp_sum.second(d_qkv[-1])
    n = half // 4
    arrays = (
        *keep_t, *got_t, *d_qkv, *across(d_qkv), *d_attn, *across(d_attn), grad_gains, over_core(grad_gains), attn_order
    )
    attn_grads = call(
        functools.partial(attn_grad_kernel, seqs=seqs, wide=wide, gain_at=nqkv),
        [shape((n, full))] * 4,
        grid=(1,),
        in_specs=by_once(*arrays) + [anywhere] * 2,
        out_specs=[in_vmem] * 4,
        vmem=32 << 20,
    )(*arrays, *sent)
    attn_sum = Reduction(*[a.reshape(1, 1, 2, block, full) for a in attn_grads])
    out_oth = over_core(out_other)
    for i in range(seqs):
        output = call(
            sum_kernel, shape((rows, features)), grid=(1,),
            in_specs=[rows_at(i, features), once(length, features), rows_at(i, padded)]
            + [anywhere] * (2 if i else 1),
            out_specs=rows_at(i, features), input_output_aliases={4: 0} if i else {}, vmem=16 << 20,
        )(out_part, mixed[i], out_oth, attn_grads[0], *([output] if i else []))
    sent = mlp_sum.z(attn_grads[0], output)
    sent = attn_sum.second(*sent)
    for step in range(z_bits):
        if step:
            sent = mlp_sum.z(*sent)
        if step == z_bits - 1:
            mlp_mine, mlp_from = None, None
        sent = attn_sum.z(*sent)
    mlp_mine, mlp_from = mlp_sum.last(*sent)
    attn_mine, attn_from = attn_sum.last(mlp_mine)

    grad_gate, grad_up = call(
        functools.partial(shards_kernel, quarter=quarter, fr=fr),
        [shape((dr, 2 * half_ff), F32)] * 2,
        grid=(1,),
        in_specs=[in_smem] + [in_vmem] * 4, out_specs=[whole(dr, 2 * half_ff)] * 2, vmem=24 << 20,
    )(place, mlp_mine, mlp_from, over_core(mlp_mine), over_core(mlp_from))
    down_oth = over_rep(grad_down)
    grad_down = call(
        sum_kernel, shape(w_down.shape, F32), grid=(1,), in_specs=[whole(*w_down.shape), in_vmem],
        out_specs=whole(*w_down.shape), vmem=16 << 20,
    )(grad_down, down_oth)
    grad_query, grad_key, grad_value, grad_gains, grad_out = call(
        functools.partial(attn_shards_kernel, quarter=quarter, wide=wide),
        [shape((dr, n), F32) for n in (nq, nk, nk, 2, features)],
        grid=(1,),
        in_specs=[in_smem] + [in_vmem] * 2, out_specs=[whole(dr, n) for n in (nq, nk, nk, 2, features)], vmem=16 << 20,
    )(place, attn_mine, attn_from)
    dims = tokens.shape
    return (
        output.reshape(dims), grad_tokens.reshape(dims), grad_gains[:, 0], grad_query, grad_key, grad_value,
        grad_out, grad_gains[:, 1], grad_gate, grad_up, grad_down,
    )


def solution(mesh):
    data = P(None, ("rep", "shard"), None, None)
    vector, matrix = P("shard"), P("shard", None)
    weights = (vector, matrix, matrix, matrix, matrix, vector, matrix, matrix, matrix)
    return jax.shard_map(
        on_device,
        mesh=mesh,
        in_specs=(data, data) + weights,
        out_specs=(data, data) + weights,
        check_vma=False,
    )
```

```python
import functools
import math

import jax
import jax.numpy as jnp
import numpy as np
from jax import lax
from jax.experimental import pallas as pl
from jax.experimental.pallas import tpu as pltpu
from jax.sharding import PartitionSpec as P

HQ = 15
KV = 5
HD = 64
EPSILON = 1e-05
THETA = 100000.0
F32 = jnp.float32
BF16 = jnp.bfloat16
LANES = 128
COLS = 256
NN = ((1,), (0,))
NT = ((1,), (1,))
TN = ((0,), (0,))
VMEM = 60 << 20
ADD_VMEM = 16 << 20


def dot(a, b, contract=NN):
    return lax.dot_general(a, b, (contract, ((), ())), preferred_element_type=F32)


def call(kernel, out_shape, *, vmem=VMEM, **how):
    return pl.pallas_call(
        kernel,
        out_shape=out_shape,
        compiler_params=pltpu.CompilerParams(vmem_limit_bytes=vmem),
        cost_estimate=pl.CostEstimate(flops=1 << 20, bytes_accessed=1 << 12, transcendentals=0),
        **how,
    )


def shape(dims, dtype=BF16):
    return jax.ShapeDtypeStruct(dims, dtype)


def whole(*dims):
    return pl.BlockSpec(dims, lambda *_: (0,) * len(dims))


def once(*dims):
    return pl.BlockSpec(dims, lambda *_: (0,) * len(dims), pipeline_mode=pl.Buffered(1))


def tables(length):
    frequency = THETA ** (-2.0 * np.arange(HD // 2, dtype=np.float32) / HD)
    angles = np.arange(length, dtype=np.float32)[:, None] * frequency.astype(np.float32)[None, :]
    cosine, sine = np.cos(angles), np.sin(angles)
    return np.tile(cosine, (1, 4)), np.concatenate([-sine, sine, -sine, sine], axis=1)


def turn(tile, cosine, sine, low):
    other = jnp.where(low, pltpu.roll(tile, LANES - 32, 1), pltpu.roll(tile, 32, 1))
    return tile * cosine + other * sine


def placed(tile, half):
    lane = lax.broadcasted_iota(jnp.int32, tile.shape, 1)
    alone = jnp.where((lane >= HD) == (half == 1), tile, 0.0)
    moved = pltpu.roll(alone, HD, 1)
    pair = (moved, alone) if half else (alone, moved)
    return [one.astype(BF16) for one in pair]


def attention_forward(x_ref, *refs, wide):
    blocks, (attn_order_ref, mlp_order_ref, plain_order_ref, cos_ref, sin_ref) = refs[:8], refs[8:13]
    two_ref, two_t_ref, keep_ref, send_ref, qkv_ref, probs_ref, mixed_ref, gain_ref, all_ref = refs[13:]

    @pl.when(pl.program_id(0) == 0)
    def _():
        n = all_ref.shape[0] // 16
        for c in range(2):
            near, over_y, over_x, over_both = blocks[4 * c : 4 * c + 4]
            pairs = ((near, over_y), (near, over_x), (over_x, over_both), (over_y, over_both))
            for i, pair in enumerate(pairs):
                for k, ref in enumerate(pair):
                    at = (8 * c + 2 * i + k) * n
                    all_ref[at : at + n, :] = ref[i % 2]

    length, features = x_ref.shape
    half = all_ref.shape[0] // 2
    to_order = attn_order_ref[:, :features]
    last = slice(wide - LANES, wide)
    gains = dot(all_ref[:, last], to_order, TN)
    gain_one, gain_two = gains[HD : HD + 1], gains[HD + 1 : HD + 2]
    gain_ref[...] = gains[HD : HD + 8]
    x = x_ref[...].astype(F32)
    r1 = lax.rsqrt(jnp.mean(x * x, axis=-1, keepdims=True) + EPSILON)
    normed = (x * r1 * gain_one).astype(BF16)
    spread = dot(normed, to_order, NT).astype(BF16)
    turned = dot(to_order, normed, NT).astype(BF16)
    keep_ref[:half, :] = turned[:half]
    send_ref[:half, :] = turned[half:]
    lane = lax.broadcasted_iota(jnp.int32, (length, LANES), 1)
    low = lane % HD < HD // 2
    cosine, sine = cos_ref[...], sin_ref[...]
    tiles, heads = [], {}
    for t in range(wide // LANES):
        cols = slice(t * LANES, (t + 1) * LANES)
        tile = dot(spread, all_ref[:, cols])
        if t * 2 < HQ + KV:
            tile = turn(tile, cosine, sine, low)
        if t == wide // LANES - 1:
            tile = jnp.where(lane < HD, tile, 0.0)
        short = tile.astype(BF16)
        qkv_ref[:, cols] = short
        tiles.append(short)
        for n in (2 * t, 2 * t + 1):
            if HQ <= n < HQ + 2 * KV:
                heads[n] = placed(tile, n % 2)
    causal = lax.broadcasted_iota(jnp.int32, (length, length), 0) >= lax.broadcasted_iota(
        jnp.int32, (length, length), 1
    )
    context = [None] * ((HQ + 1) // 2)
    for h in range(HQ):
        j, t, s = h // (HQ // KV), h // 2, h % 2
        scores = dot(tiles[t], heads[HQ + j][s], NT) * (1.0 / math.sqrt(HD))
        scores = jnp.where(causal, scores, -1e30)
        exponent = jnp.exp(scores - jnp.max(scores, axis=-1, keepdims=True))
        probs = exponent * (1.0 / jnp.sum(exponent, axis=-1, keepdims=True))
        probs = probs.astype(BF16)
        probs_ref[0, h] = probs
        part = dot(probs, heads[HQ + KV + j][s])
        context[t] = part if context[t] is None else context[t] + part
    context = jnp.concatenate([c.astype(BF16) for c in context], axis=1)
    spread = dot(context, attn_order_ref[...], NT).astype(BF16)
    mixed = x + dot(spread, all_ref[:, wide : wide + features])
    spread = dot(attn_order_ref[...], context, NT).astype(BF16)
    keep_ref[half:, :] = spread[:half]
    send_ref[half:, :] = spread[half:]
    mixed_ref[...] = mixed
    r2 = lax.rsqrt(jnp.mean(mixed * mixed, axis=-1, keepdims=True) + EPSILON)
    two = (mixed * r2 * gain_two).astype(BF16)
    two_ref[...] = dot(two, plain_order_ref[:, :features], NT).astype(BF16)
    two_t_ref[...] = dot(mlp_order_ref[:, :features], two, NT).astype(BF16)


def attention_backward(
    mine_ref, other_ref, plain_order_ref, mixed_ref, cot_ref, gain_ref, all_ref, order_ref, qkv_ref,
    probs_ref, cos_ref, sin_ref, x_ref, d_low_ref, d_high_ref, d_attn_ref, out_ref, grad_ref, *, wide
):
    length, features = mixed_ref.shape
    total = (mine_ref[...] + other_ref[...].astype(F32)).astype(BF16)
    d_two = dot(total, plain_order_ref[:, :features])
    mixed = mixed_ref[...]
    r2 = lax.rsqrt(jnp.mean(mixed * mixed, axis=-1, keepdims=True) + EPSILON)
    unit = mixed * r2
    e2 = d_two * gain_ref[1:2, :]
    d_mixed = cot_ref[...].astype(F32) + r2 * (e2 - unit * jnp.mean(e2 * unit, axis=-1, keepdims=True))
    d_attn = d_mixed.astype(BF16)
    d_attn_ref[:, :features] = d_attn
    d_attn_ref[:, features:] = jnp.zeros((length, d_attn_ref.shape[1] - features), BF16)
    grad_gain_two = jnp.sum(d_two * unit, axis=0, keepdims=True)
    d_context = dot(d_attn, all_ref[:, wide : wide + features], NT).astype(BF16)
    d_context = dot(d_context, order_ref[...]).astype(BF16)
    lane = lax.broadcasted_iota(jnp.int32, (length, LANES), 1)
    low = lane % HD < HD // 2
    cosine, sine = cos_ref[...], -sin_ref[...]

    def tile_of(n):
        t = n // 2
        return qkv_ref[:, t * LANES : (t + 1) * LANES]

    d_tiles = [None] * ((HQ + 2 * KV + 1) // 2)

    def add(t, part):
        d_tiles[t] = part if d_tiles[t] is None else d_tiles[t] + part

    groups = HQ // KV
    for j in range(KV):
        keys = placed(tile_of(HQ + j).astype(F32), (HQ + j) % 2)
        values = placed(tile_of(HQ + KV + j).astype(F32), (HQ + KV + j) % 2)
        d_key, d_value = [None, None], [None, None]
        for h in range(j * groups, (j + 1) * groups):
            t, s = h // 2, h % 2
            d_con = d_context[:, t * LANES : (t + 1) * LANES]
            probs = probs_ref[0, h]
            wide_probs = probs.astype(F32)
            d_probs = dot(d_con, values[s], NT)
            inner = jnp.sum(d_probs * wide_probs, axis=-1, keepdims=True)
            d_scores = (wide_probs * (d_probs - inner) * (1.0 / math.sqrt(HD))).astype(BF16)
            add(t, dot(d_scores, keys[s]))
            part = dot(d_scores, tile_of(h), TN)
            d_key[s] = part if d_key[s] is None else d_key[s] + part
            part = dot(probs, d_con, TN)
            d_value[s] = part if d_value[s] is None else d_value[s] + part
        for n, pair in ((HQ + j, d_key), (HQ + KV + j, d_value)):
            here = n % 2
            mask = (lane >= HD) == (here == 1)
            total = jnp.where(mask, pair[here] + pltpu.roll(pair[1 - here], HD, 1), 0.0)
            add(n // 2, total)
    for t, tile in enumerate(d_tiles):
        if t * 2 < HQ + KV:
            tile = turn(tile, cosine, sine, low)
        ref, at = (d_low_ref, t * LANES) if t * LANES < d_low_ref.shape[1] else (d_high_ref, t * LANES - d_low_ref.shape[1])
        ref[:, at : at + LANES] = tile.astype(BF16)
    split = d_low_ref.shape[1]
    d_normed = dot(d_low_ref[...], all_ref[:, :split], NT) + dot(d_high_ref[...], all_ref[:, split:wide], NT)
    d_normed = d_normed.astype(BF16)
    d_normed = dot(d_normed, order_ref[:, :features])
    x = x_ref[...].astype(F32)
    r1 = lax.rsqrt(jnp.mean(x * x, axis=-1, keepdims=True) + EPSILON)
    unit = x * r1
    e1 = d_normed * gain_ref[0:1, :]
    out = d_mixed + r1 * (e1 - unit * jnp.mean(e1 * unit, axis=-1, keepdims=True))
    out_ref[...] = out.astype(BF16)
    grad_gain_one = jnp.sum(d_normed * unit, axis=0, keepdims=True)
    grads = jnp.concatenate([grad_gain_one, grad_gain_two, jnp.zeros((6, features), F32)], axis=0)


    @pl.when(pl.program_id(0) == 0)
    def _():
        grad_ref[...] = grads

    @pl.when(pl.program_id(0) > 0)
    def _():
        grad_ref[...] += grads


def flipped(array, axis, block):
    n = array.shape[axis] // block
    parts = [lax.slice_in_dim(array, i * block, (i + 1) * block, axis=axis) for i in range(n)]
    return jnp.concatenate([parts[i ^ 1] for i in range(n)], axis=axis)


def row_quarters(w, quarter, qr):
    dr, n = w.shape
    parts = []
    for q in range(4):
        part = w[min(q * quarter, dr) : min((q + 1) * quarter, dr), :]
        parts.append(jnp.concatenate([part, jnp.zeros((qr - part.shape[0], n), F32)], axis=0))
    return parts


def pieces_kernel(
    place_ref, wq_ref, wk_ref, wv_ref, wo_ref, g1_ref, g2_ref, wg_ref, wu_ref, wd_ref, attn_ref, mlp_ref,
    *, quarter, qr, pr, fr, wide
):
    rep, dr = place_ref[1], wq_ref.shape[0]

    def store(at, w):
        parts = row_quarters(w, quarter, qr)
        for s in range(2):
            attn_ref[s, :, at : at + w.shape[1]] = jnp.where(rep == 0, parts[s], parts[2 + s]).astype(BF16)

    wide_of = lambda ref: ref[...].astype(F32)
    eye = (
        lax.broadcasted_iota(jnp.int32, (dr, dr), 0) == lax.broadcasted_iota(jnp.int32, (dr, dr), 1)
    ).astype(F32)
    columns = [jnp.sum(eye * wide_of(ref), axis=1, keepdims=True) for ref in (g1_ref, g2_ref)]
    blank = jnp.zeros((dr, wide - wq_ref.shape[1] - 2 * wk_ref.shape[1] - 2), F32)
    store(0, jnp.concatenate([wide_of(wq_ref), wide_of(wk_ref), wide_of(wv_ref)] + columns + [blank], axis=1))
    w = wide_of(wo_ref)
    store(wide, jnp.concatenate([w, jnp.zeros((dr, attn_ref.shape[2] - wide - w.shape[1]), F32)], axis=1))
    halves = []
    for ref in (wg_ref, wu_ref):
        w = wide_of(ref)
        chunks = [w[:, i * fr : (i + 1) * fr] for i in range(w.shape[1] // fr)]
        halves.append([jnp.concatenate(chunks[c::2], axis=1) for c in range(2)])
    row = jnp.concatenate([halves[0][0], halves[1][0], halves[0][1], halves[1][1]], axis=1)
    rows, lanes = pr, mlp_ref.shape[1]
    row = jnp.concatenate([row, jnp.zeros((rows - dr, row.shape[1]), F32)], axis=0).astype(BF16)
    for g in range(4):
        mlp_ref[g * rows : (g + 1) * rows, :] = row[:, g * lanes : (g + 1) * lanes]
    at, n = 4 * rows, wd_ref.shape[1]
    mlp_ref[at : at + fr, :n] = wd_ref[...]
    mlp_ref[at : at + fr, n:] = jnp.zeros((fr, lanes - n), BF16)
    if at + fr < mlp_ref.shape[0]:
        mlp_ref[at + fr :, :] = jnp.zeros((mlp_ref.shape[0] - at - fr, lanes), BF16)


def tie_kernel(*refs):
    del refs


def add_kernel(*refs, n_alpha, count, form):
    totals = [ref[...].astype(F32) for ref in refs[:count]]
    alpha, beta = functools.reduce(jnp.add, totals[:n_alpha]), functools.reduce(jnp.add, totals[n_alpha:])
    if form == "apart":
        refs[-2][:, :, 0] = alpha.astype(BF16)
        refs[-1][:, :, 0] = beta.astype(BF16)
    elif form == "stack":
        refs[-1][0, :, :, 0] = alpha.astype(BF16)
        refs[-1][1, :, :, 0] = beta.astype(BF16)
    else:
        for c in range(alpha.shape[1]):
            refs[-1][c, :, 0] = alpha[:, c].astype(BF16)
            refs[-1][c, :, 1] = beta[:, c].astype(BF16)


def shards_kernel(place_ref, mine_ref, other_ref, got_ref, got_other_ref, gate_ref, up_ref, *, quarter, fr):
    core, rep = place_ref[0], place_ref[1]
    dr = gate_ref.shape[0]
    for at, out_ref in ((0, gate_ref), (1, up_ref)):
        sides = []
        for c, mine, other in ((0, mine_ref, other_ref), (1, got_ref, got_other_ref)):
            a, b = mine[c, at].astype(F32), other[c, at].astype(F32)
            low, high = jnp.where(rep == 0, a, b), jnp.where(rep == 0, b, a)
            rows = [half[s][:quarter] for half in (low, high) for s in range(2)]
            sides.append(jnp.concatenate(rows, axis=0)[:dr])
        even, odd = jnp.where(core == 0, sides[0], sides[1]), jnp.where(core == 0, sides[1], sides[0])
        chunks = []
        for k in range(even.shape[1] // fr):
            chunks += [even[:, k * fr : (k + 1) * fr], odd[:, k * fr : (k + 1) * fr]]
        out_ref[...] = jnp.concatenate(chunks, axis=1)


def attn_shards_kernel(place_ref, mine_ref, other_ref, query_ref, key_ref, value_ref, gains_ref, out_ref, *, quarter, wide):
    rep, dr = place_ref[1], out_ref.shape[0]
    a, b = mine_ref[0, 0].astype(F32), other_ref[0, 0].astype(F32)
    low, high = jnp.where(rep == 0, a, b), jnp.where(rep == 0, b, a)
    rows = jnp.concatenate([half[s][:quarter] for half in (low, high) for s in range(2)], axis=0)[:dr]
    at = 0
    for ref in (query_ref, key_ref, value_ref, gains_ref):
        ref[...] = rows[:, at : at + ref.shape[1]]
        at += ref.shape[1]
    out_ref[...] = rows[:, wide : wide + out_ref.shape[1]]


def order_kernel(*refs):
    for feat_ref, out_ref in zip(refs[:3], refs[3:]):
        column = lax.broadcasted_iota(jnp.int32, out_ref.shape, 1)
        out_ref[...] = (feat_ref[...] == column).astype(F32).astype(BF16)


def copy_kernel(in_ref, *refs):
    out_ref, n = refs[-1], in_ref.shape[1]
    out_ref[:, :n] = in_ref[...]
    out_ref[:, n:] = jnp.zeros((out_ref.shape[0], out_ref.shape[1] - n), BF16)


def sum_kernel(*refs):
    n = refs[-1].shape[1]
    refs[-1][...] = functools.reduce(jnp.add, [r[:, :n].astype(F32) for r in (refs[:3] if len(refs) > 3 else refs[:-1])]).astype(refs[-1].dtype)


def split_attn_kernel(*refs, count):
    rows = refs[0].shape[1]
    for i, ref in enumerate(refs[:count]):
        for s in range(2):
            refs[-1][s, i * rows : (i + 1) * rows, :] = ref[s]


def join_kernel(near_ref, y_ref, x_ref, xy_ref, out_ref):
    rows = near_ref.shape[1]
    blocks = ((near_ref, y_ref), (near_ref, x_ref), (x_ref, xy_ref), (y_ref, xy_ref))
    for i, pair in enumerate(blocks):
        for k, ref in enumerate(pair):
            at = (2 * i + k) * rows
            out_ref[at : at + rows, :] = ref[i % 2]


def attn_grad_kernel(keep_ref, got_ref, *refs, wide, gain_at):
    mine, other = refs[:3], refs[3:6]
    gains_ref, gains_oth_ref, order_ref = refs[6:9]
    out_refs = refs[-4:]
    half, features = keep_ref.shape[0] // 2, gains_ref.shape[1]
    n = out_refs[0].shape[0]
    gains = (gains_ref[...] + gains_oth_ref[...]).astype(BF16)
    gains = dot(order_ref[:half, :features], gains, NT)
    lane = lax.broadcasted_iota(jnp.int32, (half, LANES), 1) + (wide - LANES)
    tile = jnp.where(lane == gain_at, gains[:, 0:1], 0.0) + jnp.where(lane == gain_at + 1, gains[:, 1:2], 0.0)
    column = 0
    for k in range(3):
        at = slice(half, 2 * half) if k == 2 else slice(0, half)
        grad = dot(keep_ref[at, :], mine[k][...]) + dot(got_ref[at, :], other[k][...])
        if k == 1:
            grad = jnp.concatenate([grad[:, :-LANES], grad[:, -LANES:] + tile], axis=1)
        for i, ref in enumerate(out_refs):
            ref[:, column : column + grad.shape[1]] = grad[i * n : (i + 1) * n].astype(BF16)
        column += grad.shape[1]


def mlp_kernel(place_ref, two_ref, two_oth_ref, t_ref, t_oth_ref, cot_ref, cot_oth_ref, w_ref, *refs):
    sends, keeps = refs[:2], refs[2:4]
    down_ref, out_ref, out_oth_ref, d_two_ref, d_two_oth_ref = refs[4:9]
    acts, acts_t, cots, wg, wu, wd, hidden, d_gate, d_up = refs[9:18]
    chunks, down, out, out_oth, d_two, d_two_oth, in_sems, out_sems = refs[18:]
    rows = cot_ref.shape[0]
    width, half_ff, features = acts_t.shape[0], hidden.shape[1], down.shape[1]
    shards, pr = wg.shape[0], wg.shape[1]
    fr, plain, n, block = 2 * half_ff // shards, shards * pr, width // 4, width // 8
    core = place_ref[0]
    started = []

    def fetch(source, target):
        copy = pltpu.make_async_copy(source, target, in_sems.at[len(started)])
        copy.start()
        started.append(copy)
        return copy

    first = [fetch(two_ref, acts.at[pl.ds(0, rows), :])]
    gate_in = fetch(w_ref.at[:, pl.ds(2 * pr * core, pr), :], wg)
    up_in = fetch(w_ref.at[:, pl.ds(2 * pr * core + pr, pr), :], wu)
    cots_in = [fetch(cot_ref, cots.at[pl.ds(0, rows), :])]
    down_in = [
        fetch(
            w_ref.at[2 * k + core, pl.ds(4 * pr, fr), pl.ds(0, wd.shape[1])], wd.at[pl.ds(k * fr, fr), :]
        )
        for k in range(shards // 2)
    ]
    second = [fetch(two_oth_ref, acts.at[pl.ds(rows, rows), :]), fetch(cot_oth_ref, cots.at[pl.ds(rows, rows), :])]
    turned = [fetch(t_ref, acts_t.at[:, pl.ds(0, rows)])]
    for k in range(8):
        source = t_oth_ref.at[pl.ds((k ^ 1) * block, block), :]
        turned.append(fetch(source, acts_t.at[pl.ds(k * block, block), pl.ds(rows, rows)]))

    def wait(copies):
        for copy in copies:
            copy.wait()

    for half in range(2):
        at = slice(half * rows, (half + 1) * rows)
        wait(second if half else first + [gate_in])
        gate = dot(acts[at, :], wg[...].reshape(plain, half_ff))
        if not half:
            wait([up_in])
        up = dot(acts[at, :], wu[...].reshape(plain, half_ff))
        sg = 1.0 / (1.0 + jnp.exp(-gate))
        silu = gate * sg
        hidden[at, :] = (silu * up).astype(BF16)
        if not half:
            wait(cots_in + down_in)
        d_hidden = dot(cots[at, :], wd[...], NT)
        d_gate[at, :] = (d_hidden * up * sg * (1.0 + gate * (1.0 - sg))).astype(BF16)
        d_up[at, :] = (d_hidden * silu).astype(BF16)
    wait(turned)

    going = []

    def put(source, target):
        copy = pltpu.make_async_copy(source, target, out_sems.at[len(going)])
        copy.start()
        going.append(copy)

    for targets, first_row in ((sends, 2 * n), (keeps, 0)):
        for i, d in ((0, d_gate), (1, d_up)):
            grad = dot(acts_t[first_row : first_row + 2 * n, :], d[...])
            for k in range(2):
                slot = len(going) % chunks.shape[0]
                if len(going) >= chunks.shape[0]:
                    going[len(going) - chunks.shape[0]].wait()
                chunks[slot] = grad[k * n : (k + 1) * n].astype(BF16)
                put(chunks.at[slot], targets[k].at[i])
    count = len(going)
    down[...] = dot(hidden[...], cots[:, :features], TN).astype(BF16)
    put(down, down_ref)

    def back(at):
        return dot(d_gate[at, :], wg[...].reshape(plain, half_ff), NT) + dot(
            d_up[at, :], wu[...].reshape(plain, half_ff), NT
        )

    d_two[...] = back(slice(0, rows))
    put(d_two, d_two_ref)
    out[...] = dot(hidden[:rows, :], wd[:, :features])
    put(out, out_ref)
    d_two_oth[...] = back(slice(rows, 2 * rows)).astype(BF16)
    put(d_two_oth, d_two_oth_ref)
    out_oth[...] = dot(hidden[rows:, :], wd[...]).astype(BF16)
    put(out_oth, out_oth_ref)
    wait(going[count - chunks.shape[0] :])


def on_device(
    tokens, cotangent, attn_gain, w_query, w_key, w_value, w_out, mlp_gain, w_gate, w_up, w_down
):
    shards = lax.axis_size("shard")
    chips = shards // 2
    zs = chips // 2
    me, rep = lax.axis_index("shard"), lax.axis_index("rep")
    core = me % 2
    micro, batch, length, features = tokens.shape
    seqs = micro * batch
    rows = seqs * length
    dr = features // shards
    quarter = -(-dr // 4)
    qr = -(-quarter // 8) * 8
    pr = -(-dr // 16) * 16
    plain = shards * pr
    width = shards * 4 * qr
    half = width // 2
    block = zs * qr
    fr = w_down.shape[0]
    half_ff = chips * fr
    nq, nk = HQ * HD, KV * HD
    nqkv = nq + 2 * nk
    wide = -(-(nqkv + 2) // LANES) * LANES
    padded = -(-features // LANES) * LANES
    full = wide + padded
    cosine, sine = (jnp.asarray(t) for t in tables(length))
    place = jnp.stack([core, rep]).astype(jnp.int32)
    in_smem = pl.BlockSpec(memory_space=pltpu.SMEM)
    in_vmem = pl.BlockSpec(memory_space=pltpu.VMEM)
    anywhere = pl.BlockSpec(memory_space=pl.ANY)
    z_bits = zs.bit_length() - 1
    z_flip = np.array([sum(((i >> b) & 1) << (z_bits - 1 - b) for b in range(z_bits)) for i in range(zs)])

    def over(array, flip):
        return lax.ppermute(array, "shard", [(s, s ^ flip) for s in range(shards)])

    def over_core(array):
        return over(array, 1)

    def over_y(array):
        return over(array, 2)

    def over_rep(array):
        return lax.ppermute(array, "rep", [(0, 1), (1, 0)])

    def tie(arrays, *deps):
        return call(
            tie_kernel, [shape(a.shape, a.dtype) for a in arrays],
            in_specs=[anywhere] * (len(arrays) + len(deps)), out_specs=[anywhere] * len(arrays),
            input_output_aliases={i: i for i in range(len(arrays))},
        )(*arrays, *deps)

    def small(kernel, outs, arrays, deps=()):
        return call(
            kernel, outs, in_specs=[in_vmem] * len(arrays) + [anywhere] * len(deps), vmem=16 << 20
        )(*arrays, *deps)

    even = [[2 * k + c for k in range(chips)] for c in range(2)]

    def feature_of(dims):
        sizes = {"core": 2, "split": 2, "f1": 2, "f2": 2, "z": zs, "row": qr}
        grid = np.meshgrid(*[np.arange(sizes[d]) for d in dims], indexing="ij")
        at = {d: g.reshape(-1) for d, g in zip(dims, grid)}
        x_flip = np.where(at["split"] == 0, at["f1"], at["f2"])
        y_flip = np.where(at["split"] == 0, at["f2"], at["f1"])
        shard = me ^ jnp.asarray(at["core"] + 2 * (y_flip + 2 * z_flip[at["z"]]), jnp.int32)
        part = 2 * (rep ^ jnp.asarray(x_flip, jnp.int32)) + jnp.asarray(at["split"], jnp.int32)
        inside = part * quarter + jnp.asarray(at["row"], jnp.int32)
        real = jnp.asarray(at["row"] < quarter) & (inside < dr)
        return jnp.where(real, shard * dr + inside, -1)[:, None]

    feats = [feature_of(("core", "f1", "split", "f2", "z", "row")), feature_of(("f1", "split", "core", "f2", "z", "row"))]
    shard, row = np.repeat(np.arange(shards), pr), np.tile(np.arange(pr), shards)
    feats.append(jnp.asarray(np.where(row < dr, shard * dr + row, -1)[:, None], jnp.int32))
    attn_order, mlp_order, plain_order = call(
        order_kernel, [shape((f.shape[0], padded)) for f in feats], grid=(1,), in_specs=[in_vmem] * 3,
        out_specs=[whole(f.shape[0], padded) for f in feats],
    )(*feats)

    floor = (16 << 20) // (2 * half_ff * shards) + 1
    depth = -(-max(4 * pr + fr, floor) // 16) * 16
    attn_piece, mlp_piece = call(
        functools.partial(pieces_kernel, quarter=quarter, qr=qr, pr=pr, fr=fr, wide=wide),
        [shape((2, qr, full)), shape((depth, half_ff))],
        grid=(1,),
        in_specs=[in_smem] + [
            whole(*w.shape)
            for w in (w_query, w_key, w_value, w_out, attn_gain[None], mlp_gain[None], w_gate, w_up, w_down)
        ],
        out_specs=[in_vmem, whole(depth, half_ff)],
    )(place, w_query, w_key, w_value, w_out, attn_gain[None], mlp_gain[None], w_gate, w_up, w_down)
    mlp = lax.all_gather(mlp_piece, "shard", axis=0, tiled=True).reshape(shards, depth, half_ff)
    parts = [attn_piece if z == 0 else over(attn_piece, 4 * z) for z in z_flip]
    x = tokens.reshape(rows, features)
    cot = cotangent.reshape(rows, features)
    cot_wide = small(copy_kernel, shape((rows, padded)), [cot], [attn_piece])
    cot_oth = over_core(cot_wide)
    attn_near = small(
        functools.partial(split_attn_kernel, count=zs), shape((2, block, full)), parts, [cot_oth, x, attn_order]
    )
    attn_y, attn_x = over_y(attn_near), over_rep(attn_near)
    attn_blocks = [attn_near, attn_y, attn_x, over_rep(attn_y)]
    attn_blocks += [over_core(b) for b in attn_blocks]

    by_rows = lambda cols: pl.BlockSpec((length, cols), lambda i: (i, 0))
    by_cols = lambda n: pl.BlockSpec((n, length), lambda i: (0, i))
    by_once = lambda *arrays: [once(*a.shape) for a in arrays]
    by_probs = pl.BlockSpec((1, HQ, length, length), lambda i: (i, 0, 0, 0))
    rows_at = lambda i, cols: pl.BlockSpec((length, cols), lambda _: (i, 0))
    shared = (*attn_blocks, attn_order, mlp_order, plain_order, cosine, sine)
    two, two_t, keep_t, send_t, qkv, probs, mixed, gain_rows, attn_all = call(
        functools.partial(attention_forward, wide=wide),
        [
            shape((rows, plain)), shape((width, rows)), shape((width, rows)), shape((width, rows)),
            shape((rows, wide)), shape((seqs, HQ, length, length)), shape((rows, features), F32),
            shape((8, features), F32), shape((width, full)),
        ],
        grid=(seqs,),
        in_specs=[by_rows(features)] + by_once(*shared),
        out_specs=[by_rows(plain)] + [by_cols(width)] * 3
        + [by_rows(wide), by_probs, by_rows(features), once(8, features), once(width, full)],
    )(x, *shared)

    n = width // 4
    (
        alpha_send, beta_send, alpha_keep, beta_keep, grad_down, out_part, out_other, d_two_mine, d_two_other
    ) = call(
        mlp_kernel,
        [shape((2, n, half_ff))] * 4 + [shape((half_ff, features))]
        + [shape((rows, features), F32), shape((rows, padded)), shape((rows, plain), F32), shape((rows, plain))],
        in_specs=[in_smem] + [anywhere] * 7,
        out_specs=[anywhere] * 9,
        scratch_shapes=[
            pltpu.VMEM((2 * rows, plain), BF16), pltpu.VMEM((width, 2 * rows), BF16), pltpu.VMEM((2 * rows, padded), BF16),
            pltpu.VMEM((shards, pr, half_ff), BF16), pltpu.VMEM((shards, pr, half_ff), BF16),
            pltpu.VMEM((half_ff, padded), BF16),
            pltpu.VMEM((2 * rows, half_ff), BF16), pltpu.VMEM((2 * rows, half_ff), BF16), pltpu.VMEM((2 * rows, half_ff), BF16),
            pltpu.VMEM((4, n, half_ff), BF16), pltpu.VMEM((half_ff, features), BF16), pltpu.VMEM((rows, features), F32),
            pltpu.VMEM((rows, padded), BF16), pltpu.VMEM((rows, plain), F32), pltpu.VMEM((rows, plain), BF16),
            pltpu.SemaphoreType.DMA((15 + chips,)), pltpu.SemaphoreType.DMA((13,)),
        ],
    )(place, two, over_core(two), two_t, over_core(two_t), cot_wide, cot_oth, mlp)
    grad_down = lax.psum_scatter(
        grad_down, "shard", scatter_dimension=0, tiled=True, axis_index_groups=even
    )

    def add(alpha, beta, at, size, form, deps):
        arrays = [p[0] for p in alpha + beta]
        j, cores, _, _, n = arrays[0].shape
        one = shape((j, cores, 1, size, n))
        outs = {"apart": [one, one], "stack": shape((2,) + one.shape), "last": shape((cores, j, 2, size, n))}[form]
        specs = []
        for _, lead, f in alpha + beta:
            spot = ((0, 0, f, at // size, 0), (j, cores, None, size, n))
            if lead is not None:
                spot = ((lead,) + spot[0], (None,) + spot[1])
            specs.append(pl.BlockSpec(spot[1], functools.partial(lambda where, _: where, spot[0])))
        return call(
            functools.partial(add_kernel, n_alpha=len(alpha), count=len(arrays), form=form), outs, grid=(1,),
            in_specs=specs + [anywhere] * len(deps),
            out_specs=[whole(*o.shape) for o in outs] if form == "apart" else whole(*outs.shape),
            vmem=ADD_VMEM,
        )(*arrays, *deps)

    class Reduction:
        def __init__(self, alpha_keep, beta_keep, alpha_send, beta_send):
            self.early = [[alpha_keep, over_rep(alpha_send)], [beta_keep, over_y(beta_send)]]
            self.late = []
            self.both = []
            self.size = block

        def parts(self, f):
            return [
                [(a, None, f) for a in self.early[s]]
                + [(pair[s], None, 0) for pair in self.late] + [(a, s, 0) for a in self.both]
                for s in range(2)
            ]

        def second(self, *deps):
            alpha_sent, beta_sent = add(*self.parts(1), 0, block, "apart", deps)
            self.late.append((over_y(alpha_sent), over_rep(beta_sent)))
            return [alpha_sent, beta_sent]

        def z(self, *deps):
            self.size //= 2
            sent = add(*self.parts(0), self.size, self.size, "stack", deps)
            self.both.append(over(sent, 4 << (len(self.both))))
            return [sent]

        def last(self, *deps):
            mine = add(*self.parts(0), 0, qr, "last", deps)
            return mine, over_rep(mine)

    mlp_sum = Reduction(
        *[a.reshape(2, 2, 2, block, half_ff) for a in (alpha_keep, beta_keep, alpha_send, beta_send)]
    )

    low = wide // LANES // 8 * 8 * LANES
    arrays = (gain_rows, attn_all, attn_order)
    d_low, d_high, d_attn, grad_tokens, grad_gains = call(
        functools.partial(attention_backward, wide=wide),
        [
            shape((rows, low)), shape((rows, wide - low)), shape((rows, padded)), shape((rows, features)),
            shape((8, features), F32),
        ],
        grid=(seqs,),
        in_specs=[by_rows(plain), by_rows(plain)] + by_once(plain_order) + [by_rows(features)] * 2
        + by_once(*arrays) + [by_rows(wide), by_probs] + by_once(cosine, sine) + [by_rows(features)],
        out_specs=[by_rows(low), by_rows(wide - low), by_rows(padded), by_rows(features), whole(8, features)],
    )(d_two_mine, over_core(d_two_other), plain_order, mixed, cot, *arrays, qkv, probs, cosine, sine, x)
    sent = mlp_sum.second(d_low)
    n = half // 4
    arrays = [d_low, d_high, d_attn]
    arrays = [
        keep_t, over_core(send_t), *arrays, *[over_core(a) for a in arrays], grad_gains, over_core(grad_gains), attn_order
    ]
    attn_grads = call(
        functools.partial(attn_grad_kernel, wide=wide, gain_at=nqkv),
        [shape((n, full))] * 4,
        grid=(1,),
        in_specs=by_once(*arrays) + [anywhere] * 2,
        out_specs=[whole(n, full)] * 4,
        vmem=32 << 20,
    )(*arrays, *sent)
    attn_sum = Reduction(*[a.reshape(1, 1, 2, block, full) for a in attn_grads])
    out_oth = over_core(out_other)
    for i in range(seqs):
        output = call(
            sum_kernel, shape((rows, features)), grid=(1,),
            in_specs=[rows_at(i, features), rows_at(i, features), rows_at(i, padded)]
            + [anywhere] * (2 if i else 1),
            out_specs=rows_at(i, features), input_output_aliases={4: 0} if i else {},
        )(out_part, mixed, out_oth, attn_grads[0], *([output] if i else []))
    sent = mlp_sum.z(attn_grads[0], output)
    sent = attn_sum.second(*sent)
    for step in range(z_bits):
        if step:
            sent = mlp_sum.z(*sent)
        if step == z_bits - 1:
            mlp_mine, mlp_from = None, None
        sent = attn_sum.z(*sent)
    mlp_mine, mlp_from = mlp_sum.last(*sent)
    attn_mine, attn_from = attn_sum.last(mlp_mine)

    grad_gate, grad_up = call(
        functools.partial(shards_kernel, quarter=quarter, fr=fr),
        [shape((dr, 2 * half_ff), F32)] * 2,
        grid=(1,),
        in_specs=[in_smem] + by_once(*[mlp_mine] * 4), out_specs=[whole(dr, 2 * half_ff)] * 2,
    )(place, mlp_mine, mlp_from, over_core(mlp_mine), over_core(mlp_from))
    down_oth = over_rep(grad_down)
    grad_down = call(
        sum_kernel, shape(w_down.shape, F32), grid=(1,), in_specs=[whole(*w_down.shape)] * 2,
        out_specs=whole(*w_down.shape),
    )(grad_down, down_oth)
    grad_query, grad_key, grad_value, grad_gains, grad_out = call(
        functools.partial(attn_shards_kernel, quarter=quarter, wide=wide),
        [shape((dr, n), F32) for n in (nq, nk, nk, 2, features)],
        grid=(1,),
        in_specs=[in_smem] + by_once(attn_mine, attn_mine), out_specs=[whole(dr, n) for n in (nq, nk, nk, 2, features)],
    )(place, attn_mine, attn_from)
    dims = tokens.shape
    return (
        output.reshape(dims), grad_tokens.reshape(dims), grad_gains[:, 0], grad_query, grad_key, grad_value,
        grad_out, grad_gains[:, 1], grad_gate, grad_up, grad_down,
    )


def solution(mesh):
    data = P(None, ("rep", "shard"), None, None)
    vector, matrix = P("shard"), P("shard", None)
    weights = (vector, matrix, matrix, matrix, matrix, vector, matrix, matrix, matrix)
    return jax.shard_map(
        on_device,
        mesh=mesh,
        in_specs=(data, data) + weights,
        out_specs=(data, data) + weights,
        check_vma=False,
    )
```

```python
import functools
import math

import jax
import jax.numpy as jnp
import numpy as np
from jax import lax
from jax.experimental import pallas as pl
from jax.experimental.pallas import tpu as pltpu
from jax.sharding import PartitionSpec as P

HQ = 15
KV = 5
HD = 64
EPSILON = 1e-05
THETA = 100000.0
F32 = jnp.float32
BF16 = jnp.bfloat16
LANES = 128
COLS = 256
NN = ((1,), (0,))
NT = ((1,), (1,))
TN = ((0,), (0,))
VMEM = 60 << 20
ADD_VMEM = 16 << 20


def dot(a, b, contract=NN):
    return lax.dot_general(a, b, (contract, ((), ())), preferred_element_type=F32)


def call(kernel, out_shape, *, vmem=VMEM, **how):
    return pl.pallas_call(
        kernel,
        out_shape=out_shape,
        compiler_params=pltpu.CompilerParams(vmem_limit_bytes=vmem),
        cost_estimate=pl.CostEstimate(flops=1 << 20, bytes_accessed=1 << 12, transcendentals=0),
        **how,
    )


def shape(dims, dtype=BF16):
    return jax.ShapeDtypeStruct(dims, dtype)


def whole(*dims):
    return pl.BlockSpec(dims, lambda *_: (0,) * len(dims))


def once(*dims):
    return pl.BlockSpec(dims, lambda *_: (0,) * len(dims), pipeline_mode=pl.Buffered(1))


def tables(length):
    frequency = THETA ** (-2.0 * np.arange(HD // 2, dtype=np.float32) / HD)
    angles = np.arange(length, dtype=np.float32)[:, None] * frequency.astype(np.float32)[None, :]
    cosine, sine = np.cos(angles), np.sin(angles)
    return np.tile(cosine, (1, 4)), np.concatenate([-sine, sine, -sine, sine], axis=1)


def turn(tile, cosine, sine, low):
    other = jnp.where(low, pltpu.roll(tile, LANES - 32, 1), pltpu.roll(tile, 32, 1))
    return tile * cosine + other * sine


def placed(tile, half):
    lane = lax.broadcasted_iota(jnp.int32, tile.shape, 1)
    alone = jnp.where((lane >= HD) == (half == 1), tile, 0.0)
    moved = pltpu.roll(alone, HD, 1)
    pair = (moved, alone) if half else (alone, moved)
    return [one.astype(BF16) for one in pair]


def attention_forward(x_ref, *refs, wide):
    blocks, (attn_order_ref, mlp_order_ref, plain_order_ref, cos_ref, sin_ref) = refs[:8], refs[8:13]
    two_ref, two_t_ref, keep_ref, send_ref, qkv_ref, probs_ref, mixed_ref, gain_ref, all_ref = refs[13:]

    @pl.when(pl.program_id(0) == 0)
    def _():
        n = all_ref.shape[0] // 16
        for c in range(2):
            near, over_y, over_x, over_both = blocks[4 * c : 4 * c + 4]
            pairs = ((near, over_y), (near, over_x), (over_x, over_both), (over_y, over_both))
            for i, pair in enumerate(pairs):
                for k, ref in enumerate(pair):
                    at = (8 * c + 2 * i + k) * n
                    all_ref[at : at + n, :] = ref[i % 2]

    length, features = x_ref.shape
    half = all_ref.shape[0] // 2
    to_order = attn_order_ref[:, :features]
    last = slice(wide - LANES, wide)
    gains = dot(all_ref[:, last], to_order, TN)
    gain_one, gain_two = gains[HD : HD + 1], gains[HD + 1 : HD + 2]
    gain_ref[...] = gains[HD : HD + 8]
    x = x_ref[...].astype(F32)
    r1 = lax.rsqrt(jnp.mean(x * x, axis=-1, keepdims=True) + EPSILON)
    normed = (x * r1 * gain_one).astype(BF16)
    spread = dot(normed, to_order, NT).astype(BF16)
    turned = dot(to_order, normed, NT).astype(BF16)
    keep_ref[:half, :] = turned[:half]
    send_ref[:half, :] = turned[half:]
    lane = lax.broadcasted_iota(jnp.int32, (length, LANES), 1)
    low = lane % HD < HD // 2
    cosine, sine = cos_ref[...], sin_ref[...]
    tiles, heads = [], {}
    for t in range(wide // LANES):
        cols = slice(t * LANES, (t + 1) * LANES)
        tile = dot(spread, all_ref[:, cols])
        if t * 2 < HQ + KV:
            tile = turn(tile, cosine, sine, low)
        if t == wide // LANES - 1:
            tile = jnp.where(lane < HD, tile, 0.0)
        short = tile.astype(BF16)
        qkv_ref[:, cols] = short
        tiles.append(short)
        for n in (2 * t, 2 * t + 1):
            if HQ <= n < HQ + 2 * KV:
                heads[n] = placed(tile, n % 2)
    causal = lax.broadcasted_iota(jnp.int32, (length, length), 0) >= lax.broadcasted_iota(
        jnp.int32, (length, length), 1
    )
    context = [None] * ((HQ + 1) // 2)
    for h in range(HQ):
        j, t, s = h // (HQ // KV), h // 2, h % 2
        scores = dot(tiles[t], heads[HQ + j][s], NT) * (1.0 / math.sqrt(HD))
        scores = jnp.where(causal, scores, -1e30)
        exponent = jnp.exp(scores - jnp.max(scores, axis=-1, keepdims=True))
        probs = exponent * (1.0 / jnp.sum(exponent, axis=-1, keepdims=True))
        probs = probs.astype(BF16)
        probs_ref[0, h] = probs
        part = dot(probs, heads[HQ + KV + j][s])
        context[t] = part if context[t] is None else context[t] + part
    context = jnp.concatenate([c.astype(BF16) for c in context], axis=1)
    spread = dot(context, attn_order_ref[...], NT).astype(BF16)
    mixed = x + dot(spread, all_ref[:, wide : wide + features])
    spread = dot(attn_order_ref[...], context, NT).astype(BF16)
    keep_ref[half:, :] = spread[:half]
    send_ref[half:, :] = spread[half:]
    mixed_ref[...] = mixed
    r2 = lax.rsqrt(jnp.mean(mixed * mixed, axis=-1, keepdims=True) + EPSILON)
    two = (mixed * r2 * gain_two).astype(BF16)
    two_ref[...] = dot(two, plain_order_ref[:, :features], NT).astype(BF16)
    two_t_ref[...] = dot(mlp_order_ref[:, :features], two, NT).astype(BF16)


def attention_backward(
    mine_ref, other_ref, plain_order_ref, mixed_ref, cot_ref, gain_ref, all_ref, order_ref, qkv_ref,
    probs_ref, cos_ref, sin_ref, x_ref, d_low_ref, d_high_ref, d_attn_ref, out_ref, grad_ref, *, wide
):
    length, features = mixed_ref.shape
    total = (mine_ref[...] + other_ref[...].astype(F32)).astype(BF16)
    d_two = dot(total, plain_order_ref[:, :features])
    mixed = mixed_ref[...]
    r2 = lax.rsqrt(jnp.mean(mixed * mixed, axis=-1, keepdims=True) + EPSILON)
    unit = mixed * r2
    e2 = d_two * gain_ref[1:2, :]
    d_mixed = cot_ref[...].astype(F32) + r2 * (e2 - unit * jnp.mean(e2 * unit, axis=-1, keepdims=True))
    d_attn = d_mixed.astype(BF16)
    d_attn_ref[:, :features] = d_attn
    d_attn_ref[:, features:] = jnp.zeros((length, d_attn_ref.shape[1] - features), BF16)
    grad_gain_two = jnp.sum(d_two * unit, axis=0, keepdims=True)
    d_context = dot(d_attn, all_ref[:, wide : wide + features], NT).astype(BF16)
    d_context = dot(d_context, order_ref[...]).astype(BF16)
    lane = lax.broadcasted_iota(jnp.int32, (length, LANES), 1)
    low = lane % HD < HD // 2
    cosine, sine = cos_ref[...], -sin_ref[...]

    def tile_of(n):
        t = n // 2
        return qkv_ref[:, t * LANES : (t + 1) * LANES]

    d_tiles = [None] * ((HQ + 2 * KV + 1) // 2)

    def add(t, part):
        d_tiles[t] = part if d_tiles[t] is None else d_tiles[t] + part

    groups = HQ // KV
    for j in range(KV):
        keys = placed(tile_of(HQ + j).astype(F32), (HQ + j) % 2)
        values = placed(tile_of(HQ + KV + j).astype(F32), (HQ + KV + j) % 2)
        d_key, d_value = [None, None], [None, None]
        for h in range(j * groups, (j + 1) * groups):
            t, s = h // 2, h % 2
            d_con = d_context[:, t * LANES : (t + 1) * LANES]
            probs = probs_ref[0, h]
            wide_probs = probs.astype(F32)
            d_probs = dot(d_con, values[s], NT)
            inner = jnp.sum(d_probs * wide_probs, axis=-1, keepdims=True)
            d_scores = (wide_probs * (d_probs - inner) * (1.0 / math.sqrt(HD))).astype(BF16)
            add(t, dot(d_scores, keys[s]))
            part = dot(d_scores, tile_of(h), TN)
            d_key[s] = part if d_key[s] is None else d_key[s] + part
            part = dot(probs, d_con, TN)
            d_value[s] = part if d_value[s] is None else d_value[s] + part
        for n, pair in ((HQ + j, d_key), (HQ + KV + j, d_value)):
            here = n % 2
            mask = (lane >= HD) == (here == 1)
            total = jnp.where(mask, pair[here] + pltpu.roll(pair[1 - here], HD, 1), 0.0)
            add(n // 2, total)
    for t, tile in enumerate(d_tiles):
        if t * 2 < HQ + KV:
            tile = turn(tile, cosine, sine, low)
        ref, at = (d_low_ref, t * LANES) if t * LANES < d_low_ref.shape[1] else (d_high_ref, t * LANES - d_low_ref.shape[1])
        ref[:, at : at + LANES] = tile.astype(BF16)
    split = d_low_ref.shape[1]
    d_normed = dot(d_low_ref[...], all_ref[:, :split], NT) + dot(d_high_ref[...], all_ref[:, split:wide], NT)
    d_normed = d_normed.astype(BF16)
    d_normed = dot(d_normed, order_ref[:, :features])
    x = x_ref[...].astype(F32)
    r1 = lax.rsqrt(jnp.mean(x * x, axis=-1, keepdims=True) + EPSILON)
    unit = x * r1
    e1 = d_normed * gain_ref[0:1, :]
    out = d_mixed + r1 * (e1 - unit * jnp.mean(e1 * unit, axis=-1, keepdims=True))
    out_ref[...] = out.astype(BF16)
    grad_gain_one = jnp.sum(d_normed * unit, axis=0, keepdims=True)
    grads = jnp.concatenate([grad_gain_one, grad_gain_two, jnp.zeros((6, features), F32)], axis=0)


    @pl.when(pl.program_id(0) == 0)
    def _():
        grad_ref[...] = grads

    @pl.when(pl.program_id(0) > 0)
    def _():
        grad_ref[...] += grads


def flipped(array, axis, block):
    n = array.shape[axis] // block
    parts = [lax.slice_in_dim(array, i * block, (i + 1) * block, axis=axis) for i in range(n)]
    return jnp.concatenate([parts[i ^ 1] for i in range(n)], axis=axis)


def row_quarters(w, quarter, qr):
    dr, n = w.shape
    parts = []
    for q in range(4):
        part = w[min(q * quarter, dr) : min((q + 1) * quarter, dr), :]
        parts.append(jnp.concatenate([part, jnp.zeros((qr - part.shape[0], n), F32)], axis=0))
    return parts


def pieces_kernel(
    place_ref, wq_ref, wk_ref, wv_ref, wo_ref, g1_ref, g2_ref, wg_ref, wu_ref, wd_ref, attn_ref, mlp_ref,
    *, quarter, qr, pr, fr, wide
):
    rep, dr = place_ref[1], wq_ref.shape[0]

    def store(at, w):
        parts = row_quarters(w, quarter, qr)
        for s in range(2):
            attn_ref[s, :, at : at + w.shape[1]] = jnp.where(rep == 0, parts[s], parts[2 + s]).astype(BF16)

    wide_of = lambda ref: ref[...].astype(F32)
    eye = (
        lax.broadcasted_iota(jnp.int32, (dr, dr), 0) == lax.broadcasted_iota(jnp.int32, (dr, dr), 1)
    ).astype(F32)
    columns = [jnp.sum(eye * wide_of(ref), axis=1, keepdims=True) for ref in (g1_ref, g2_ref)]
    blank = jnp.zeros((dr, wide - wq_ref.shape[1] - 2 * wk_ref.shape[1] - 2), F32)
    store(0, jnp.concatenate([wide_of(wq_ref), wide_of(wk_ref), wide_of(wv_ref)] + columns + [blank], axis=1))
    w = wide_of(wo_ref)
    store(wide, jnp.concatenate([w, jnp.zeros((dr, attn_ref.shape[2] - wide - w.shape[1]), F32)], axis=1))
    halves = []
    for ref in (wg_ref, wu_ref):
        w = wide_of(ref)
        chunks = [w[:, i * fr : (i + 1) * fr] for i in range(w.shape[1] // fr)]
        halves.append([jnp.concatenate(chunks[c::2], axis=1) for c in range(2)])
    row = jnp.concatenate([halves[0][0], halves[1][0], halves[0][1], halves[1][1]], axis=1)
    rows, lanes = pr, mlp_ref.shape[1]
    row = jnp.concatenate([row, jnp.zeros((rows - dr, row.shape[1]), F32)], axis=0).astype(BF16)
    for g in range(4):
        mlp_ref[g * rows : (g + 1) * rows, :] = row[:, g * lanes : (g + 1) * lanes]
    at, n = 4 * rows, wd_ref.shape[1]
    mlp_ref[at : at + fr, :n] = wd_ref[...]
    mlp_ref[at : at + fr, n:] = jnp.zeros((fr, lanes - n), BF16)
    if at + fr < mlp_ref.shape[0]:
        mlp_ref[at + fr :, :] = jnp.zeros((mlp_ref.shape[0] - at - fr, lanes), BF16)


def tie_kernel(*refs):
    del refs


def add_kernel(*refs, n_alpha, count, form):
    totals = [ref[...].astype(F32) for ref in refs[:count]]
    alpha, beta = functools.reduce(jnp.add, totals[:n_alpha]), functools.reduce(jnp.add, totals[n_alpha:])
    if form == "apart":
        refs[-2][:, :, 0] = alpha.astype(BF16)
        refs[-1][:, :, 0] = beta.astype(BF16)
    elif form == "stack":
        refs[-1][0, :, :, 0] = alpha.astype(BF16)
        refs[-1][1, :, :, 0] = beta.astype(BF16)
    else:
        for c in range(alpha.shape[1]):
            refs[-1][c, :, 0] = alpha[:, c].astype(BF16)
            refs[-1][c, :, 1] = beta[:, c].astype(BF16)


def shards_kernel(place_ref, mine_ref, other_ref, got_ref, got_other_ref, gate_ref, up_ref, *, quarter, fr):
    core, rep = place_ref[0], place_ref[1]
    dr = gate_ref.shape[0]
    for at, out_ref in ((0, gate_ref), (1, up_ref)):
        sides = []
        for c, mine, other in ((0, mine_ref, other_ref), (1, got_ref, got_other_ref)):
            a, b = mine[c, at].astype(F32), other[c, at].astype(F32)
            low, high = jnp.where(rep == 0, a, b), jnp.where(rep == 0, b, a)
            rows = [half[s][:quarter] for half in (low, high) for s in range(2)]
            sides.append(jnp.concatenate(rows, axis=0)[:dr])
        even, odd = jnp.where(core == 0, sides[0], sides[1]), jnp.where(core == 0, sides[1], sides[0])
        chunks = []
        for k in range(even.shape[1] // fr):
            chunks += [even[:, k * fr : (k + 1) * fr], odd[:, k * fr : (k + 1) * fr]]
        out_ref[...] = jnp.concatenate(chunks, axis=1)


def attn_shards_kernel(place_ref, mine_ref, other_ref, *refs, quarter, wide):
    query_ref, key_ref, value_ref, *gain_refs, out_ref = refs[-6:]
    rep, dr = place_ref[1], out_ref.shape[0]
    a, b = mine_ref[0, 0].astype(F32), other_ref[0, 0].astype(F32)
    low, high = jnp.where(rep == 0, a, b), jnp.where(rep == 0, b, a)
    rows = jnp.concatenate([half[s][:quarter] for half in (low, high) for s in range(2)], axis=0)[:dr]
    at = 0
    for ref in (query_ref, key_ref, value_ref):
        ref[...] = rows[:, at : at + ref.shape[1]]
        at += ref.shape[1]
    out_ref[...] = rows[:, wide : wide + out_ref.shape[1]]
    eye = lax.broadcasted_iota(jnp.int32, (dr, dr), 0) == lax.broadcasted_iota(jnp.int32, (dr, dr), 1)
    for i, ref in enumerate(gain_refs):
        ref[...] = jnp.sum(jnp.where(eye, rows[:, at + i : at + i + 1], 0.0), axis=0, keepdims=True)


def order_kernel(*refs):
    for feat_ref, out_ref in zip(refs[:3], refs[3:]):
        column = lax.broadcasted_iota(jnp.int32, out_ref.shape, 1)
        out_ref[...] = (feat_ref[...] == column).astype(F32).astype(BF16)


def copy_kernel(in_ref, *refs):
    out_ref, n = refs[-1], in_ref.shape[1]
    out_ref[:, :n] = in_ref[...]
    out_ref[:, n:] = jnp.zeros((out_ref.shape[0], out_ref.shape[1] - n), BF16)


def sum_kernel(*refs):
    n = refs[-1].shape[1]
    refs[-1][...] = functools.reduce(jnp.add, [r[:, :n].astype(F32) for r in (refs[:3] if len(refs) > 3 else refs[:-1])]).astype(refs[-1].dtype)


def split_attn_kernel(*refs, count):
    rows = refs[0].shape[1]
    for i, ref in enumerate(refs[:count]):
        for s in range(2):
            refs[-1][s, i * rows : (i + 1) * rows, :] = ref[s]


def join_kernel(near_ref, y_ref, x_ref, xy_ref, out_ref):
    rows = near_ref.shape[1]
    blocks = ((near_ref, y_ref), (near_ref, x_ref), (x_ref, xy_ref), (y_ref, xy_ref))
    for i, pair in enumerate(blocks):
        for k, ref in enumerate(pair):
            at = (2 * i + k) * rows
            out_ref[at : at + rows, :] = ref[i % 2]


def attn_grad_kernel(keep_ref, got_ref, *refs, wide, gain_at):
    mine, other = refs[:3], refs[3:6]
    gains_ref, gains_oth_ref, order_ref = refs[6:9]
    out_refs = refs[-4:]
    half, features = keep_ref.shape[0] // 2, gains_ref.shape[1]
    n = out_refs[0].shape[0]
    gains = (gains_ref[...] + gains_oth_ref[...]).astype(BF16)
    gains = dot(order_ref[:half, :features], gains, NT)
    lane = lax.broadcasted_iota(jnp.int32, (half, LANES), 1) + (wide - LANES)
    tile = jnp.where(lane == gain_at, gains[:, 0:1], 0.0) + jnp.where(lane == gain_at + 1, gains[:, 1:2], 0.0)
    column = 0
    for k in range(3):
        at = slice(half, 2 * half) if k == 2 else slice(0, half)
        grad = dot(keep_ref[at, :], mine[k][...]) + dot(got_ref[at, :], other[k][...])
        if k == 1:
            grad = jnp.concatenate([grad[:, :-LANES], grad[:, -LANES:] + tile], axis=1)
        for i, ref in enumerate(out_refs):
            ref[:, column : column + grad.shape[1]] = grad[i * n : (i + 1) * n].astype(BF16)
        column += grad.shape[1]


def chip_flips(chips):
    bits = (chips // 2).bit_length() - 1
    z = [sum(((i >> b) & 1) << (bits - 1 - b) for b in range(bits)) for i in range(chips // 2)]
    return [2 * flip + y for flip in z for y in range(2)]


def fold_kernel(*refs, count):
    refs[-1][...] = functools.reduce(jnp.add, [r[...].astype(F32) for r in refs[:count]]).astype(refs[-1].dtype)


def mlp_kernel(place_ref, two_ref, two_oth_ref, t_ref, t_oth_ref, cot_ref, cot_oth_ref, w_ref, *refs):
    sends, keeps = refs[:2], refs[2:4]
    downs, (out_ref, out_oth_ref, d_two_ref, d_two_oth_ref) = refs[4:6], refs[6:10]
    acts, acts_t, cots, wg, wu, wd, hidden, d_gate, d_up = refs[10:19]
    chunks, down, out, out_oth, d_two, d_two_oth, in_sems, out_sems = refs[19:]
    rows = cot_ref.shape[0]
    width, half_ff, features = acts_t.shape[0], hidden.shape[1], down.shape[1]
    shards, pr = wg.shape[0], wg.shape[1]
    fr, plain, n, block = 2 * half_ff // shards, shards * pr, width // 4, width // 8
    core = place_ref[0]
    started = []

    def fetch(source, target):
        copy = pltpu.make_async_copy(source, target, in_sems.at[len(started)])
        copy.start()
        started.append(copy)
        return copy

    first = [fetch(two_ref, acts.at[pl.ds(0, rows), :])]
    gate_in = fetch(w_ref.at[:, pl.ds(2 * pr * core, pr), :], wg)
    up_in = fetch(w_ref.at[:, pl.ds(2 * pr * core + pr, pr), :], wu)
    cots_in = [fetch(cot_ref, cots.at[pl.ds(0, rows), :])]
    down_in = [
        fetch(
            w_ref.at[2 * k + core, pl.ds(4 * pr, fr), pl.ds(0, wd.shape[1])], wd.at[pl.ds(k * fr, fr), :]
        )
        for k in range(shards // 2)
    ]
    second = [fetch(two_oth_ref, acts.at[pl.ds(rows, rows), :]), fetch(cot_oth_ref, cots.at[pl.ds(rows, rows), :])]
    turned = [fetch(t_ref, acts_t.at[:, pl.ds(0, rows)])]
    for k in range(8):
        source = t_oth_ref.at[pl.ds((k ^ 1) * block, block), :]
        turned.append(fetch(source, acts_t.at[pl.ds(k * block, block), pl.ds(rows, rows)]))

    def wait(copies):
        for copy in copies:
            copy.wait()

    for half in range(2):
        at = slice(half * rows, (half + 1) * rows)
        wait(second if half else first + [gate_in])
        gate = dot(acts[at, :], wg[...].reshape(plain, half_ff))
        if not half:
            wait([up_in])
        up = dot(acts[at, :], wu[...].reshape(plain, half_ff))
        sg = 1.0 / (1.0 + jnp.exp(-gate))
        silu = gate * sg
        hidden[at, :] = (silu * up).astype(BF16)
        if not half:
            wait(cots_in + down_in)
        d_hidden = dot(cots[at, :], wd[...], NT)
        d_gate[at, :] = (d_hidden * up * sg * (1.0 + gate * (1.0 - sg))).astype(BF16)
        d_up[at, :] = (d_hidden * silu).astype(BF16)
    wait(turned)

    going = []

    def put(source, target):
        copy = pltpu.make_async_copy(source, target, out_sems.at[len(going)])
        copy.start()
        going.append(copy)

    for targets, first_row in ((sends, 2 * n), (keeps, 0)):
        for i, d in ((0, d_gate), (1, d_up)):
            grad = dot(acts_t[first_row : first_row + 2 * n, :], d[...])
            for k in range(2):
                slot = len(going) % chunks.shape[0]
                if len(going) >= chunks.shape[0]:
                    going[len(going) - chunks.shape[0]].wait()
                chunks[slot] = grad[k * n : (k + 1) * n].astype(BF16)
                put(chunks.at[slot], targets[k].at[i])
    count = len(going)
    down[...] = dot(hidden[...], cots[:, :features], TN).astype(BF16)
    chips = shards // 2
    for k, flip in enumerate(chip_flips(chips)):
        source = pl.multiple_of((place_ref[2] ^ flip) * fr, fr)
        put(down.at[pl.ds(source, fr), :], downs[1 - 2 * k // chips].at[k % (chips // 2)])

    def back(at):
        return dot(d_gate[at, :], wg[...].reshape(plain, half_ff), NT) + dot(
            d_up[at, :], wu[...].reshape(plain, half_ff), NT
        )

    d_two[...] = back(slice(0, rows))
    put(d_two, d_two_ref)
    out[...] = dot(hidden[:rows, :], wd[:, :features])
    put(out, out_ref)
    d_two_oth[...] = back(slice(rows, 2 * rows)).astype(BF16)
    put(d_two_oth, d_two_oth_ref)
    out_oth[...] = dot(hidden[rows:, :], wd[...]).astype(BF16)
    put(out_oth, out_oth_ref)
    wait(going[count - chunks.shape[0] :])


def on_device(
    tokens, cotangent, attn_gain, w_query, w_key, w_value, w_out, mlp_gain, w_gate, w_up, w_down
):
    shards = lax.axis_size("shard")
    chips = shards // 2
    zs = chips // 2
    me, rep = lax.axis_index("shard"), lax.axis_index("rep")
    core = me % 2
    micro, batch, length, features = tokens.shape
    seqs = micro * batch
    rows = seqs * length
    dr = features // shards
    quarter = -(-dr // 4)
    qr = -(-quarter // 8) * 8
    pr = -(-dr // 16) * 16
    plain = shards * pr
    width = shards * 4 * qr
    half = width // 2
    block = zs * qr
    fr = w_down.shape[0]
    half_ff = chips * fr
    nq, nk = HQ * HD, KV * HD
    nqkv = nq + 2 * nk
    wide = -(-(nqkv + 2) // LANES) * LANES
    padded = -(-features // LANES) * LANES
    full = wide + padded
    cosine, sine = (jnp.asarray(t) for t in tables(length))
    place = jnp.stack([core, rep, me // 2]).astype(jnp.int32)
    in_smem = pl.BlockSpec(memory_space=pltpu.SMEM)
    in_vmem = pl.BlockSpec(memory_space=pltpu.VMEM)
    anywhere = pl.BlockSpec(memory_space=pl.ANY)
    z_bits = zs.bit_length() - 1
    z_flip = np.array([sum(((i >> b) & 1) << (z_bits - 1 - b) for b in range(z_bits)) for i in range(zs)])

    def over(array, flip):
        return lax.ppermute(array, "shard", [(s, s ^ flip) for s in range(shards)])

    def over_core(array):
        return over(array, 1)

    def over_y(array):
        return over(array, 2)

    def over_rep(array):
        return lax.ppermute(array, "rep", [(0, 1), (1, 0)])

    def tie(arrays, *deps):
        return call(
            tie_kernel, [shape(a.shape, a.dtype) for a in arrays],
            in_specs=[anywhere] * (len(arrays) + len(deps)), out_specs=[anywhere] * len(arrays),
            input_output_aliases={i: i for i in range(len(arrays))},
        )(*arrays, *deps)

    def small(kernel, outs, arrays, deps=()):
        return call(
            kernel, outs, in_specs=[in_vmem] * len(arrays) + [anywhere] * len(deps), vmem=16 << 20
        )(*arrays, *deps)


    def feature_of(dims):
        sizes = {"core": 2, "split": 2, "f1": 2, "f2": 2, "z": zs, "row": qr}
        grid = np.meshgrid(*[np.arange(sizes[d]) for d in dims], indexing="ij")
        at = {d: g.reshape(-1) for d, g in zip(dims, grid)}
        x_flip = np.where(at["split"] == 0, at["f1"], at["f2"])
        y_flip = np.where(at["split"] == 0, at["f2"], at["f1"])
        shard = me ^ jnp.asarray(at["core"] + 2 * (y_flip + 2 * z_flip[at["z"]]), jnp.int32)
        part = 2 * (rep ^ jnp.asarray(x_flip, jnp.int32)) + jnp.asarray(at["split"], jnp.int32)
        inside = part * quarter + jnp.asarray(at["row"], jnp.int32)
        real = jnp.asarray(at["row"] < quarter) & (inside < dr)
        return jnp.where(real, shard * dr + inside, -1)[:, None]

    feats = [feature_of(("core", "f1", "split", "f2", "z", "row")), feature_of(("f1", "split", "core", "f2", "z", "row"))]
    shard, row = np.repeat(np.arange(shards), pr), np.tile(np.arange(pr), shards)
    feats.append(jnp.asarray(np.where(row < dr, shard * dr + row, -1)[:, None], jnp.int32))
    attn_order, mlp_order, plain_order = call(
        order_kernel, [shape((f.shape[0], padded)) for f in feats], grid=(1,), in_specs=[in_vmem] * 3,
        out_specs=[whole(f.shape[0], padded) for f in feats],
    )(*feats)

    floor = (16 << 20) // (2 * half_ff * shards) + 1
    depth = -(-max(4 * pr + fr, floor) // 16) * 16
    attn_piece, mlp_piece = call(
        functools.partial(pieces_kernel, quarter=quarter, qr=qr, pr=pr, fr=fr, wide=wide),
        [shape((2, qr, full)), shape((depth, half_ff))],
        grid=(1,),
        in_specs=[in_smem] + [
            whole(*w.shape)
            for w in (w_query, w_key, w_value, w_out, attn_gain[None], mlp_gain[None], w_gate, w_up, w_down)
        ],
        out_specs=[in_vmem, whole(depth, half_ff)],
    )(place, w_query, w_key, w_value, w_out, attn_gain[None], mlp_gain[None], w_gate, w_up, w_down)
    mlp = lax.all_gather(mlp_piece, "shard", axis=0, tiled=True).reshape(shards, depth, half_ff)
    parts = [attn_piece if z == 0 else over(attn_piece, 4 * z) for z in z_flip]
    x = tokens.reshape(rows, features)
    cot = cotangent.reshape(rows, features)
    cot_wide = small(copy_kernel, shape((rows, padded)), [cot], [attn_piece])
    cot_oth = over_core(cot_wide)
    attn_near = small(
        functools.partial(split_attn_kernel, count=zs), shape((2, block, full)), parts, [cot_oth, x, attn_order]
    )
    attn_y, attn_x = over_y(attn_near), over_rep(attn_near)
    attn_blocks = [attn_near, attn_y, attn_x, over_rep(attn_y)]
    attn_blocks += [over_core(b) for b in attn_blocks]

    by_rows = lambda cols: pl.BlockSpec((length, cols), lambda i: (i, 0))
    by_cols = lambda n: pl.BlockSpec((n, length), lambda i: (0, i))
    by_once = lambda *arrays: [once(*a.shape) for a in arrays]
    by_probs = pl.BlockSpec((1, HQ, length, length), lambda i: (i, 0, 0, 0))
    rows_at = lambda i, cols: pl.BlockSpec((length, cols), lambda _: (i, 0))
    shared = (*attn_blocks, attn_order, mlp_order, plain_order, cosine, sine)
    two, two_t, keep_t, send_t, qkv, probs, mixed, gain_rows, attn_all = call(
        functools.partial(attention_forward, wide=wide),
        [
            shape((rows, plain)), shape((width, rows)), shape((width, rows)), shape((width, rows)),
            shape((rows, wide)), shape((seqs, HQ, length, length)), shape((rows, features), F32),
            shape((8, features), F32), shape((width, full)),
        ],
        grid=(seqs,),
        in_specs=[by_rows(features)] + by_once(*shared),
        out_specs=[by_rows(plain)] + [by_cols(width)] * 3
        + [by_rows(wide), by_probs, by_rows(features), once(8, features), once(width, full)],
    )(x, *shared)

    n = width // 4
    (
        alpha_send, beta_send, alpha_keep, beta_keep, down_send, down_keep, out_part, out_other, d_two_mine,
        d_two_other,
    ) = call(
        mlp_kernel,
        [shape((2, n, half_ff))] * 4 + [shape((chips // 2, fr, features))] * 2
        + [shape((rows, features), F32), shape((rows, padded)), shape((rows, plain), F32), shape((rows, plain))],
        in_specs=[in_smem] + [anywhere] * 7,
        out_specs=[anywhere] * 10,
        scratch_shapes=[
            pltpu.VMEM((2 * rows, plain), BF16), pltpu.VMEM((width, 2 * rows), BF16), pltpu.VMEM((2 * rows, padded), BF16),
            pltpu.VMEM((shards, pr, half_ff), BF16), pltpu.VMEM((shards, pr, half_ff), BF16),
            pltpu.VMEM((half_ff, padded), BF16),
            pltpu.VMEM((2 * rows, half_ff), BF16), pltpu.VMEM((2 * rows, half_ff), BF16), pltpu.VMEM((2 * rows, half_ff), BF16),
            pltpu.VMEM((4, n, half_ff), BF16), pltpu.VMEM((half_ff, features), BF16), pltpu.VMEM((rows, features), F32),
            pltpu.VMEM((rows, padded), BF16), pltpu.VMEM((rows, plain), F32), pltpu.VMEM((rows, plain), BF16),
            pltpu.SemaphoreType.DMA((15 + chips,)), pltpu.SemaphoreType.DMA((12 + chips,)),
        ],
    )(place, two, over_core(two), two_t, over_core(two_t), cot_wide, cot_oth, mlp)
    def fold(parts, n, at, deps=()):
        spec = pl.BlockSpec((n, fr, features), lambda _: (at, 0, 0))
        return call(
            functools.partial(fold_kernel, count=len(parts)), shape((n, fr, features)), grid=(1,),
            in_specs=[spec] * len(parts) + [anywhere] * len(deps), out_specs=whole(n, fr, features), vmem=ADD_VMEM,
        )(*parts, *deps)

    down_parts = [down_keep, over(down_send, 4)]

    def down_stages():
        n = chips // 2
        for flip in [4 << b for b in range(1, z_bits)] + [2]:
            n //= 2
            yield n, flip

    def down_stage(n, flip, *deps):
        sent = fold(down_parts, n, 1, deps)
        down_parts.append(over(sent, flip))
        return [sent]

    def add(alpha, beta, at, size, form, deps):
        arrays = [p[0] for p in alpha + beta]
        j, cores, _, _, n = arrays[0].shape
        one = shape((j, cores, 1, size, n))
        outs = {"apart": [one, one], "stack": shape((2,) + one.shape), "last": shape((cores, j, 2, size, n))}[form]
        specs = []
        for _, lead, f in alpha + beta:
            spot = ((0, 0, f, at // size, 0), (j, cores, None, size, n))
            if lead is not None:
                spot = ((lead,) + spot[0], (None,) + spot[1])
            specs.append(pl.BlockSpec(spot[1], functools.partial(lambda where, _: where, spot[0])))
        return call(
            functools.partial(add_kernel, n_alpha=len(alpha), count=len(arrays), form=form), outs, grid=(1,),
            in_specs=specs + [anywhere] * len(deps),
            out_specs=[whole(*o.shape) for o in outs] if form == "apart" else whole(*outs.shape),
            vmem=ADD_VMEM,
        )(*arrays, *deps)

    class Reduction:
        def __init__(self, alpha_keep, beta_keep, alpha_send, beta_send):
            self.early = [[alpha_keep, over_rep(alpha_send)], [beta_keep, over_y(beta_send)]]
            self.late = []
            self.both = []
            self.size = block

        def parts(self, f):
            return [
                [(a, None, f) for a in self.early[s]]
                + [(pair[s], None, 0) for pair in self.late] + [(a, s, 0) for a in self.both]
                for s in range(2)
            ]

        def second(self, *deps):
            alpha_sent, beta_sent = add(*self.parts(1), 0, block, "apart", deps)
            self.late.append((over_y(alpha_sent), over_rep(beta_sent)))
            return [alpha_sent, beta_sent]

        def z(self, *deps):
            self.size //= 2
            sent = add(*self.parts(0), self.size, self.size, "stack", deps)
            self.both.append(over(sent, 4 << (len(self.both))))
            return [sent]

        def last(self, *deps):
            mine = add(*self.parts(0), 0, qr, "last", deps)
            return mine, over_rep(mine)

    mlp_sum = Reduction(
        *[a.reshape(2, 2, 2, block, half_ff) for a in (alpha_keep, beta_keep, alpha_send, beta_send)]
    )

    low = wide // LANES // 8 * 8 * LANES
    arrays = (gain_rows, attn_all, attn_order)
    d_low, d_high, d_attn, grad_tokens, grad_gains = call(
        functools.partial(attention_backward, wide=wide),
        [
            shape((rows, low)), shape((rows, wide - low)), shape((rows, padded)), shape((rows, features)),
            shape((8, features), F32),
        ],
        grid=(seqs,),
        in_specs=[by_rows(plain), by_rows(plain)] + by_once(plain_order) + [by_rows(features)] * 2
        + by_once(*arrays) + [by_rows(wide), by_probs] + by_once(cosine, sine) + [by_rows(features)],
        out_specs=[by_rows(low), by_rows(wide - low), by_rows(padded), by_rows(features), whole(8, features)],
        vmem=40 << 20,
    )(d_two_mine, over_core(d_two_other), plain_order, mixed, cot, *arrays, qkv, probs, cosine, sine, x)
    down_left = list(down_stages())
    out_oth, got_t = over_core(out_other), over_core(send_t)
    sent = down_stage(*down_left.pop(0), d_low, out_oth, got_t)
    sent += mlp_sum.second(*sent)
    n = half // 4
    arrays = [d_low, d_high, d_attn]
    arrays = [
        keep_t, got_t, *arrays, *[over_core(a) for a in arrays], grad_gains, over_core(grad_gains), attn_order
    ]
    attn_grads = call(
        functools.partial(attn_grad_kernel, wide=wide, gain_at=nqkv),
        [shape((n, full))] * 4,
        grid=(1,),
        in_specs=by_once(*arrays) + [anywhere] * len(sent),
        out_specs=[whole(n, full)] * 4,
        vmem=32 << 20,
    )(*arrays, *sent)
    attn_sum = Reduction(*[a.reshape(1, 1, 2, block, full) for a in attn_grads])
    for i in range(seqs):
        output = call(
            sum_kernel, shape((rows, features)), grid=(1,),
            in_specs=[rows_at(i, features), rows_at(i, features), rows_at(i, padded)]
            + [anywhere] * (2 if i else 1),
            out_specs=rows_at(i, features), input_output_aliases={4: 0} if i else {},
        )(out_part, mixed, out_oth, attn_grads[0], *([output] if i else []))
    sent = mlp_sum.z(attn_grads[0], output)
    sent = attn_sum.second(*sent)
    for step in range(z_bits):
        if step:
            sent = mlp_sum.z(*sent)
        if down_left:
            sent = down_stage(*down_left.pop(0), *sent)
        sent = attn_sum.z(*sent)
    while down_left:
        sent = down_stage(*down_left.pop(0), *sent)
    down_mine = fold(down_parts, 1, 0, sent)
    down_from = over_rep(down_mine)
    mlp_mine, mlp_from = mlp_sum.last(down_mine)
    attn_mine, attn_from = attn_sum.last(mlp_mine)

    grad_gate, grad_up = call(
        functools.partial(shards_kernel, quarter=quarter, fr=fr),
        [shape((dr, 2 * half_ff), F32)] * 2,
        grid=(1,),
        in_specs=[in_smem] + by_once(*[mlp_mine] * 4), out_specs=[whole(dr, 2 * half_ff)] * 2,
    )(place, mlp_mine, mlp_from, over_core(mlp_mine), over_core(mlp_from))
    grad_down = call(
        functools.partial(fold_kernel, count=2), shape((1, fr, features), F32), grid=(1,),
        in_specs=by_once(down_mine, down_mine) + [anywhere], out_specs=whole(1, fr, features), vmem=ADD_VMEM,
    )(down_mine, down_from, grad_gate)
    attn_dims = ((dr, nq), (dr, nk), (dr, nk), (1, dr), (1, dr), (dr, features))
    grad_query, grad_key, grad_value, grad_gain_one, grad_gain_two, grad_out = call(
        functools.partial(attn_shards_kernel, quarter=quarter, wide=wide),
        [shape(dims, F32) for dims in attn_dims],
        grid=(1,),
        in_specs=[in_smem] + by_once(attn_mine, attn_mine) + [anywhere] * 2,
        out_specs=[whole(*dims) for dims in attn_dims],
    )(place, attn_mine, attn_from, grad_down, grad_gate)
    dims = tokens.shape
    return (
        output.reshape(dims), grad_tokens.reshape(dims), grad_gain_one.reshape(dr), grad_query, grad_key, grad_value,
        grad_out, grad_gain_two.reshape(dr), grad_gate, grad_up, grad_down[0],
    )


def solution(mesh):
    data = P(None, ("rep", "shard"), None, None)
    vector, matrix = P("shard"), P("shard", None)
    weights = (vector, matrix, matrix, matrix, matrix, vector, matrix, matrix, matrix)
    return jax.shard_map(
        on_device,
        mesh=mesh,
        in_specs=(data, data) + weights,
        out_specs=(data, data) + weights,
        check_vma=False,
    )
```

```python
import functools
import math

import jax
import jax.numpy as jnp
import numpy as np
from jax import lax
from jax.experimental import pallas as pl
from jax.experimental.pallas import tpu as pltpu
from jax.sharding import PartitionSpec as P

HQ = 15
KV = 5
HD = 64
EPSILON = 1e-05
THETA = 100000.0
F32 = jnp.float32
BF16 = jnp.bfloat16
LANES = 128
COLS = 256
NN = ((1,), (0,))
NT = ((1,), (1,))
TN = ((0,), (0,))
VMEM = 60 << 20
ADD_VMEM = 16 << 20


def dot(a, b, contract=NN):
    return lax.dot_general(a, b, (contract, ((), ())), preferred_element_type=F32)


def call(kernel, out_shape, *, vmem=VMEM, **how):
    return pl.pallas_call(
        kernel,
        out_shape=out_shape,
        compiler_params=pltpu.CompilerParams(vmem_limit_bytes=vmem),
        cost_estimate=pl.CostEstimate(flops=1 << 20, bytes_accessed=1 << 12, transcendentals=0),
        **how,
    )


def shape(dims, dtype=BF16):
    return jax.ShapeDtypeStruct(dims, dtype)


def whole(*dims):
    return pl.BlockSpec(dims, lambda *_: (0,) * len(dims))


def once(*dims):
    return pl.BlockSpec(dims, lambda *_: (0,) * len(dims), pipeline_mode=pl.Buffered(1))


def tables(length):
    frequency = THETA ** (-2.0 * np.arange(HD // 2, dtype=np.float32) / HD)
    angles = np.arange(length, dtype=np.float32)[:, None] * frequency.astype(np.float32)[None, :]
    cosine, sine = np.cos(angles), np.sin(angles)
    return np.tile(cosine, (1, 4)), np.concatenate([-sine, sine, -sine, sine], axis=1)


def turn(tile, cosine, sine, low):
    other = jnp.where(low, pltpu.roll(tile, LANES - 32, 1), pltpu.roll(tile, 32, 1))
    return tile * cosine + other * sine


def placed(tile, half):
    lane = lax.broadcasted_iota(jnp.int32, tile.shape, 1)
    alone = jnp.where((lane >= HD) == (half == 1), tile, 0.0)
    moved = pltpu.roll(alone, HD, 1)
    pair = (moved, alone) if half else (alone, moved)
    return [one.astype(BF16) for one in pair]


def placed_turned(tile, half):
    tile = tile.T
    row = lax.broadcasted_iota(jnp.int32, tile.shape, 0)
    alone = jnp.where((row >= HD) == (half == 1), tile, 0.0)
    moved = jnp.concatenate([alone[HD:], alone[:HD]], axis=0)
    pair = (moved, alone) if half else (alone, moved)
    return [one.astype(BF16) for one in pair]


def attention_forward(x_ref, *refs, wide):
    blocks, (attn_order_ref, mlp_order_ref, plain_order_ref, cos_ref, sin_ref) = refs[:8], refs[8:13]
    two_ref, two_t_ref, keep_ref, send_ref, qkv_ref, probs_ref, mixed_ref, gain_ref, all_ref = refs[13:]

    @pl.when(pl.program_id(0) == 0)
    def _():
        n = all_ref.shape[0] // 16
        for c in range(2):
            near, over_y, over_x, over_both = blocks[4 * c : 4 * c + 4]
            pairs = ((near, over_y), (near, over_x), (over_x, over_both), (over_y, over_both))
            for i, pair in enumerate(pairs):
                for k, ref in enumerate(pair):
                    at = (8 * c + 2 * i + k) * n
                    all_ref[at : at + n, :] = ref[i % 2]

    length, features = x_ref.shape
    half = all_ref.shape[0] // 2
    to_order = attn_order_ref[:, :features]
    last = slice(wide - LANES, wide)
    gains = dot(all_ref[:, last], to_order, TN)
    gain_one, gain_two = gains[HD : HD + 1], gains[HD + 1 : HD + 2]
    gain_ref[...] = gains[HD : HD + 8]
    x = x_ref[...].astype(F32)
    r1 = lax.rsqrt(jnp.mean(x * x, axis=-1, keepdims=True) + EPSILON)
    normed = (x * r1 * gain_one).astype(BF16)
    spread = dot(normed, to_order, NT).astype(BF16)
    turned = dot(to_order, normed, NT).astype(BF16)
    keep_ref[:half, :] = turned[:half]
    send_ref[:half, :] = turned[half:]
    lane = lax.broadcasted_iota(jnp.int32, (length, LANES), 1)
    low = lane % HD < HD // 2
    cosine, sine = cos_ref[...], sin_ref[...]
    tiles, heads = [], {}
    for t in range(wide // LANES):
        cols = slice(t * LANES, (t + 1) * LANES)
        tile = dot(spread, all_ref[:, cols])
        if t * 2 < HQ + KV:
            tile = turn(tile, cosine, sine, low)
        if t == wide // LANES - 1:
            tile = jnp.where(lane < HD, tile, 0.0)
        short = tile.astype(BF16)
        qkv_ref[:, cols] = short
        tiles.append(short)
        for n in (2 * t, 2 * t + 1):
            if HQ <= n < HQ + KV:
                heads[n] = placed(tile, n % 2)
            elif HQ + KV <= n < HQ + 2 * KV:
                heads[n] = placed_turned(tile, n % 2)
    causal = lax.broadcasted_iota(jnp.int32, (length, length), 0) <= lax.broadcasted_iota(
        jnp.int32, (length, length), 1
    )
    context = [None] * ((HQ + 1) // 2)
    for h in range(HQ):
        j, t, s = h // (HQ // KV), h // 2, h % 2
        scores = dot(heads[HQ + j][s], tiles[t], NT) * (1.0 / math.sqrt(HD))
        scores = jnp.where(causal, scores, -1e30)
        exponent = jnp.exp(scores - jnp.max(scores, axis=0, keepdims=True))
        probs = exponent * (1.0 / jnp.sum(exponent, axis=0, keepdims=True))
        probs = probs.astype(BF16)
        probs_ref[0, h] = probs
        part = dot(heads[HQ + KV + j][s], probs)
        context[t] = part if context[t] is None else context[t] + part
    context = jnp.concatenate([c.astype(BF16) for c in context], axis=0)
    turned = dot(attn_order_ref[...], context).astype(BF16)
    mixed = x + dot(turned, all_ref[:, wide : wide + features], TN)
    keep_ref[half:, :] = turned[:half]
    send_ref[half:, :] = turned[half:]
    mixed_ref[...] = mixed
    r2 = lax.rsqrt(jnp.mean(mixed * mixed, axis=-1, keepdims=True) + EPSILON)
    two = (mixed * r2 * gain_two).astype(BF16)
    two_ref[...] = dot(two, plain_order_ref[:, :features], NT).astype(BF16)
    two_t_ref[...] = dot(mlp_order_ref[:, :features], two, NT).astype(BF16)


def attention_backward(
    mine_ref, other_ref, plain_order_ref, mixed_ref, cot_ref, gain_ref, all_ref, order_ref, qkv_ref,
    probs_ref, cos_ref, sin_ref, x_ref, d_low_ref, d_high_ref, d_attn_ref, out_ref, grad_ref, *, wide
):
    length, features = mixed_ref.shape
    total = (mine_ref[...] + other_ref[...].astype(F32)).astype(BF16)
    d_two = dot(total, plain_order_ref[:, :features])
    mixed = mixed_ref[...]
    r2 = lax.rsqrt(jnp.mean(mixed * mixed, axis=-1, keepdims=True) + EPSILON)
    unit = mixed * r2
    e2 = d_two * gain_ref[1:2, :]
    d_mixed = cot_ref[...].astype(F32) + r2 * (e2 - unit * jnp.mean(e2 * unit, axis=-1, keepdims=True))
    d_attn = d_mixed.astype(BF16)
    d_attn_ref[:, :features] = d_attn
    d_attn_ref[:, features:] = jnp.zeros((length, d_attn_ref.shape[1] - features), BF16)
    grad_gain_two = jnp.sum(d_two * unit, axis=0, keepdims=True)
    d_context = dot(d_attn, all_ref[:, wide : wide + features], NT).astype(BF16)
    d_context = dot(d_context, order_ref[...]).astype(BF16)
    lane = lax.broadcasted_iota(jnp.int32, (length, LANES), 1)
    low = lane % HD < HD // 2
    cosine, sine = cos_ref[...], -sin_ref[...]

    def tile_of(n):
        t = n // 2
        return qkv_ref[:, t * LANES : (t + 1) * LANES]

    d_tiles = [None] * ((HQ + 2 * KV + 1) // 2)

    def add(t, part):
        d_tiles[t] = part if d_tiles[t] is None else d_tiles[t] + part

    groups = HQ // KV
    d_query = [None] * ((HQ + 1) // 2)
    for j in range(KV):
        keys = placed_turned(tile_of(HQ + j).astype(F32), (HQ + j) % 2)
        values = placed(tile_of(HQ + KV + j).astype(F32), (HQ + KV + j) % 2)
        d_key, d_value = [None, None], [None, None]
        for h in range(j * groups, (j + 1) * groups):
            t, s = h // 2, h % 2
            d_con = d_context[:, t * LANES : (t + 1) * LANES]
            probs = probs_ref[0, h]
            wide_probs = probs.astype(F32)
            d_probs = dot(values[s], d_con, NT)
            inner = jnp.sum(d_probs * wide_probs, axis=0, keepdims=True)
            d_scores = (wide_probs * (d_probs - inner) * (1.0 / math.sqrt(HD))).astype(BF16)
            part = dot(keys[s], d_scores)
            d_query[t] = part if d_query[t] is None else d_query[t] + part
            part = dot(d_scores, tile_of(h))
            d_key[s] = part if d_key[s] is None else d_key[s] + part
            part = dot(probs, d_con)
            d_value[s] = part if d_value[s] is None else d_value[s] + part
        for n, pair in ((HQ + j, d_key), (HQ + KV + j, d_value)):
            here = n % 2
            mask = (lane >= HD) == (here == 1)
            total = jnp.where(mask, pair[here] + pltpu.roll(pair[1 - here], HD, 1), 0.0)
            add(n // 2, total)
    for t, tile in enumerate(d_query):
        add(t, tile.T)
    for t, tile in enumerate(d_tiles):
        if t * 2 < HQ + KV:
            tile = turn(tile, cosine, sine, low)
        ref, at = (d_low_ref, t * LANES) if t * LANES < d_low_ref.shape[1] else (d_high_ref, t * LANES - d_low_ref.shape[1])
        ref[:, at : at + LANES] = tile.astype(BF16)
    split = d_low_ref.shape[1]
    d_normed = dot(d_low_ref[...], all_ref[:, :split], NT) + dot(d_high_ref[...], all_ref[:, split:wide], NT)
    d_normed = d_normed.astype(BF16)
    d_normed = dot(d_normed, order_ref[:, :features])
    x = x_ref[...].astype(F32)
    r1 = lax.rsqrt(jnp.mean(x * x, axis=-1, keepdims=True) + EPSILON)
    unit = x * r1
    e1 = d_normed * gain_ref[0:1, :]
    out = d_mixed + r1 * (e1 - unit * jnp.mean(e1 * unit, axis=-1, keepdims=True))
    out_ref[...] = out.astype(BF16)
    grad_gain_one = jnp.sum(d_normed * unit, axis=0, keepdims=True)
    grads = jnp.concatenate([grad_gain_one, grad_gain_two, jnp.zeros((6, features), F32)], axis=0)


    @pl.when(pl.program_id(0) == 0)
    def _():
        grad_ref[...] = grads

    @pl.when(pl.program_id(0) > 0)
    def _():
        grad_ref[...] += grads


def flipped(array, axis, block):
    n = array.shape[axis] // block
    parts = [lax.slice_in_dim(array, i * block, (i + 1) * block, axis=axis) for i in range(n)]
    return jnp.concatenate([parts[i ^ 1] for i in range(n)], axis=axis)


def row_quarters(w, quarter, qr):
    dr, n = w.shape
    parts = []
    for q in range(4):
        part = w[min(q * quarter, dr) : min((q + 1) * quarter, dr), :]
        parts.append(jnp.concatenate([part, jnp.zeros((qr - part.shape[0], n), F32)], axis=0))
    return parts


def pieces_kernel(
    place_ref, wq_ref, wk_ref, wv_ref, wo_ref, g1_ref, g2_ref, wg_ref, wu_ref, wd_ref, attn_ref, mlp_ref,
    *, quarter, qr, pr, fr, wide
):
    rep, dr = place_ref[1], wq_ref.shape[0]

    def store(at, w):
        parts = row_quarters(w, quarter, qr)
        for s in range(2):
            attn_ref[s, :, at : at + w.shape[1]] = jnp.where(rep == 0, parts[s], parts[2 + s]).astype(BF16)

    wide_of = lambda ref: ref[...].astype(F32)
    eye = (
        lax.broadcasted_iota(jnp.int32, (dr, dr), 0) == lax.broadcasted_iota(jnp.int32, (dr, dr), 1)
    ).astype(F32)
    columns = [jnp.sum(eye * wide_of(ref), axis=1, keepdims=True) for ref in (g1_ref, g2_ref)]
    blank = jnp.zeros((dr, wide - wq_ref.shape[1] - 2 * wk_ref.shape[1] - 2), F32)
    store(0, jnp.concatenate([wide_of(wq_ref), wide_of(wk_ref), wide_of(wv_ref)] + columns + [blank], axis=1))
    w = wide_of(wo_ref)
    store(wide, jnp.concatenate([w, jnp.zeros((dr, attn_ref.shape[2] - wide - w.shape[1]), F32)], axis=1))
    halves = []
    for ref in (wg_ref, wu_ref):
        w = wide_of(ref)
        chunks = [w[:, i * fr : (i + 1) * fr] for i in range(w.shape[1] // fr)]
        halves.append([jnp.concatenate(chunks[c::2], axis=1) for c in range(2)])
    row = jnp.concatenate([halves[0][0], halves[1][0], halves[0][1], halves[1][1]], axis=1)
    rows, lanes = pr, mlp_ref.shape[1]
    row = jnp.concatenate([row, jnp.zeros((rows - dr, row.shape[1]), F32)], axis=0).astype(BF16)
    for g in range(4):
        mlp_ref[g * rows : (g + 1) * rows, :] = row[:, g * lanes : (g + 1) * lanes]
    at, n = 4 * rows, wd_ref.shape[1]
    mlp_ref[at : at + fr, :n] = wd_ref[...]
    mlp_ref[at : at + fr, n:] = jnp.zeros((fr, lanes - n), BF16)
    if at + fr < mlp_ref.shape[0]:
        mlp_ref[at + fr :, :] = jnp.zeros((mlp_ref.shape[0] - at - fr, lanes), BF16)


def tie_kernel(*refs):
    del refs


def add_kernel(*refs, n_alpha, count, form):
    totals = [ref[...].astype(F32) for ref in refs[:count]]
    alpha, beta = functools.reduce(jnp.add, totals[:n_alpha]), functools.reduce(jnp.add, totals[n_alpha:])
    if form == "apart":
        refs[-2][:, :, 0] = alpha.astype(BF16)
        refs[-1][:, :, 0] = beta.astype(BF16)
    elif form == "stack":
        refs[-1][0, :, :, 0] = alpha.astype(BF16)
        refs[-1][1, :, :, 0] = beta.astype(BF16)
    else:
        for c in range(alpha.shape[1]):
            refs[-1][c, :, 0] = alpha[:, c].astype(BF16)
            refs[-1][c, :, 1] = beta[:, c].astype(BF16)


def shards_kernel(place_ref, mine_ref, other_ref, got_ref, got_other_ref, gate_ref, up_ref, *, quarter, fr):
    core, rep = place_ref[0], place_ref[1]
    dr = gate_ref.shape[0]
    for at, out_ref in ((0, gate_ref), (1, up_ref)):
        sides = []
        for c, mine, other in ((0, mine_ref, other_ref), (1, got_ref, got_other_ref)):
            a, b = mine[c, at].astype(F32), other[c, at].astype(F32)
            low, high = jnp.where(rep == 0, a, b), jnp.where(rep == 0, b, a)
            rows = [half[s][:quarter] for half in (low, high) for s in range(2)]
            sides.append(jnp.concatenate(rows, axis=0)[:dr])
        even, odd = jnp.where(core == 0, sides[0], sides[1]), jnp.where(core == 0, sides[1], sides[0])
        chunks = []
        for k in range(even.shape[1] // fr):
            chunks += [even[:, k * fr : (k + 1) * fr], odd[:, k * fr : (k + 1) * fr]]
        out_ref[...] = jnp.concatenate(chunks, axis=1)


def attn_shards_kernel(place_ref, mine_ref, other_ref, *refs, quarter, wide):
    query_ref, key_ref, value_ref, *gain_refs, out_ref = refs[-6:]
    rep, dr = place_ref[1], out_ref.shape[0]
    a, b = mine_ref[0, 0].astype(F32), other_ref[0, 0].astype(F32)
    low, high = jnp.where(rep == 0, a, b), jnp.where(rep == 0, b, a)
    rows = jnp.concatenate([half[s][:quarter] for half in (low, high) for s in range(2)], axis=0)[:dr]
    at = 0
    for ref in (query_ref, key_ref, value_ref):
        ref[...] = rows[:, at : at + ref.shape[1]]
        at += ref.shape[1]
    out_ref[...] = rows[:, wide : wide + out_ref.shape[1]]
    eye = lax.broadcasted_iota(jnp.int32, (dr, dr), 0) == lax.broadcasted_iota(jnp.int32, (dr, dr), 1)
    for i, ref in enumerate(gain_refs):
        ref[...] = jnp.sum(jnp.where(eye, rows[:, at + i : at + i + 1], 0.0), axis=0, keepdims=True)


def order_kernel(*refs):
    for feat_ref, out_ref in zip(refs[:3], refs[3:]):
        column = lax.broadcasted_iota(jnp.int32, out_ref.shape, 1)
        out_ref[...] = (feat_ref[...] == column).astype(F32).astype(BF16)


def copy_kernel(in_ref, *refs):
    out_ref, n = refs[-1], in_ref.shape[1]
    out_ref[:, :n] = in_ref[...]
    out_ref[:, n:] = jnp.zeros((out_ref.shape[0], out_ref.shape[1] - n), BF16)


def sum_kernel(*refs):
    n = refs[-1].shape[1]
    refs[-1][...] = functools.reduce(jnp.add, [r[:, :n].astype(F32) for r in (refs[:3] if len(refs) > 3 else refs[:-1])]).astype(refs[-1].dtype)


def split_attn_kernel(*refs, count):
    rows = refs[0].shape[1]
    for i, ref in enumerate(refs[:count]):
        for s in range(2):
            refs[-1][s, i * rows : (i + 1) * rows, :] = ref[s]


def join_kernel(near_ref, y_ref, x_ref, xy_ref, out_ref):
    rows = near_ref.shape[1]
    blocks = ((near_ref, y_ref), (near_ref, x_ref), (x_ref, xy_ref), (y_ref, xy_ref))
    for i, pair in enumerate(blocks):
        for k, ref in enumerate(pair):
            at = (2 * i + k) * rows
            out_ref[at : at + rows, :] = ref[i % 2]


def attn_grad_kernel(keep_ref, got_ref, *refs, wide, gain_at):
    mine, other = refs[:3], refs[3:6]
    gains_ref, gains_oth_ref, order_ref = refs[6:9]
    out_refs = refs[-4:]
    half, features = keep_ref.shape[0] // 2, gains_ref.shape[1]
    n = out_refs[0].shape[0]
    gains = (gains_ref[...] + gains_oth_ref[...]).astype(BF16)
    gains = dot(order_ref[:half, :features], gains, NT)
    lane = lax.broadcasted_iota(jnp.int32, (half, LANES), 1) + (wide - LANES)
    tile = jnp.where(lane == gain_at, gains[:, 0:1], 0.0) + jnp.where(lane == gain_at + 1, gains[:, 1:2], 0.0)
    column = 0
    for k in range(3):
        at = slice(half, 2 * half) if k == 2 else slice(0, half)
        grad = dot(keep_ref[at, :], mine[k][...]) + dot(got_ref[at, :], other[k][...])
        if k == 1:
            grad = jnp.concatenate([grad[:, :-LANES], grad[:, -LANES:] + tile], axis=1)
        for i, ref in enumerate(out_refs):
            ref[:, column : column + grad.shape[1]] = grad[i * n : (i + 1) * n].astype(BF16)
        column += grad.shape[1]


def chip_flips(chips):
    bits = (chips // 2).bit_length() - 1
    z = [sum(((i >> b) & 1) << (bits - 1 - b) for b in range(bits)) for i in range(chips // 2)]
    return [2 * flip + y for flip in z for y in range(2)]


def fold_kernel(*refs, count):
    refs[-1][...] = functools.reduce(jnp.add, [r[...].astype(F32) for r in refs[:count]]).astype(refs[-1].dtype)


def mlp_kernel(place_ref, two_ref, two_oth_ref, t_ref, t_oth_ref, cot_ref, cot_oth_ref, w_ref, *refs):
    sends, keeps = refs[:2], refs[2:4]
    downs, (out_ref, out_oth_ref, d_two_ref, d_two_oth_ref) = refs[4:6], refs[6:10]
    acts, acts_t, cots, wg, wu, wd, hidden, d_gate, d_up = refs[10:19]
    chunks, down, out, out_oth, d_two, d_two_oth, in_sems, out_sems = refs[19:]
    rows = cot_ref.shape[0]
    width, half_ff, features = acts_t.shape[0], hidden.shape[1], down.shape[1]
    shards, pr = wg.shape[0], wg.shape[1]
    fr, plain, n, block = 2 * half_ff // shards, shards * pr, width // 4, width // 8
    core = place_ref[0]
    started = []

    def fetch(source, target):
        copy = pltpu.make_async_copy(source, target, in_sems.at[len(started)])
        copy.start()
        started.append(copy)
        return copy

    first = [fetch(two_ref, acts.at[pl.ds(0, rows), :])]
    gate_in = fetch(w_ref.at[:, pl.ds(2 * pr * core, pr), :], wg)
    up_in = fetch(w_ref.at[:, pl.ds(2 * pr * core + pr, pr), :], wu)
    cots_in = [fetch(cot_ref, cots.at[pl.ds(0, rows), :])]
    down_in = [
        fetch(
            w_ref.at[2 * k + core, pl.ds(4 * pr, fr), pl.ds(0, wd.shape[1])], wd.at[pl.ds(k * fr, fr), :]
        )
        for k in range(shards // 2)
    ]
    second = [fetch(two_oth_ref, acts.at[pl.ds(rows, rows), :]), fetch(cot_oth_ref, cots.at[pl.ds(rows, rows), :])]
    turned = [fetch(t_ref, acts_t.at[:, pl.ds(0, rows)])]
    for k in range(8):
        source = t_oth_ref.at[pl.ds((k ^ 1) * block, block), :]
        turned.append(fetch(source, acts_t.at[pl.ds(k * block, block), pl.ds(rows, rows)]))

    def wait(copies):
        for copy in copies:
            copy.wait()

    for half in range(2):
        at = slice(half * rows, (half + 1) * rows)
        wait(second if half else first + [gate_in])
        gate = dot(acts[at, :], wg[...].reshape(plain, half_ff))
        if not half:
            wait([up_in])
        up = dot(acts[at, :], wu[...].reshape(plain, half_ff))
        sg = 1.0 / (1.0 + jnp.exp(-gate))
        silu = gate * sg
        hidden[at, :] = (silu * up).astype(BF16)
        if not half:
            wait(cots_in + down_in)
        d_hidden = dot(cots[at, :], wd[...], NT)
        d_gate[at, :] = (d_hidden * up * sg * (1.0 + gate * (1.0 - sg))).astype(BF16)
        d_up[at, :] = (d_hidden * silu).astype(BF16)
    wait(turned)

    going = []

    def put(source, target):
        copy = pltpu.make_async_copy(source, target, out_sems.at[len(going)])
        copy.start()
        going.append(copy)

    for targets, first_row in ((sends, 2 * n), (keeps, 0)):
        for i, d in ((0, d_gate), (1, d_up)):
            grad = dot(acts_t[first_row : first_row + 2 * n, :], d[...])
            for k in range(2):
                slot = len(going) % chunks.shape[0]
                if len(going) >= chunks.shape[0]:
                    going[len(going) - chunks.shape[0]].wait()
                chunks[slot] = grad[k * n : (k + 1) * n].astype(BF16)
                put(chunks.at[slot], targets[k].at[i])
    count = len(going)
    down[...] = dot(hidden[...], cots[:, :features], TN).astype(BF16)
    chips = shards // 2
    for k, flip in enumerate(chip_flips(chips)):
        source = pl.multiple_of((place_ref[2] ^ flip) * fr, fr)
        put(down.at[pl.ds(source, fr), :], downs[1 - 2 * k // chips].at[k % (chips // 2)])

    def back(at):
        return dot(d_gate[at, :], wg[...].reshape(plain, half_ff), NT) + dot(
            d_up[at, :], wu[...].reshape(plain, half_ff), NT
        )

    d_two[...] = back(slice(0, rows))
    put(d_two, d_two_ref)
    out[...] = dot(hidden[:rows, :], wd[:, :features])
    put(out, out_ref)
    d_two_oth[...] = back(slice(rows, 2 * rows)).astype(BF16)
    put(d_two_oth, d_two_oth_ref)
    out_oth[...] = dot(hidden[rows:, :], wd[...]).astype(BF16)
    put(out_oth, out_oth_ref)
    wait(going[count - chunks.shape[0] :])


def on_device(
    tokens, cotangent, attn_gain, w_query, w_key, w_value, w_out, mlp_gain, w_gate, w_up, w_down
):
    shards = lax.axis_size("shard")
    chips = shards // 2
    zs = chips // 2
    me, rep = lax.axis_index("shard"), lax.axis_index("rep")
    core = me % 2
    micro, batch, length, features = tokens.shape
    seqs = micro * batch
    rows = seqs * length
    dr = features // shards
    quarter = -(-dr // 4)
    qr = -(-quarter // 8) * 8
    pr = -(-dr // 16) * 16
    plain = shards * pr
    width = shards * 4 * qr
    half = width // 2
    block = zs * qr
    fr = w_down.shape[0]
    half_ff = chips * fr
    nq, nk = HQ * HD, KV * HD
    nqkv = nq + 2 * nk
    wide = -(-(nqkv + 2) // LANES) * LANES
    padded = -(-features // LANES) * LANES
    full = wide + padded
    cosine, sine = (jnp.asarray(t) for t in tables(length))
    place = jnp.stack([core, rep, me // 2]).astype(jnp.int32)
    in_smem = pl.BlockSpec(memory_space=pltpu.SMEM)
    in_vmem = pl.BlockSpec(memory_space=pltpu.VMEM)
    anywhere = pl.BlockSpec(memory_space=pl.ANY)
    z_bits = zs.bit_length() - 1
    z_flip = np.array([sum(((i >> b) & 1) << (z_bits - 1 - b) for b in range(z_bits)) for i in range(zs)])

    def over(array, flip):
        return lax.ppermute(array, "shard", [(s, s ^ flip) for s in range(shards)])

    def over_core(array):
        return over(array, 1)

    def over_y(array):
        return over(array, 2)

    def over_rep(array):
        return lax.ppermute(array, "rep", [(0, 1), (1, 0)])

    def tie(arrays, *deps):
        return call(
            tie_kernel, [shape(a.shape, a.dtype) for a in arrays],
            in_specs=[anywhere] * (len(arrays) + len(deps)), out_specs=[anywhere] * len(arrays),
            input_output_aliases={i: i for i in range(len(arrays))},
        )(*arrays, *deps)

    def small(kernel, outs, arrays, deps=()):
        return call(
            kernel, outs, in_specs=[in_vmem] * len(arrays) + [anywhere] * len(deps), vmem=16 << 20
        )(*arrays, *deps)


    def feature_of(dims):
        sizes = {"core": 2, "split": 2, "f1": 2, "f2": 2, "z": zs, "row": qr}
        grid = np.meshgrid(*[np.arange(sizes[d]) for d in dims], indexing="ij")
        at = {d: g.reshape(-1) for d, g in zip(dims, grid)}
        x_flip = np.where(at["split"] == 0, at["f1"], at["f2"])
        y_flip = np.where(at["split"] == 0, at["f2"], at["f1"])
        shard = me ^ jnp.asarray(at["core"] + 2 * (y_flip + 2 * z_flip[at["z"]]), jnp.int32)
        part = 2 * (rep ^ jnp.asarray(x_flip, jnp.int32)) + jnp.asarray(at["split"], jnp.int32)
        inside = part * quarter + jnp.asarray(at["row"], jnp.int32)
        real = jnp.asarray(at["row"] < quarter) & (inside < dr)
        return jnp.where(real, shard * dr + inside, -1)[:, None]

    feats = [feature_of(("core", "f1", "split", "f2", "z", "row")), feature_of(("f1", "split", "core", "f2", "z", "row"))]
    shard, row = np.repeat(np.arange(shards), pr), np.tile(np.arange(pr), shards)
    feats.append(jnp.asarray(np.where(row < dr, shard * dr + row, -1)[:, None], jnp.int32))
    attn_order, mlp_order, plain_order = call(
        order_kernel, [shape((f.shape[0], padded)) for f in feats], grid=(1,), in_specs=[in_vmem] * 3,
        out_specs=[whole(f.shape[0], padded) for f in feats],
    )(*feats)

    floor = (16 << 20) // (2 * half_ff * shards) + 1
    depth = -(-max(4 * pr + fr, floor) // 16) * 16
    attn_piece, mlp_piece = call(
        functools.partial(pieces_kernel, quarter=quarter, qr=qr, pr=pr, fr=fr, wide=wide),
        [shape((2, qr, full)), shape((depth, half_ff))],
        grid=(1,),
        in_specs=[in_smem] + [
            whole(*w.shape)
            for w in (w_query, w_key, w_value, w_out, attn_gain[None], mlp_gain[None], w_gate, w_up, w_down)
        ],
        out_specs=[in_vmem, whole(depth, half_ff)],
    )(place, w_query, w_key, w_value, w_out, attn_gain[None], mlp_gain[None], w_gate, w_up, w_down)
    mlp = lax.all_gather(mlp_piece, "shard", axis=0, tiled=True).reshape(shards, depth, half_ff)
    parts = [attn_piece if z == 0 else over(attn_piece, 4 * z) for z in z_flip]
    x = tokens.reshape(rows, features)
    cot = cotangent.reshape(rows, features)
    cot_wide = small(copy_kernel, shape((rows, padded)), [cot], [attn_piece])
    cot_oth = over_core(cot_wide)
    attn_near = small(
        functools.partial(split_attn_kernel, count=zs), shape((2, block, full)), parts, [cot_oth, x, attn_order]
    )
    attn_y, attn_x = over_y(attn_near), over_rep(attn_near)
    attn_blocks = [attn_near, attn_y, attn_x, over_rep(attn_y)]
    attn_blocks += [over_core(b) for b in attn_blocks]

    by_rows = lambda cols: pl.BlockSpec((length, cols), lambda i: (i, 0))
    by_cols = lambda n: pl.BlockSpec((n, length), lambda i: (0, i))
    by_once = lambda *arrays: [once(*a.shape) for a in arrays]
    by_probs = pl.BlockSpec((1, HQ, length, length), lambda i: (i, 0, 0, 0))
    rows_at = lambda i, cols: pl.BlockSpec((length, cols), lambda _: (i, 0))
    shared = (*attn_blocks, attn_order, mlp_order, plain_order, cosine, sine)
    two, two_t, keep_t, send_t, qkv, probs, mixed, gain_rows, attn_all = call(
        functools.partial(attention_forward, wide=wide),
        [
            shape((rows, plain)), shape((width, rows)), shape((width, rows)), shape((width, rows)),
            shape((rows, wide)), shape((seqs, HQ, length, length)), shape((rows, features), F32),
            shape((8, features), F32), shape((width, full)),
        ],
        grid=(seqs,),
        in_specs=[by_rows(features)] + by_once(*shared),
        out_specs=[by_rows(plain)] + [by_cols(width)] * 3
        + [by_rows(wide), by_probs, by_rows(features), once(8, features), once(width, full)],
    )(x, *shared)

    n = width // 4
    (
        alpha_send, beta_send, alpha_keep, beta_keep, down_send, down_keep, out_part, out_other, d_two_mine,
        d_two_other,
    ) = call(
        mlp_kernel,
        [shape((2, n, half_ff))] * 4 + [shape((chips // 2, fr, features))] * 2
        + [shape((rows, features), F32), shape((rows, padded)), shape((rows, plain), F32), shape((rows, plain))],
        in_specs=[in_smem] + [anywhere] * 7,
        out_specs=[anywhere] * 10,
        scratch_shapes=[
            pltpu.VMEM((2 * rows, plain), BF16), pltpu.VMEM((width, 2 * rows), BF16), pltpu.VMEM((2 * rows, padded), BF16),
            pltpu.VMEM((shards, pr, half_ff), BF16), pltpu.VMEM((shards, pr, half_ff), BF16),
            pltpu.VMEM((half_ff, padded), BF16),
            pltpu.VMEM((2 * rows, half_ff), BF16), pltpu.VMEM((2 * rows, half_ff), BF16), pltpu.VMEM((2 * rows, half_ff), BF16),
            pltpu.VMEM((4, n, half_ff), BF16), pltpu.VMEM((half_ff, features), BF16), pltpu.VMEM((rows, features), F32),
            pltpu.VMEM((rows, padded), BF16), pltpu.VMEM((rows, plain), F32), pltpu.VMEM((rows, plain), BF16),
            pltpu.SemaphoreType.DMA((15 + chips,)), pltpu.SemaphoreType.DMA((12 + chips,)),
        ],
    )(place, two, over_core(two), two_t, over_core(two_t), cot_wide, cot_oth, mlp)
    def fold(parts, n, at, deps=()):
        spec = pl.BlockSpec((n, fr, features), lambda _: (at, 0, 0))
        return call(
            functools.partial(fold_kernel, count=len(parts)), shape((n, fr, features)), grid=(1,),
            in_specs=[spec] * len(parts) + [anywhere] * len(deps), out_specs=whole(n, fr, features), vmem=ADD_VMEM,
        )(*parts, *deps)

    down_parts = [down_keep, over(down_send, 4)]

    def down_stages():
        n = chips // 2
        for flip in [4 << b for b in range(1, z_bits)] + [2]:
            n //= 2
            yield n, flip

    def down_stage(n, flip, *deps):
        sent = fold(down_parts, n, 1, deps)
        down_parts.append(over(sent, flip))
        return [sent]

    def add(alpha, beta, at, size, form, deps):
        arrays = [p[0] for p in alpha + beta]
        j, cores, _, _, n = arrays[0].shape
        one = shape((j, cores, 1, size, n))
        outs = {"apart": [one, one], "stack": shape((2,) + one.shape), "last": shape((cores, j, 2, size, n))}[form]
        specs = []
        for _, lead, f in alpha + beta:
            spot = ((0, 0, f, at // size, 0), (j, cores, None, size, n))
            if lead is not None:
                spot = ((lead,) + spot[0], (None,) + spot[1])
            specs.append(pl.BlockSpec(spot[1], functools.partial(lambda where, _: where, spot[0])))
        return call(
            functools.partial(add_kernel, n_alpha=len(alpha), count=len(arrays), form=form), outs, grid=(1,),
            in_specs=specs + [anywhere] * len(deps),
            out_specs=[whole(*o.shape) for o in outs] if form == "apart" else whole(*outs.shape),
            vmem=ADD_VMEM,
        )(*arrays, *deps)

    class Reduction:
        def __init__(self, alpha_keep, beta_keep, alpha_send, beta_send):
            self.early = [[alpha_keep, over_rep(alpha_send)], [beta_keep, over_y(beta_send)]]
            self.late = []
            self.both = []
            self.size = block

        def parts(self, f):
            return [
                [(a, None, f) for a in self.early[s]]
                + [(pair[s], None, 0) for pair in self.late] + [(a, s, 0) for a in self.both]
                for s in range(2)
            ]

        def second(self, *deps):
            alpha_sent, beta_sent = add(*self.parts(1), 0, block, "apart", deps)
            self.late.append((over_y(alpha_sent), over_rep(beta_sent)))
            return [alpha_sent, beta_sent]

        def z(self, *deps):
            self.size //= 2
            sent = add(*self.parts(0), self.size, self.size, "stack", deps)
            self.both.append(over(sent, 4 << (len(self.both))))
            return [sent]

        def last(self, *deps):
            mine = add(*self.parts(0), 0, qr, "last", deps)
            return mine, over_rep(mine)

    mlp_sum = Reduction(
        *[a.reshape(2, 2, 2, block, half_ff) for a in (alpha_keep, beta_keep, alpha_send, beta_send)]
    )

    low = wide // LANES // 8 * 8 * LANES
    arrays = (gain_rows, attn_all, attn_order)
    d_low, d_high, d_attn, grad_tokens, grad_gains = call(
        functools.partial(attention_backward, wide=wide),
        [
            shape((rows, low)), shape((rows, wide - low)), shape((rows, padded)), shape((rows, features)),
            shape((8, features), F32),
        ],
        grid=(seqs,),
        in_specs=[by_rows(plain), by_rows(plain)] + by_once(plain_order) + [by_rows(features)] * 2
        + by_once(*arrays) + [by_rows(wide), by_probs] + by_once(cosine, sine) + [by_rows(features)],
        out_specs=[by_rows(low), by_rows(wide - low), by_rows(padded), by_rows(features), whole(8, features)],
        vmem=40 << 20,
    )(d_two_mine, over_core(d_two_other), plain_order, mixed, cot, *arrays, qkv, probs, cosine, sine, x)
    down_left = list(down_stages())
    out_oth, got_t = over_core(out_other), over_core(send_t)
    sent = down_stage(*down_left.pop(0), d_low, out_oth, got_t)
    sent += mlp_sum.second(*sent)
    n = half // 4
    arrays = [d_low, d_high, d_attn]
    arrays = [
        keep_t, got_t, *arrays, *[over_core(a) for a in arrays], grad_gains, over_core(grad_gains), attn_order
    ]
    attn_grads = call(
        functools.partial(attn_grad_kernel, wide=wide, gain_at=nqkv),
        [shape((n, full))] * 4,
        grid=(1,),
        in_specs=by_once(*arrays) + [anywhere] * len(sent),
        out_specs=[whole(n, full)] * 4,
        vmem=32 << 20,
    )(*arrays, *sent)
    attn_sum = Reduction(*[a.reshape(1, 1, 2, block, full) for a in attn_grads])
    for i in range(seqs):
        output = call(
            sum_kernel, shape((rows, features)), grid=(1,),
            in_specs=[rows_at(i, features), rows_at(i, features), rows_at(i, padded)]
            + [anywhere] * (2 if i else 1),
            out_specs=rows_at(i, features), input_output_aliases={4: 0} if i else {},
        )(out_part, mixed, out_oth, attn_grads[0], *([output] if i else []))
    sent = mlp_sum.z(attn_grads[0], output)
    sent = attn_sum.second(*sent)
    for step in range(z_bits):
        if step:
            sent = mlp_sum.z(*sent)
        if down_left:
            sent = down_stage(*down_left.pop(0), *sent)
        sent = attn_sum.z(*sent)
    while down_left:
        sent = down_stage(*down_left.pop(0), *sent)
    down_mine = fold(down_parts, 1, 0, sent)
    down_from = over_rep(down_mine)
    mlp_mine, mlp_from = mlp_sum.last(down_mine)
    attn_mine, attn_from = attn_sum.last(mlp_mine)

    grad_gate, grad_up = call(
        functools.partial(shards_kernel, quarter=quarter, fr=fr),
        [shape((dr, 2 * half_ff), F32)] * 2,
        grid=(1,),
        in_specs=[in_smem] + by_once(*[mlp_mine] * 4), out_specs=[whole(dr, 2 * half_ff)] * 2,
    )(place, mlp_mine, mlp_from, over_core(mlp_mine), over_core(mlp_from))
    grad_down = call(
        functools.partial(fold_kernel, count=2), shape((1, fr, features), F32), grid=(1,),
        in_specs=by_once(down_mine, down_mine) + [anywhere], out_specs=whole(1, fr, features), vmem=ADD_VMEM,
    )(down_mine, down_from, grad_gate)
    attn_dims = ((dr, nq), (dr, nk), (dr, nk), (1, dr), (1, dr), (dr, features))
    grad_query, grad_key, grad_value, grad_gain_one, grad_gain_two, grad_out = call(
        functools.partial(attn_shards_kernel, quarter=quarter, wide=wide),
        [shape(dims, F32) for dims in attn_dims],
        grid=(1,),
        in_specs=[in_smem] + by_once(attn_mine, attn_mine) + [anywhere] * 2,
        out_specs=[whole(*dims) for dims in attn_dims],
    )(place, attn_mine, attn_from, grad_down, grad_gate)
    dims = tokens.shape
    return (
        output.reshape(dims), grad_tokens.reshape(dims), grad_gain_one.reshape(dr), grad_query, grad_key, grad_value,
        grad_out, grad_gain_two.reshape(dr), grad_gate, grad_up, grad_down[0],
    )


def solution(mesh):
    data = P(None, ("rep", "shard"), None, None)
    vector, matrix = P("shard"), P("shard", None)
    weights = (vector, matrix, matrix, matrix, matrix, vector, matrix, matrix, matrix)
    return jax.shard_map(
        on_device,
        mesh=mesh,
        in_specs=(data, data) + weights,
        out_specs=(data, data) + weights,
        check_vma=False,
    )
```

```python
import functools
import math

import jax
import jax.numpy as jnp
import numpy as np
from jax import lax
from jax.experimental import pallas as pl
from jax.experimental.pallas import tpu as pltpu
from jax.sharding import PartitionSpec as P

HQ = 15
KV = 5
HD = 64
EPSILON = 1e-05
THETA = 100000.0
F32 = jnp.float32
BF16 = jnp.bfloat16
LANES = 128
COLS = 256
NN = ((1,), (0,))
NT = ((1,), (1,))
TN = ((0,), (0,))
VMEM = 60 << 20
ADD_VMEM = 16 << 20


def dot(a, b, contract=NN):
    return lax.dot_general(a, b, (contract, ((), ())), preferred_element_type=F32)


def call(kernel, out_shape, *, vmem=VMEM, **how):
    return pl.pallas_call(
        kernel,
        out_shape=out_shape,
        compiler_params=pltpu.CompilerParams(vmem_limit_bytes=vmem),
        cost_estimate=pl.CostEstimate(flops=1 << 20, bytes_accessed=1 << 12, transcendentals=0),
        **how,
    )


def shape(dims, dtype=BF16):
    return jax.ShapeDtypeStruct(dims, dtype)


def whole(*dims):
    return pl.BlockSpec(dims, lambda *_: (0,) * len(dims))


def once(*dims):
    return pl.BlockSpec(dims, lambda *_: (0,) * len(dims), pipeline_mode=pl.Buffered(1))


def tables(length):
    frequency = THETA ** (-2.0 * np.arange(HD // 2, dtype=np.float32) / HD)
    angles = np.arange(length, dtype=np.float32)[:, None] * frequency.astype(np.float32)[None, :]
    cosine, sine = np.cos(angles), np.sin(angles)
    return np.tile(cosine, (1, 4)), np.concatenate([-sine, sine, -sine, sine], axis=1)


def turn(tile, cosine, sine, low):
    other = jnp.where(low, pltpu.roll(tile, LANES - 32, 1), pltpu.roll(tile, 32, 1))
    return tile * cosine + other * sine


def placed(tile, half):
    lane = lax.broadcasted_iota(jnp.int32, tile.shape, 1)
    alone = jnp.where((lane >= HD) == (half == 1), tile, 0.0)
    moved = pltpu.roll(alone, HD, 1)
    pair = (moved, alone) if half else (alone, moved)
    return [one.astype(BF16) for one in pair]


def placed_turned(tile, half):
    tile = tile.T
    row = lax.broadcasted_iota(jnp.int32, tile.shape, 0)
    alone = jnp.where((row >= HD) == (half == 1), tile, 0.0)
    moved = jnp.concatenate([alone[HD:], alone[:HD]], axis=0)
    pair = (moved, alone) if half else (alone, moved)
    return [one.astype(BF16) for one in pair]


def attention_forward(x_ref, *refs, wide):
    blocks, (attn_order_ref, mlp_order_ref, plain_order_ref, cos_ref, sin_ref) = refs[:8], refs[8:13]
    two_ref, two_t_ref, keep_ref, send_ref, qkv_ref, probs_ref, mixed_ref, gain_ref, all_ref = refs[13:]

    @pl.when(pl.program_id(0) == 0)
    def _():
        n = all_ref.shape[0] // 16
        for c in range(2):
            near, over_y, over_x, over_both = blocks[4 * c : 4 * c + 4]
            pairs = ((near, over_y), (near, over_x), (over_x, over_both), (over_y, over_both))
            for i, pair in enumerate(pairs):
                for k, ref in enumerate(pair):
                    at = (8 * c + 2 * i + k) * n
                    all_ref[at : at + n, :] = ref[i % 2]

    length, features = x_ref.shape
    half = all_ref.shape[0] // 2
    to_order = attn_order_ref[:, :features]
    last = slice(wide - LANES, wide)
    gains = dot(all_ref[:, last], to_order, TN)
    gain_one, gain_two = gains[HD : HD + 1], gains[HD + 1 : HD + 2]
    gain_ref[...] = gains[HD : HD + 8]
    x = x_ref[...].astype(F32)
    r1 = lax.rsqrt(jnp.mean(x * x, axis=-1, keepdims=True) + EPSILON)
    normed = (x * r1 * gain_one).astype(BF16)
    spread = dot(normed, to_order, NT).astype(BF16)
    turned = dot(to_order, normed, NT).astype(BF16)
    keep_ref[:half, :] = turned[:half]
    send_ref[:half, :] = turned[half:]
    lane = lax.broadcasted_iota(jnp.int32, (length, LANES), 1)
    low = lane % HD < HD // 2
    cosine, sine = cos_ref[...], sin_ref[...]
    tiles, heads = [], {}
    for t in range(wide // LANES):
        cols = slice(t * LANES, (t + 1) * LANES)
        tile = dot(spread, all_ref[:, cols])
        if t * 2 < HQ + KV:
            tile = turn(tile, cosine, sine, low)
        if t == wide // LANES - 1:
            tile = jnp.where(lane < HD, tile, 0.0)
        short = tile.astype(BF16)
        qkv_ref[:, cols] = short
        tiles.append(short)
        for n in (2 * t, 2 * t + 1):
            if HQ <= n < HQ + KV:
                heads[n] = placed(tile, n % 2)
            elif HQ + KV <= n < HQ + 2 * KV:
                heads[n] = placed_turned(tile, n % 2)
    causal = lax.broadcasted_iota(jnp.int32, (length, length), 0) <= lax.broadcasted_iota(
        jnp.int32, (length, length), 1
    )
    context = [None] * ((HQ + 1) // 2)
    for h in range(HQ):
        j, t, s = h // (HQ // KV), h // 2, h % 2
        scores = dot(heads[HQ + j][s], tiles[t], NT) * (1.0 / math.sqrt(HD))
        scores = jnp.where(causal, scores, -1e30)
        exponent = jnp.exp(scores - jnp.max(scores, axis=0, keepdims=True))
        probs = exponent * (1.0 / jnp.sum(exponent, axis=0, keepdims=True))
        probs = probs.astype(BF16)
        probs_ref[0, h] = probs
        part = dot(heads[HQ + KV + j][s], probs)
        context[t] = part if context[t] is None else context[t] + part
    context = jnp.concatenate([c.astype(BF16) for c in context], axis=0)
    turned = dot(attn_order_ref[...], context).astype(BF16)
    mixed = x + dot(turned, all_ref[:, wide : wide + features], TN)
    keep_ref[half:, :] = turned[:half]
    send_ref[half:, :] = turned[half:]
    mixed_ref[...] = mixed
    r2 = lax.rsqrt(jnp.mean(mixed * mixed, axis=-1, keepdims=True) + EPSILON)
    two = (mixed * r2 * gain_two).astype(BF16)
    two_ref[...] = dot(two, plain_order_ref[:, :features], NT).astype(BF16)
    two_t_ref[...] = dot(mlp_order_ref[:, :features], two, NT).astype(BF16)


def attention_backward(
    mine_ref, other_ref, plain_order_ref, mixed_ref, cot_ref, gain_ref, all_ref, order_ref, qkv_ref,
    probs_ref, cos_ref, sin_ref, x_ref, d_low_ref, d_high_ref, d_attn_ref, out_ref, grad_ref, *, wide
):
    length, features = mixed_ref.shape
    total = (mine_ref[...] + other_ref[...].astype(F32)).astype(BF16)
    d_two = dot(total, plain_order_ref[:, :features])
    mixed = mixed_ref[...]
    r2 = lax.rsqrt(jnp.mean(mixed * mixed, axis=-1, keepdims=True) + EPSILON)
    unit = mixed * r2
    e2 = d_two * gain_ref[1:2, :]
    d_mixed = cot_ref[...].astype(F32) + r2 * (e2 - unit * jnp.mean(e2 * unit, axis=-1, keepdims=True))
    d_attn = d_mixed.astype(BF16)
    d_attn_ref[:, :features] = d_attn
    d_attn_ref[:, features:] = jnp.zeros((length, d_attn_ref.shape[1] - features), BF16)
    grad_gain_two = jnp.sum(d_two * unit, axis=0, keepdims=True)
    d_context = dot(d_attn, all_ref[:, wide : wide + features], NT).astype(BF16)
    d_context = dot(d_context, order_ref[...]).astype(BF16)
    lane = lax.broadcasted_iota(jnp.int32, (length, LANES), 1)
    low = lane % HD < HD // 2
    cosine, sine = cos_ref[...], -sin_ref[...]

    def tile_of(n):
        t = n // 2
        return qkv_ref[:, t * LANES : (t + 1) * LANES]

    d_tiles = [None] * ((HQ + 2 * KV + 1) // 2)

    def add(t, part):
        d_tiles[t] = part if d_tiles[t] is None else d_tiles[t] + part

    groups = HQ // KV
    d_query = [None] * ((HQ + 1) // 2)
    for j in range(KV):
        keys = placed_turned(tile_of(HQ + j).astype(F32), (HQ + j) % 2)
        values = placed(tile_of(HQ + KV + j).astype(F32), (HQ + KV + j) % 2)
        d_key, d_value = [None, None], [None, None]
        for h in range(j * groups, (j + 1) * groups):
            t, s = h // 2, h % 2
            d_con = d_context[:, t * LANES : (t + 1) * LANES]
            probs = probs_ref[0, h]
            wide_probs = probs.astype(F32)
            d_probs = dot(values[s], d_con, NT)
            inner = jnp.sum(d_probs * wide_probs, axis=0, keepdims=True)
            d_scores = (wide_probs * (d_probs - inner) * (1.0 / math.sqrt(HD))).astype(BF16)
            part = dot(keys[s], d_scores)
            d_query[t] = part if d_query[t] is None else d_query[t] + part
            part = dot(d_scores, tile_of(h))
            d_key[s] = part if d_key[s] is None else d_key[s] + part
            part = dot(probs, d_con)
            d_value[s] = part if d_value[s] is None else d_value[s] + part
        for n, pair in ((HQ + j, d_key), (HQ + KV + j, d_value)):
            here = n % 2
            mask = (lane >= HD) == (here == 1)
            total = jnp.where(mask, pair[here] + pltpu.roll(pair[1 - here], HD, 1), 0.0)
            add(n // 2, total)
    for t, tile in enumerate(d_query):
        add(t, tile.T)
    for t, tile in enumerate(d_tiles):
        if t * 2 < HQ + KV:
            tile = turn(tile, cosine, sine, low)
        ref, at = (d_low_ref, t * LANES) if t * LANES < d_low_ref.shape[1] else (d_high_ref, t * LANES - d_low_ref.shape[1])
        ref[:, at : at + LANES] = tile.astype(BF16)
    split = d_low_ref.shape[1]
    d_normed = dot(d_low_ref[...], all_ref[:, :split], NT) + dot(d_high_ref[...], all_ref[:, split:wide], NT)
    d_normed = d_normed.astype(BF16)
    d_normed = dot(d_normed, order_ref[:, :features])
    x = x_ref[...].astype(F32)
    r1 = lax.rsqrt(jnp.mean(x * x, axis=-1, keepdims=True) + EPSILON)
    unit = x * r1
    e1 = d_normed * gain_ref[0:1, :]
    out = d_mixed + r1 * (e1 - unit * jnp.mean(e1 * unit, axis=-1, keepdims=True))
    out_ref[...] = out.astype(BF16)
    grad_gain_one = jnp.sum(d_normed * unit, axis=0, keepdims=True)
    grads = jnp.concatenate([grad_gain_one, grad_gain_two, jnp.zeros((6, features), F32)], axis=0)


    @pl.when(pl.program_id(0) == 0)
    def _():
        grad_ref[...] = grads

    @pl.when(pl.program_id(0) > 0)
    def _():
        grad_ref[...] += grads


def flipped(array, axis, block):
    n = array.shape[axis] // block
    parts = [lax.slice_in_dim(array, i * block, (i + 1) * block, axis=axis) for i in range(n)]
    return jnp.concatenate([parts[i ^ 1] for i in range(n)], axis=axis)


def row_quarters(w, quarter, qr):
    dr, n = w.shape
    parts = []
    for q in range(4):
        part = w[min(q * quarter, dr) : min((q + 1) * quarter, dr), :]
        parts.append(jnp.concatenate([part, jnp.zeros((qr - part.shape[0], n), F32)], axis=0))
    return parts


def pieces_kernel(
    place_ref, wq_ref, wk_ref, wv_ref, wo_ref, g1_ref, g2_ref, wg_ref, wu_ref, wd_ref, attn_ref, mlp_ref,
    *, quarter, qr, pr, fr, wide
):
    rep, dr = place_ref[1], wq_ref.shape[0]

    def store(at, w):
        parts = row_quarters(w, quarter, qr)
        for s in range(2):
            attn_ref[s, :, at : at + w.shape[1]] = jnp.where(rep == 0, parts[s], parts[2 + s]).astype(BF16)

    wide_of = lambda ref: ref[...].astype(F32)
    eye = (
        lax.broadcasted_iota(jnp.int32, (dr, dr), 0) == lax.broadcasted_iota(jnp.int32, (dr, dr), 1)
    ).astype(F32)
    columns = [jnp.sum(eye * wide_of(ref), axis=1, keepdims=True) for ref in (g1_ref, g2_ref)]
    blank = jnp.zeros((dr, wide - wq_ref.shape[1] - 2 * wk_ref.shape[1] - 2), F32)
    store(0, jnp.concatenate([wide_of(wq_ref), wide_of(wk_ref), wide_of(wv_ref)] + columns + [blank], axis=1))
    w = wide_of(wo_ref)
    store(wide, jnp.concatenate([w, jnp.zeros((dr, attn_ref.shape[2] - wide - w.shape[1]), F32)], axis=1))
    halves = []
    for ref in (wg_ref, wu_ref):
        w = wide_of(ref)
        chunks = [w[:, i * fr : (i + 1) * fr] for i in range(w.shape[1] // fr)]
        halves.append([jnp.concatenate(chunks[c::2], axis=1) for c in range(2)])
    row = jnp.concatenate([halves[0][0], halves[1][0], halves[0][1], halves[1][1]], axis=1)
    rows, lanes = pr, mlp_ref.shape[1]
    row = jnp.concatenate([row, jnp.zeros((rows - dr, row.shape[1]), F32)], axis=0).astype(BF16)
    for g in range(4):
        mlp_ref[g * rows : (g + 1) * rows, :] = row[:, g * lanes : (g + 1) * lanes]
    at, n = 4 * rows, wd_ref.shape[1]
    mlp_ref[at : at + fr, :n] = wd_ref[...]
    mlp_ref[at : at + fr, n:] = jnp.zeros((fr, lanes - n), BF16)
    if at + fr < mlp_ref.shape[0]:
        mlp_ref[at + fr :, :] = jnp.zeros((mlp_ref.shape[0] - at - fr, lanes), BF16)


def tie_kernel(*refs):
    del refs


def add_kernel(*refs, n_alpha, count, form):
    totals = [ref[...].astype(F32) for ref in refs[:count]]
    alpha, beta = functools.reduce(jnp.add, totals[:n_alpha]), functools.reduce(jnp.add, totals[n_alpha:])
    if form == "apart":
        refs[-2][:, :, 0] = alpha.astype(BF16)
        refs[-1][:, :, 0] = beta.astype(BF16)
    elif form == "stack":
        refs[-1][0, :, :, 0] = alpha.astype(BF16)
        refs[-1][1, :, :, 0] = beta.astype(BF16)
    else:
        for c in range(alpha.shape[1]):
            refs[-1][c, :, 0] = alpha[:, c].astype(BF16)
            refs[-1][c, :, 1] = beta[:, c].astype(BF16)


def shards_kernel(place_ref, mine_ref, other_ref, got_ref, got_other_ref, *refs, quarter, fr):
    gate_ref, up_ref = refs[-2:]
    core, rep = place_ref[0], place_ref[1]
    dr = gate_ref.shape[0]
    for at, out_ref in ((0, gate_ref), (1, up_ref)):
        sides = []
        for c, mine, other in ((0, mine_ref, other_ref), (1, got_ref, got_other_ref)):
            a, b = mine[c, at].astype(F32), other[c, at].astype(F32)
            low, high = jnp.where(rep == 0, a, b), jnp.where(rep == 0, b, a)
            rows = [half[s][:quarter] for half in (low, high) for s in range(2)]
            sides.append(jnp.concatenate(rows, axis=0)[:dr])
        even, odd = jnp.where(core == 0, sides[0], sides[1]), jnp.where(core == 0, sides[1], sides[0])
        chunks = []
        for k in range(even.shape[1] // fr):
            chunks += [even[:, k * fr : (k + 1) * fr], odd[:, k * fr : (k + 1) * fr]]
        out_ref[...] = jnp.concatenate(chunks, axis=1)


def attn_shards_kernel(place_ref, mine_ref, other_ref, down_mine_ref, down_other_ref, *refs, quarter, wide):
    query_ref, key_ref, value_ref, *gain_refs, out_ref, down_ref = refs[-7:]
    down_ref[...] = down_mine_ref[...].astype(F32) + down_other_ref[...].astype(F32)
    rep, dr = place_ref[1], out_ref.shape[0]
    a, b = mine_ref[0, 0].astype(F32), other_ref[0, 0].astype(F32)
    low, high = jnp.where(rep == 0, a, b), jnp.where(rep == 0, b, a)
    rows = jnp.concatenate([half[s][:quarter] for half in (low, high) for s in range(2)], axis=0)[:dr]
    at = 0
    for ref in (query_ref, key_ref, value_ref):
        ref[...] = rows[:, at : at + ref.shape[1]]
        at += ref.shape[1]
    out_ref[...] = rows[:, wide : wide + out_ref.shape[1]]
    eye = lax.broadcasted_iota(jnp.int32, (dr, dr), 0) == lax.broadcasted_iota(jnp.int32, (dr, dr), 1)
    for i, ref in enumerate(gain_refs):
        ref[...] = jnp.sum(jnp.where(eye, rows[:, at + i : at + i + 1], 0.0), axis=0, keepdims=True)


def order_kernel(*refs):
    for feat_ref, out_ref in zip(refs[:3], refs[3:]):
        column = lax.broadcasted_iota(jnp.int32, out_ref.shape, 1)
        out_ref[...] = (feat_ref[...] == column).astype(F32).astype(BF16)


def copy_kernel(in_ref, *refs):
    out_ref, n = refs[-1], in_ref.shape[1]
    out_ref[:, :n] = in_ref[...]
    out_ref[:, n:] = jnp.zeros((out_ref.shape[0], out_ref.shape[1] - n), BF16)


def sum_kernel(*refs):
    n = refs[-1].shape[1]
    refs[-1][...] = functools.reduce(jnp.add, [r[:, :n].astype(F32) for r in (refs[:3] if len(refs) > 3 else refs[:-1])]).astype(refs[-1].dtype)


def split_attn_kernel(*refs, count):
    rows = refs[0].shape[1]
    for i, ref in enumerate(refs[:count]):
        for s in range(2):
            refs[-1][s, i * rows : (i + 1) * rows, :] = ref[s]


def join_kernel(near_ref, y_ref, x_ref, xy_ref, out_ref):
    rows = near_ref.shape[1]
    blocks = ((near_ref, y_ref), (near_ref, x_ref), (x_ref, xy_ref), (y_ref, xy_ref))
    for i, pair in enumerate(blocks):
        for k, ref in enumerate(pair):
            at = (2 * i + k) * rows
            out_ref[at : at + rows, :] = ref[i % 2]


def attn_grad_kernel(keep_ref, got_ref, *refs, wide, gain_at):
    mine, other = refs[:3], refs[3:6]
    gains_ref, gains_oth_ref, order_ref = refs[6:9]
    out_refs = refs[-4:]
    half, features = keep_ref.shape[0] // 2, gains_ref.shape[1]
    n = out_refs[0].shape[0]
    gains = (gains_ref[...] + gains_oth_ref[...]).astype(BF16)
    gains = dot(order_ref[:half, :features], gains, NT)
    lane = lax.broadcasted_iota(jnp.int32, (half, LANES), 1) + (wide - LANES)
    tile = jnp.where(lane == gain_at, gains[:, 0:1], 0.0) + jnp.where(lane == gain_at + 1, gains[:, 1:2], 0.0)
    column = 0
    for k in range(3):
        at = slice(half, 2 * half) if k == 2 else slice(0, half)
        grad = dot(keep_ref[at, :], mine[k][...]) + dot(got_ref[at, :], other[k][...])
        if k == 1:
            grad = jnp.concatenate([grad[:, :-LANES], grad[:, -LANES:] + tile], axis=1)
        for i, ref in enumerate(out_refs):
            ref[:, column : column + grad.shape[1]] = grad[i * n : (i + 1) * n].astype(BF16)
        column += grad.shape[1]


def chip_flips(chips):
    bits = (chips // 2).bit_length() - 1
    z = [sum(((i >> b) & 1) << (bits - 1 - b) for b in range(bits)) for i in range(chips // 2)]
    return [2 * flip + y for flip in z for y in range(2)]


def fold_kernel(*refs, count):
    refs[-1][...] = functools.reduce(jnp.add, [r[...].astype(F32) for r in refs[:count]]).astype(refs[-1].dtype)


def mlp_kernel(place_ref, two_ref, two_oth_ref, t_ref, t_oth_ref, cot_ref, cot_oth_ref, w_ref, *refs):
    sends, keeps = refs[:2], refs[2:4]
    downs, (out_ref, out_oth_ref, d_two_ref, d_two_oth_ref) = refs[4:6], refs[6:10]
    acts, acts_t, cots, wg, wu, wd, hidden, d_gate, d_up = refs[10:19]
    chunks, down, out, out_oth, d_two, d_two_oth, in_sems, out_sems = refs[19:]
    rows = cot_ref.shape[0]
    width, half_ff, features = acts_t.shape[0], hidden.shape[1], down.shape[1]
    shards, pr = wg.shape[0], wg.shape[1]
    fr, plain, n, block = 2 * half_ff // shards, shards * pr, width // 4, width // 8
    core = place_ref[0]
    started = []

    def fetch(source, target):
        copy = pltpu.make_async_copy(source, target, in_sems.at[len(started)])
        copy.start()
        started.append(copy)
        return copy

    first = [fetch(two_ref, acts.at[pl.ds(0, rows), :])]
    gate_in = fetch(w_ref.at[:, pl.ds(2 * pr * core, pr), :], wg)
    up_in = fetch(w_ref.at[:, pl.ds(2 * pr * core + pr, pr), :], wu)
    cots_in = [fetch(cot_ref, cots.at[pl.ds(0, rows), :])]
    down_in = [
        fetch(
            w_ref.at[2 * k + core, pl.ds(4 * pr, fr), pl.ds(0, wd.shape[1])], wd.at[pl.ds(k * fr, fr), :]
        )
        for k in range(shards // 2)
    ]
    second = [fetch(two_oth_ref, acts.at[pl.ds(rows, rows), :]), fetch(cot_oth_ref, cots.at[pl.ds(rows, rows), :])]
    turned = [fetch(t_ref, acts_t.at[:, pl.ds(0, rows)])]
    for k in range(8):
        source = t_oth_ref.at[pl.ds((k ^ 1) * block, block), :]
        turned.append(fetch(source, acts_t.at[pl.ds(k * block, block), pl.ds(rows, rows)]))

    def wait(copies):
        for copy in copies:
            copy.wait()

    for half in range(2):
        at = slice(half * rows, (half + 1) * rows)
        wait(second if half else first + [gate_in])
        gate = dot(acts[at, :], wg[...].reshape(plain, half_ff))
        if not half:
            wait([up_in])
        up = dot(acts[at, :], wu[...].reshape(plain, half_ff))
        sg = 1.0 / (1.0 + jnp.exp(-gate))
        silu = gate * sg
        hidden[at, :] = (silu * up).astype(BF16)
        if not half:
            wait(cots_in + down_in)
        d_hidden = dot(cots[at, :], wd[...], NT)
        d_gate[at, :] = (d_hidden * up * sg * (1.0 + gate * (1.0 - sg))).astype(BF16)
        d_up[at, :] = (d_hidden * silu).astype(BF16)
    wait(turned)

    going = []

    def put(source, target):
        copy = pltpu.make_async_copy(source, target, out_sems.at[len(going)])
        copy.start()
        going.append(copy)

    for targets, first_row in ((sends, 2 * n), (keeps, 0)):
        for i, d in ((0, d_gate), (1, d_up)):
            grad = dot(acts_t[first_row : first_row + 2 * n, :], d[...])
            for k in range(2):
                slot = len(going) % chunks.shape[0]
                if len(going) >= chunks.shape[0]:
                    going[len(going) - chunks.shape[0]].wait()
                chunks[slot] = grad[k * n : (k + 1) * n].astype(BF16)
                put(chunks.at[slot], targets[k].at[i])
    count = len(going)
    down[...] = dot(hidden[...], cots[:, :features], TN).astype(BF16)
    chips = shards // 2
    for k, flip in enumerate(chip_flips(chips)):
        source = pl.multiple_of((place_ref[2] ^ flip) * fr, fr)
        put(down.at[pl.ds(source, fr), :], downs[1 - 2 * k // chips].at[k % (chips // 2)])

    def back(at):
        return dot(d_gate[at, :], wg[...].reshape(plain, half_ff), NT) + dot(
            d_up[at, :], wu[...].reshape(plain, half_ff), NT
        )

    d_two[...] = back(slice(0, rows))
    put(d_two, d_two_ref)
    out[...] = dot(hidden[:rows, :], wd[:, :features])
    put(out, out_ref)
    d_two_oth[...] = back(slice(rows, 2 * rows)).astype(BF16)
    put(d_two_oth, d_two_oth_ref)
    out_oth[...] = dot(hidden[rows:, :], wd[...]).astype(BF16)
    put(out_oth, out_oth_ref)
    wait(going[count - chunks.shape[0] :])


def on_device(
    tokens, cotangent, attn_gain, w_query, w_key, w_value, w_out, mlp_gain, w_gate, w_up, w_down
):
    shards = lax.axis_size("shard")
    chips = shards // 2
    zs = chips // 2
    me, rep = lax.axis_index("shard"), lax.axis_index("rep")
    core = me % 2
    micro, batch, length, features = tokens.shape
    seqs = micro * batch
    rows = seqs * length
    dr = features // shards
    quarter = -(-dr // 4)
    qr = -(-quarter // 8) * 8
    pr = -(-dr // 16) * 16
    plain = shards * pr
    width = shards * 4 * qr
    half = width // 2
    block = zs * qr
    fr = w_down.shape[0]
    half_ff = chips * fr
    nq, nk = HQ * HD, KV * HD
    nqkv = nq + 2 * nk
    wide = -(-(nqkv + 2) // LANES) * LANES
    padded = -(-features // LANES) * LANES
    full = wide + padded
    cosine, sine = (jnp.asarray(t) for t in tables(length))
    place = jnp.stack([core, rep, me // 2]).astype(jnp.int32)
    in_smem = pl.BlockSpec(memory_space=pltpu.SMEM)
    in_vmem = pl.BlockSpec(memory_space=pltpu.VMEM)
    anywhere = pl.BlockSpec(memory_space=pl.ANY)
    z_bits = zs.bit_length() - 1
    z_flip = np.array([sum(((i >> b) & 1) << (z_bits - 1 - b) for b in range(z_bits)) for i in range(zs)])

    def over(array, flip):
        return lax.ppermute(array, "shard", [(s, s ^ flip) for s in range(shards)])

    def over_core(array):
        return over(array, 1)

    def over_y(array):
        return over(array, 2)

    def over_rep(array):
        return lax.ppermute(array, "rep", [(0, 1), (1, 0)])

    def tie(arrays, *deps):
        return call(
            tie_kernel, [shape(a.shape, a.dtype) for a in arrays],
            in_specs=[anywhere] * (len(arrays) + len(deps)), out_specs=[anywhere] * len(arrays),
            input_output_aliases={i: i for i in range(len(arrays))},
        )(*arrays, *deps)

    def small(kernel, outs, arrays, deps=()):
        return call(
            kernel, outs, in_specs=[in_vmem] * len(arrays) + [anywhere] * len(deps), vmem=16 << 20
        )(*arrays, *deps)


    def feature_of(dims):
        sizes = {"core": 2, "split": 2, "f1": 2, "f2": 2, "z": zs, "row": qr}
        grid = np.meshgrid(*[np.arange(sizes[d]) for d in dims], indexing="ij")
        at = {d: g.reshape(-1) for d, g in zip(dims, grid)}
        x_flip = np.where(at["split"] == 0, at["f1"], at["f2"])
        y_flip = np.where(at["split"] == 0, at["f2"], at["f1"])
        shard = me ^ jnp.asarray(at["core"] + 2 * (y_flip + 2 * z_flip[at["z"]]), jnp.int32)
        part = 2 * (rep ^ jnp.asarray(x_flip, jnp.int32)) + jnp.asarray(at["split"], jnp.int32)
        inside = part * quarter + jnp.asarray(at["row"], jnp.int32)
        real = jnp.asarray(at["row"] < quarter) & (inside < dr)
        return jnp.where(real, shard * dr + inside, -1)[:, None]

    feats = [feature_of(("core", "f1", "split", "f2", "z", "row")), feature_of(("f1", "split", "core", "f2", "z", "row"))]
    shard, row = np.repeat(np.arange(shards), pr), np.tile(np.arange(pr), shards)
    feats.append(jnp.asarray(np.where(row < dr, shard * dr + row, -1)[:, None], jnp.int32))
    attn_order, mlp_order, plain_order = call(
        order_kernel, [shape((f.shape[0], padded)) for f in feats], grid=(1,), in_specs=[in_vmem] * 3,
        out_specs=[whole(f.shape[0], padded) for f in feats],
    )(*feats)

    floor = (16 << 20) // (2 * half_ff * shards) + 1
    depth = -(-max(4 * pr + fr, floor) // 16) * 16
    attn_piece, mlp_piece = call(
        functools.partial(pieces_kernel, quarter=quarter, qr=qr, pr=pr, fr=fr, wide=wide),
        [shape((2, qr, full)), shape((depth, half_ff))],
        grid=(1,),
        in_specs=[in_smem] + [
            whole(*w.shape)
            for w in (w_query, w_key, w_value, w_out, attn_gain[None], mlp_gain[None], w_gate, w_up, w_down)
        ],
        out_specs=[in_vmem, whole(depth, half_ff)],
    )(place, w_query, w_key, w_value, w_out, attn_gain[None], mlp_gain[None], w_gate, w_up, w_down)
    mlp = lax.all_gather(mlp_piece, "shard", axis=0, tiled=True).reshape(shards, depth, half_ff)
    parts = [attn_piece if z == 0 else over(attn_piece, 4 * z) for z in z_flip]
    x = tokens.reshape(rows, features)
    cot = cotangent.reshape(rows, features)
    cot_wide = small(copy_kernel, shape((rows, padded)), [cot], [attn_piece])
    cot_oth = over_core(cot_wide)
    attn_near = small(
        functools.partial(split_attn_kernel, count=zs), shape((2, block, full)), parts, [cot_oth, x, attn_order]
    )
    attn_y, attn_x = over_y(attn_near), over_rep(attn_near)
    attn_blocks = [attn_near, attn_y, attn_x, over_rep(attn_y)]
    attn_blocks += [over_core(b) for b in attn_blocks]

    by_rows = lambda cols: pl.BlockSpec((length, cols), lambda i: (i, 0))
    by_cols = lambda n: pl.BlockSpec((n, length), lambda i: (0, i))
    by_once = lambda *arrays: [once(*a.shape) for a in arrays]
    by_probs = pl.BlockSpec((1, HQ, length, length), lambda i: (i, 0, 0, 0))
    rows_at = lambda i, cols: pl.BlockSpec((length, cols), lambda _: (i, 0))
    shared = (*attn_blocks, attn_order, mlp_order, plain_order, cosine, sine)
    two, two_t, keep_t, send_t, qkv, probs, mixed, gain_rows, attn_all = call(
        functools.partial(attention_forward, wide=wide),
        [
            shape((rows, plain)), shape((width, rows)), shape((width, rows)), shape((width, rows)),
            shape((rows, wide)), shape((seqs, HQ, length, length)), shape((rows, features), F32),
            shape((8, features), F32), shape((width, full)),
        ],
        grid=(seqs,),
        in_specs=[by_rows(features)] + by_once(*shared),
        out_specs=[by_rows(plain)] + [by_cols(width)] * 3
        + [by_rows(wide), by_probs, by_rows(features), once(8, features), once(width, full)],
    )(x, *shared)

    n = width // 4
    (
        alpha_send, beta_send, alpha_keep, beta_keep, down_send, down_keep, out_part, out_other, d_two_mine,
        d_two_other,
    ) = call(
        mlp_kernel,
        [shape((2, n, half_ff))] * 4 + [shape((chips // 2, fr, features))] * 2
        + [shape((rows, features), F32), shape((rows, padded)), shape((rows, plain), F32), shape((rows, plain))],
        in_specs=[in_smem] + [anywhere] * 7,
        out_specs=[anywhere] * 10,
        scratch_shapes=[
            pltpu.VMEM((2 * rows, plain), BF16), pltpu.VMEM((width, 2 * rows), BF16), pltpu.VMEM((2 * rows, padded), BF16),
            pltpu.VMEM((shards, pr, half_ff), BF16), pltpu.VMEM((shards, pr, half_ff), BF16),
            pltpu.VMEM((half_ff, padded), BF16),
            pltpu.VMEM((2 * rows, half_ff), BF16), pltpu.VMEM((2 * rows, half_ff), BF16), pltpu.VMEM((2 * rows, half_ff), BF16),
            pltpu.VMEM((4, n, half_ff), BF16), pltpu.VMEM((half_ff, features), BF16), pltpu.VMEM((rows, features), F32),
            pltpu.VMEM((rows, padded), BF16), pltpu.VMEM((rows, plain), F32), pltpu.VMEM((rows, plain), BF16),
            pltpu.SemaphoreType.DMA((15 + chips,)), pltpu.SemaphoreType.DMA((12 + chips,)),
        ],
    )(place, two, over_core(two), two_t, over_core(two_t), cot_wide, cot_oth, mlp)
    def fold(parts, n, at, deps=()):
        spec = pl.BlockSpec((n, fr, features), lambda _: (at, 0, 0))
        return call(
            functools.partial(fold_kernel, count=len(parts)), shape((n, fr, features)), grid=(1,),
            in_specs=[spec] * len(parts) + [anywhere] * len(deps), out_specs=whole(n, fr, features), vmem=ADD_VMEM,
        )(*parts, *deps)

    down_parts = [down_keep, over(down_send, 4)]

    def down_stages():
        n = chips // 2
        for flip in [4 << b for b in range(1, z_bits)] + [2]:
            n //= 2
            yield n, flip

    def down_stage(n, flip, *deps):
        sent = fold(down_parts, n, 1, deps)
        down_parts.append(over(sent, flip))
        return [sent]

    def add(alpha, beta, at, size, form, deps):
        arrays = [p[0] for p in alpha + beta]
        j, cores, _, _, n = arrays[0].shape
        one = shape((j, cores, 1, size, n))
        outs = {"apart": [one, one], "stack": shape((2,) + one.shape), "last": shape((cores, j, 2, size, n))}[form]
        specs = []
        for _, lead, f in alpha + beta:
            spot = ((0, 0, f, at // size, 0), (j, cores, None, size, n))
            if lead is not None:
                spot = ((lead,) + spot[0], (None,) + spot[1])
            specs.append(pl.BlockSpec(spot[1], functools.partial(lambda where, _: where, spot[0])))
        return call(
            functools.partial(add_kernel, n_alpha=len(alpha), count=len(arrays), form=form), outs, grid=(1,),
            in_specs=specs + [anywhere] * len(deps),
            out_specs=[whole(*o.shape) for o in outs] if form == "apart" else whole(*outs.shape),
            vmem=ADD_VMEM,
        )(*arrays, *deps)

    class Reduction:
        def __init__(self, alpha_keep, beta_keep, alpha_send, beta_send):
            self.early = [[alpha_keep, over_rep(alpha_send)], [beta_keep, over_y(beta_send)]]
            self.late = []
            self.both = []
            self.size = block

        def parts(self, f):
            return [
                [(a, None, f) for a in self.early[s]]
                + [(pair[s], None, 0) for pair in self.late] + [(a, s, 0) for a in self.both]
                for s in range(2)
            ]

        def second(self, *deps):
            alpha_sent, beta_sent = add(*self.parts(1), 0, block, "apart", deps)
            self.late.append((over_y(alpha_sent), over_rep(beta_sent)))
            return [alpha_sent, beta_sent]

        def z(self, *deps):
            self.size //= 2
            sent = add(*self.parts(0), self.size, self.size, "stack", deps)
            self.both.append(over(sent, 4 << (len(self.both))))
            return [sent]

        def last(self, *deps):
            mine = add(*self.parts(0), 0, qr, "last", deps)
            return mine, over_rep(mine)

    mlp_sum = Reduction(
        *[a.reshape(2, 2, 2, block, half_ff) for a in (alpha_keep, beta_keep, alpha_send, beta_send)]
    )

    low = wide // LANES // 8 * 8 * LANES
    arrays = (gain_rows, attn_all, attn_order)
    d_low, d_high, d_attn, grad_tokens, grad_gains = call(
        functools.partial(attention_backward, wide=wide),
        [
            shape((rows, low)), shape((rows, wide - low)), shape((rows, padded)), shape((rows, features)),
            shape((8, features), F32),
        ],
        grid=(seqs,),
        in_specs=[by_rows(plain), by_rows(plain)] + by_once(plain_order) + [by_rows(features)] * 2
        + by_once(*arrays) + [by_rows(wide), by_probs] + by_once(cosine, sine) + [by_rows(features)],
        out_specs=[by_rows(low), by_rows(wide - low), by_rows(padded), by_rows(features), whole(8, features)],
        vmem=40 << 20,
    )(d_two_mine, over_core(d_two_other), plain_order, mixed, cot, *arrays, qkv, probs, cosine, sine, x)
    down_left = list(down_stages())
    out_oth, got_t = over_core(out_other), over_core(send_t)
    sent = down_stage(*down_left.pop(0), d_low, out_oth, got_t)
    sent += mlp_sum.second(*sent)
    n = half // 4
    arrays = [d_low, d_high, d_attn]
    arrays = [
        keep_t, got_t, *arrays, *[over_core(a) for a in arrays], grad_gains, over_core(grad_gains), attn_order
    ]
    attn_grads = call(
        functools.partial(attn_grad_kernel, wide=wide, gain_at=nqkv),
        [shape((n, full))] * 4,
        grid=(1,),
        in_specs=by_once(*arrays) + [anywhere] * len(sent),
        out_specs=[whole(n, full)] * 4,
        vmem=32 << 20,
    )(*arrays, *sent)
    attn_sum = Reduction(*[a.reshape(1, 1, 2, block, full) for a in attn_grads])
    for i in range(seqs):
        output = call(
            sum_kernel, shape((rows, features)), grid=(1,),
            in_specs=[rows_at(i, features), rows_at(i, features), rows_at(i, padded)]
            + [anywhere] * (2 if i else 1),
            out_specs=rows_at(i, features), input_output_aliases={4: 0} if i else {},
        )(out_part, mixed, out_oth, attn_grads[0], *([output] if i else []))
    sent = mlp_sum.z(attn_grads[0], output)
    sent = attn_sum.second(*sent)
    for step in range(z_bits):
        if step:
            sent = mlp_sum.z(*sent)
        if down_left:
            sent = down_stage(*down_left.pop(0), *sent)
        sent = attn_sum.z(*sent)
    while down_left:
        sent = down_stage(*down_left.pop(0), *sent)
    down_mine = fold(down_parts, 1, 0, sent)
    down_from = over_rep(down_mine)
    mlp_mine, mlp_from = mlp_sum.last(down_mine)
    attn_mine, attn_from = attn_sum.last(mlp_mine)

    grad_gate, grad_up = call(
        functools.partial(shards_kernel, quarter=quarter, fr=fr),
        [shape((dr, 2 * half_ff), F32)] * 2,
        grid=(1,),
        in_specs=[in_smem] + by_once(*[mlp_mine] * 4) + [anywhere], out_specs=[whole(dr, 2 * half_ff)] * 2,
    )(place, mlp_mine, mlp_from, over_core(mlp_mine), over_core(mlp_from), down_from)
    attn_dims = ((dr, nq), (dr, nk), (dr, nk), (1, dr), (1, dr), (dr, features), (1, fr, features))
    grad_query, grad_key, grad_value, grad_gain_one, grad_gain_two, grad_out, grad_down = call(
        functools.partial(attn_shards_kernel, quarter=quarter, wide=wide),
        [shape(dims, F32) for dims in attn_dims],
        grid=(1,),
        in_specs=[in_smem] + by_once(attn_mine, attn_mine, down_mine, down_mine) + [anywhere],
        out_specs=[whole(*dims) for dims in attn_dims],
    )(place, attn_mine, attn_from, down_mine, down_from, grad_gate)
    dims = tokens.shape
    return (
        output.reshape(dims), grad_tokens.reshape(dims), grad_gain_one.reshape(dr), grad_query, grad_key, grad_value,
        grad_out, grad_gain_two.reshape(dr), grad_gate, grad_up, grad_down[0],
    )


def solution(mesh):
    data = P(None, ("rep", "shard"), None, None)
    vector, matrix = P("shard"), P("shard", None)
    weights = (vector, matrix, matrix, matrix, matrix, vector, matrix, matrix, matrix)
    return jax.shard_map(
        on_device,
        mesh=mesh,
        in_specs=(data, data) + weights,
        out_specs=(data, data) + weights,
        check_vma=False,
    )
```

```python
import functools
import math

import jax
import jax.numpy as jnp
import numpy as np
from jax import lax
from jax.experimental import pallas as pl
from jax.experimental.pallas import tpu as pltpu
from jax.sharding import PartitionSpec as P

HQ = 15
KV = 5
HD = 64
EPSILON = 1e-05
THETA = 100000.0
F32 = jnp.float32
BF16 = jnp.bfloat16
LANES = 128
COLS = 256
NN = ((1,), (0,))
NT = ((1,), (1,))
TN = ((0,), (0,))
VMEM = 60 << 20
ADD_VMEM = 16 << 20


def dot(a, b, contract=NN):
    return lax.dot_general(a, b, (contract, ((), ())), preferred_element_type=F32)


def call(kernel, out_shape, *, vmem=VMEM, **how):
    return pl.pallas_call(
        kernel,
        out_shape=out_shape,
        compiler_params=pltpu.CompilerParams(vmem_limit_bytes=vmem),
        cost_estimate=pl.CostEstimate(flops=1 << 20, bytes_accessed=1 << 12, transcendentals=0),
        **how,
    )


def shape(dims, dtype=BF16):
    return jax.ShapeDtypeStruct(dims, dtype)


def whole(*dims):
    return pl.BlockSpec(dims, lambda *_: (0,) * len(dims))


def once(*dims):
    return pl.BlockSpec(dims, lambda *_: (0,) * len(dims), pipeline_mode=pl.Buffered(1))


def tables(length):
    frequency = THETA ** (-2.0 * np.arange(HD // 2, dtype=np.float32) / HD)
    angles = np.arange(length, dtype=np.float32)[:, None] * frequency.astype(np.float32)[None, :]
    cosine, sine = np.cos(angles), np.sin(angles)
    return np.tile(cosine, (1, 4)), np.concatenate([-sine, sine, -sine, sine], axis=1)


def turn(tile, cosine, sine, low):
    other = jnp.where(low, pltpu.roll(tile, LANES - 32, 1), pltpu.roll(tile, 32, 1))
    return tile * cosine + other * sine


def placed(tile, half):
    lane = lax.broadcasted_iota(jnp.int32, tile.shape, 1)
    alone = jnp.where((lane >= HD) == (half == 1), tile, 0.0)
    moved = pltpu.roll(alone, HD, 1)
    pair = (moved, alone) if half else (alone, moved)
    return [one.astype(BF16) for one in pair]


def placed_turned(tile, half):
    tile = tile.T
    row = lax.broadcasted_iota(jnp.int32, tile.shape, 0)
    alone = jnp.where((row >= HD) == (half == 1), tile, 0.0)
    moved = jnp.concatenate([alone[HD:], alone[:HD]], axis=0)
    pair = (moved, alone) if half else (alone, moved)
    return [one.astype(BF16) for one in pair]


def attention_forward(x_ref, *refs, wide):
    blocks, (attn_order_ref, mlp_order_ref, plain_order_ref, cos_ref, sin_ref) = refs[:8], refs[8:13]
    two_ref, two_t_ref, keep_ref, send_ref, qkv_ref, probs_ref, mixed_ref, gain_ref, all_ref = refs[13:]

    @pl.when(pl.program_id(0) == 0)
    def _():
        n = all_ref.shape[0] // 16
        for c in range(2):
            near, over_y, over_x, over_both = blocks[4 * c : 4 * c + 4]
            pairs = ((near, over_y), (near, over_x), (over_x, over_both), (over_y, over_both))
            for i, pair in enumerate(pairs):
                for k, ref in enumerate(pair):
                    at = (8 * c + 2 * i + k) * n
                    all_ref[at : at + n, :] = ref[i % 2]

    length, features = x_ref.shape
    half = all_ref.shape[0] // 2
    to_order = attn_order_ref[:, :features]
    last = slice(wide - LANES, wide)
    gains = dot(all_ref[:, last], to_order, TN)
    gain_one, gain_two = gains[HD : HD + 1], gains[HD + 1 : HD + 2]
    gain_ref[...] = gains[HD : HD + 8]
    x = x_ref[...].astype(F32)
    r1 = lax.rsqrt(jnp.mean(x * x, axis=-1, keepdims=True) + EPSILON)
    normed = (x * r1 * gain_one).astype(BF16)
    spread = dot(normed, to_order, NT).astype(BF16)
    turned = dot(to_order, normed, NT).astype(BF16)
    keep_ref[:half, :] = turned[:half]
    send_ref[:half, :] = turned[half:]
    lane = lax.broadcasted_iota(jnp.int32, (length, LANES), 1)
    low = lane % HD < HD // 2
    cosine, sine = cos_ref[...], sin_ref[...]
    tiles, heads = [], {}
    for t in range(wide // LANES):
        cols = slice(t * LANES, (t + 1) * LANES)
        tile = dot(spread, all_ref[:, cols])
        if t * 2 < HQ + KV:
            tile = turn(tile, cosine, sine, low)
        if t == wide // LANES - 1:
            tile = jnp.where(lane < HD, tile, 0.0)
        short = tile.astype(BF16)
        qkv_ref[:, cols] = short
        tiles.append(short)
        for n in (2 * t, 2 * t + 1):
            if HQ <= n < HQ + KV:
                heads[n] = placed(tile, n % 2)
            elif HQ + KV <= n < HQ + 2 * KV:
                heads[n] = placed_turned(tile, n % 2)
    causal = lax.broadcasted_iota(jnp.int32, (length, length), 0) <= lax.broadcasted_iota(
        jnp.int32, (length, length), 1
    )
    context = [None] * ((HQ + 1) // 2)
    for h in range(HQ):
        j, t, s = h // (HQ // KV), h // 2, h % 2
        scores = dot(heads[HQ + j][s], tiles[t], NT) * (1.0 / math.sqrt(HD))
        scores = jnp.where(causal, scores, -1e30)
        exponent = jnp.exp(scores - jnp.max(scores, axis=0, keepdims=True))
        probs = exponent * (1.0 / jnp.sum(exponent, axis=0, keepdims=True))
        probs = probs.astype(BF16)
        probs_ref[0, h] = probs
        part = dot(heads[HQ + KV + j][s], probs)
        context[t] = part if context[t] is None else context[t] + part
    context = jnp.concatenate([c.astype(BF16) for c in context], axis=0)
    turned = dot(attn_order_ref[...], context).astype(BF16)
    mixed = x + dot(turned, all_ref[:, wide : wide + features], TN)
    keep_ref[half:, :] = turned[:half]
    send_ref[half:, :] = turned[half:]
    mixed_ref[...] = mixed
    r2 = lax.rsqrt(jnp.mean(mixed * mixed, axis=-1, keepdims=True) + EPSILON)
    two = (mixed * r2 * gain_two).astype(BF16)
    two_ref[...] = dot(two, plain_order_ref[:, :features], NT).astype(BF16)
    two_t_ref[...] = dot(mlp_order_ref[:, :features], two, NT).astype(BF16)


def attention_backward(
    mine_ref, other_ref, plain_order_ref, mixed_ref, cot_ref, gain_ref, all_ref, order_ref, qkv_ref,
    probs_ref, cos_ref, sin_ref, x_ref, d_low_ref, d_high_ref, d_attn_ref, out_ref, grad_ref, *, wide
):
    length, features = mixed_ref.shape
    total = (mine_ref[...] + other_ref[...].astype(F32)).astype(BF16)
    d_two = dot(total, plain_order_ref[:, :features])
    mixed = mixed_ref[...]
    r2 = lax.rsqrt(jnp.mean(mixed * mixed, axis=-1, keepdims=True) + EPSILON)
    unit = mixed * r2
    e2 = d_two * gain_ref[1:2, :]
    d_mixed = cot_ref[...].astype(F32) + r2 * (e2 - unit * jnp.mean(e2 * unit, axis=-1, keepdims=True))
    d_attn = d_mixed.astype(BF16)
    d_attn_ref[:, :features] = d_attn
    d_attn_ref[:, features:] = jnp.zeros((length, d_attn_ref.shape[1] - features), BF16)
    grad_gain_two = jnp.sum(d_two * unit, axis=0, keepdims=True)
    d_context = dot(d_attn, all_ref[:, wide : wide + features], NT).astype(BF16)
    d_context = dot(d_context, order_ref[...]).astype(BF16)
    lane = lax.broadcasted_iota(jnp.int32, (length, LANES), 1)
    low = lane % HD < HD // 2
    cosine, sine = cos_ref[...], -sin_ref[...]

    def tile_of(n):
        t = n // 2
        return qkv_ref[:, t * LANES : (t + 1) * LANES]

    d_tiles = [None] * ((HQ + 2 * KV + 1) // 2)

    def add(t, part):
        d_tiles[t] = part if d_tiles[t] is None else d_tiles[t] + part

    groups = HQ // KV
    d_query = [None] * ((HQ + 1) // 2)
    for j in range(KV):
        keys = placed_turned(tile_of(HQ + j).astype(F32), (HQ + j) % 2)
        values = placed(tile_of(HQ + KV + j).astype(F32), (HQ + KV + j) % 2)
        d_key, d_value = [None, None], [None, None]
        for h in range(j * groups, (j + 1) * groups):
            t, s = h // 2, h % 2
            d_con = d_context[:, t * LANES : (t + 1) * LANES]
            probs = probs_ref[0, h]
            wide_probs = probs.astype(F32)
            d_probs = dot(values[s], d_con, NT)
            inner = jnp.sum(d_probs * wide_probs, axis=0, keepdims=True)
            d_scores = (wide_probs * (d_probs - inner) * (1.0 / math.sqrt(HD))).astype(BF16)
            part = dot(keys[s], d_scores)
            d_query[t] = part if d_query[t] is None else d_query[t] + part
            part = dot(d_scores, tile_of(h))
            d_key[s] = part if d_key[s] is None else d_key[s] + part
            part = dot(probs, d_con)
            d_value[s] = part if d_value[s] is None else d_value[s] + part
        for n, pair in ((HQ + j, d_key), (HQ + KV + j, d_value)):
            here = n % 2
            mask = (lane >= HD) == (here == 1)
            total = jnp.where(mask, pair[here] + pltpu.roll(pair[1 - here], HD, 1), 0.0)
            add(n // 2, total)
    for t, tile in enumerate(d_query):
        add(t, tile.T)
    for t, tile in enumerate(d_tiles):
        if t * 2 < HQ + KV:
            tile = turn(tile, cosine, sine, low)
        ref, at = (d_low_ref, t * LANES) if t * LANES < d_low_ref.shape[1] else (d_high_ref, t * LANES - d_low_ref.shape[1])
        ref[:, at : at + LANES] = tile.astype(BF16)
    split = d_low_ref.shape[1]
    d_normed = dot(d_low_ref[...], all_ref[:, :split], NT) + dot(d_high_ref[...], all_ref[:, split:wide], NT)
    d_normed = d_normed.astype(BF16)
    d_normed = dot(d_normed, order_ref[:, :features])
    x = x_ref[...].astype(F32)
    r1 = lax.rsqrt(jnp.mean(x * x, axis=-1, keepdims=True) + EPSILON)
    unit = x * r1
    e1 = d_normed * gain_ref[0:1, :]
    out = d_mixed + r1 * (e1 - unit * jnp.mean(e1 * unit, axis=-1, keepdims=True))
    out_ref[...] = out.astype(BF16)
    grad_gain_one = jnp.sum(d_normed * unit, axis=0, keepdims=True)
    grads = jnp.concatenate([grad_gain_one, grad_gain_two, jnp.zeros((6, features), F32)], axis=0)


    @pl.when(pl.program_id(0) == 0)
    def _():
        grad_ref[...] = grads

    @pl.when(pl.program_id(0) > 0)
    def _():
        grad_ref[...] += grads


def flipped(array, axis, block):
    n = array.shape[axis] // block
    parts = [lax.slice_in_dim(array, i * block, (i + 1) * block, axis=axis) for i in range(n)]
    return jnp.concatenate([parts[i ^ 1] for i in range(n)], axis=axis)


def row_quarters(w, quarter, qr):
    dr, n = w.shape
    parts = []
    for q in range(4):
        part = w[min(q * quarter, dr) : min((q + 1) * quarter, dr), :]
        parts.append(jnp.concatenate([part, jnp.zeros((qr - part.shape[0], n), F32)], axis=0))
    return parts


def pieces_kernel(
    place_ref, wq_ref, wk_ref, wv_ref, wo_ref, g1_ref, g2_ref, wg_ref, wu_ref, wd_ref, attn_ref, mlp_ref,
    *, quarter, qr, pr, fr, wide
):
    rep, dr = place_ref[1], wq_ref.shape[0]

    def store(at, w):
        parts = row_quarters(w, quarter, qr)
        for s in range(2):
            attn_ref[s, :, at : at + w.shape[1]] = jnp.where(rep == 0, parts[s], parts[2 + s]).astype(BF16)

    wide_of = lambda ref: ref[...].astype(F32)
    eye = (
        lax.broadcasted_iota(jnp.int32, (dr, dr), 0) == lax.broadcasted_iota(jnp.int32, (dr, dr), 1)
    ).astype(F32)
    columns = [jnp.sum(eye * wide_of(ref), axis=1, keepdims=True) for ref in (g1_ref, g2_ref)]
    blank = jnp.zeros((dr, wide - wq_ref.shape[1] - 2 * wk_ref.shape[1] - 2), F32)
    store(0, jnp.concatenate([wide_of(wq_ref), wide_of(wk_ref), wide_of(wv_ref)] + columns + [blank], axis=1))
    w = wide_of(wo_ref)
    store(wide, jnp.concatenate([w, jnp.zeros((dr, attn_ref.shape[2] - wide - w.shape[1]), F32)], axis=1))
    halves = []
    for ref in (wg_ref, wu_ref):
        w = wide_of(ref)
        chunks = [w[:, i * fr : (i + 1) * fr] for i in range(w.shape[1] // fr)]
        halves.append([jnp.concatenate(chunks[c::2], axis=1) for c in range(2)])
    row = jnp.concatenate([halves[0][0], halves[1][0], halves[0][1], halves[1][1]], axis=1)
    rows, lanes = pr, mlp_ref.shape[1]
    row = jnp.concatenate([row, jnp.zeros((rows - dr, row.shape[1]), F32)], axis=0).astype(BF16)
    for g in range(4):
        mlp_ref[g * rows : (g + 1) * rows, :] = row[:, g * lanes : (g + 1) * lanes]
    at, n = 4 * rows, wd_ref.shape[1]
    mlp_ref[at : at + fr, :n] = wd_ref[...]
    mlp_ref[at : at + fr, n:] = jnp.zeros((fr, lanes - n), BF16)
    if at + fr < mlp_ref.shape[0]:
        mlp_ref[at + fr :, :] = jnp.zeros((mlp_ref.shape[0] - at - fr, lanes), BF16)


def tie_kernel(*refs):
    del refs


def add_kernel(*refs, n_alpha, count, form):
    totals = [ref[...].astype(F32) for ref in refs[:count]]
    alpha, beta = functools.reduce(jnp.add, totals[:n_alpha]), functools.reduce(jnp.add, totals[n_alpha:])
    if form == "apart":
        refs[-2][:, :, 0] = alpha.astype(BF16)
        refs[-1][:, :, 0] = beta.astype(BF16)
    elif form == "stack":
        refs[-1][0, :, :, 0] = alpha.astype(BF16)
        refs[-1][1, :, :, 0] = beta.astype(BF16)
    else:
        for c in range(alpha.shape[1]):
            refs[-1][c, :, 0] = alpha[:, c].astype(BF16)
            refs[-1][c, :, 1] = beta[:, c].astype(BF16)


def shards_kernel(place_ref, mine_ref, other_ref, got_ref, got_other_ref, gate_ref, up_ref, *, quarter, fr):
    core, rep = place_ref[0], place_ref[1]
    dr = gate_ref.shape[0]
    for at, out_ref in ((0, gate_ref), (1, up_ref)):
        sides = []
        for c, mine, other in ((0, mine_ref, other_ref), (1, got_ref, got_other_ref)):
            a, b = mine[c, at].astype(F32), other[c, at].astype(F32)
            low, high = jnp.where(rep == 0, a, b), jnp.where(rep == 0, b, a)
            rows = [half[s][:quarter] for half in (low, high) for s in range(2)]
            sides.append(jnp.concatenate(rows, axis=0)[:dr])
        even, odd = jnp.where(core == 0, sides[0], sides[1]), jnp.where(core == 0, sides[1], sides[0])
        chunks = []
        for k in range(even.shape[1] // fr):
            chunks += [even[:, k * fr : (k + 1) * fr], odd[:, k * fr : (k + 1) * fr]]
        out_ref[...] = jnp.concatenate(chunks, axis=1)


def attn_shards_kernel(place_ref, mine_ref, other_ref, *refs, quarter, wide):
    query_ref, key_ref, value_ref, *gain_refs, out_ref = refs[-6:]
    rep, dr = place_ref[1], out_ref.shape[0]
    a, b = mine_ref[0, 0].astype(F32), other_ref[0, 0].astype(F32)
    low, high = jnp.where(rep == 0, a, b), jnp.where(rep == 0, b, a)
    rows = jnp.concatenate([half[s][:quarter] for half in (low, high) for s in range(2)], axis=0)[:dr]
    at = 0
    for ref in (query_ref, key_ref, value_ref):
        ref[...] = rows[:, at : at + ref.shape[1]]
        at += ref.shape[1]
    out_ref[...] = rows[:, wide : wide + out_ref.shape[1]]
    eye = lax.broadcasted_iota(jnp.int32, (dr, dr), 0) == lax.broadcasted_iota(jnp.int32, (dr, dr), 1)
    for i, ref in enumerate(gain_refs):
        ref[...] = jnp.sum(jnp.where(eye, rows[:, at + i : at + i + 1], 0.0), axis=0, keepdims=True)


def order_kernel(*refs):
    for feat_ref, out_ref in zip(refs[:3], refs[3:]):
        column = lax.broadcasted_iota(jnp.int32, out_ref.shape, 1)
        out_ref[...] = (feat_ref[...] == column).astype(F32).astype(BF16)


def copy_kernel(in_ref, *refs):
    out_ref, n = refs[-1], in_ref.shape[1]
    out_ref[:, :n] = in_ref[...]
    out_ref[:, n:] = jnp.zeros((out_ref.shape[0], out_ref.shape[1] - n), BF16)


def sum_kernel(*refs):
    n = refs[-1].shape[1]
    refs[-1][...] = functools.reduce(jnp.add, [r[:, :n].astype(F32) for r in (refs[:3] if len(refs) > 3 else refs[:-1])]).astype(refs[-1].dtype)


def split_attn_kernel(*refs, count):
    rows = refs[0].shape[1]
    for i, ref in enumerate(refs[:count]):
        for s in range(2):
            refs[-1][s, i * rows : (i + 1) * rows, :] = ref[s]


def join_kernel(near_ref, y_ref, x_ref, xy_ref, out_ref):
    rows = near_ref.shape[1]
    blocks = ((near_ref, y_ref), (near_ref, x_ref), (x_ref, xy_ref), (y_ref, xy_ref))
    for i, pair in enumerate(blocks):
        for k, ref in enumerate(pair):
            at = (2 * i + k) * rows
            out_ref[at : at + rows, :] = ref[i % 2]


def attn_grad_kernel(keep_ref, got_ref, *refs, wide, gain_at):
    mine, other = refs[:3], refs[3:6]
    gains_ref, gains_oth_ref, order_ref = refs[6:9]
    out_refs = refs[-4:]
    half, features = keep_ref.shape[0] // 2, gains_ref.shape[1]
    n = out_refs[0].shape[0]
    gains = (gains_ref[...] + gains_oth_ref[...]).astype(BF16)
    gains = dot(order_ref[:half, :features], gains, NT)
    lane = lax.broadcasted_iota(jnp.int32, (half, LANES), 1) + (wide - LANES)
    tile = jnp.where(lane == gain_at, gains[:, 0:1], 0.0) + jnp.where(lane == gain_at + 1, gains[:, 1:2], 0.0)
    column = 0
    for k in range(3):
        at = slice(half, 2 * half) if k == 2 else slice(0, half)
        grad = dot(keep_ref[at, :], mine[k][...]) + dot(got_ref[at, :], other[k][...])
        if k == 1:
            grad = jnp.concatenate([grad[:, :-LANES], grad[:, -LANES:] + tile], axis=1)
        for i, ref in enumerate(out_refs):
            ref[:, column : column + grad.shape[1]] = grad[i * n : (i + 1) * n].astype(BF16)
        column += grad.shape[1]


def chip_flips(chips):
    bits = (chips // 2).bit_length() - 1
    z = [sum(((i >> b) & 1) << (bits - 1 - b) for b in range(bits)) for i in range(chips // 2)]
    return [2 * flip + y for flip in z for y in range(2)]


def fold_kernel(*refs, count):
    refs[-1][...] = functools.reduce(jnp.add, [r[...].astype(F32) for r in refs[:count]]).astype(refs[-1].dtype)


def mlp_kernel(place_ref, two_ref, two_oth_ref, t_ref, t_oth_ref, cot_ref, cot_oth_ref, w_ref, *refs):
    sends, keeps = refs[:2], refs[2:4]
    downs, (out_ref, out_oth_ref, d_two_ref, d_two_oth_ref) = refs[4:6], refs[6:10]
    acts, acts_t, cots, wg, wu, wd, hidden, d_gate, d_up = refs[10:19]
    chunks, down, out, out_oth, d_two, d_two_oth, in_sems, out_sems = refs[19:]
    rows = cot_ref.shape[0]
    width, half_ff, features = acts_t.shape[0], hidden.shape[1], down.shape[1]
    shards, pr = wg.shape[0], wg.shape[1]
    fr, plain, n, block = 2 * half_ff // shards, shards * pr, width // 4, width // 8
    core = place_ref[0]
    started = []

    def fetch(source, target):
        copy = pltpu.make_async_copy(source, target, in_sems.at[len(started)])
        copy.start()
        started.append(copy)
        return copy

    first = [fetch(two_ref, acts.at[pl.ds(0, rows), :])]
    gate_in = fetch(w_ref.at[:, pl.ds(2 * pr * core, pr), :], wg)
    up_in = fetch(w_ref.at[:, pl.ds(2 * pr * core + pr, pr), :], wu)
    cots_in = [fetch(cot_ref, cots.at[pl.ds(0, rows), :])]
    down_in = [
        fetch(
            w_ref.at[2 * k + core, pl.ds(4 * pr, fr), pl.ds(0, wd.shape[1])], wd.at[pl.ds(k * fr, fr), :]
        )
        for k in range(shards // 2)
    ]
    second = [fetch(two_oth_ref, acts.at[pl.ds(rows, rows), :]), fetch(cot_oth_ref, cots.at[pl.ds(rows, rows), :])]
    turned = [fetch(t_ref, acts_t.at[:, pl.ds(0, rows)])]
    for k in range(8):
        source = t_oth_ref.at[pl.ds((k ^ 1) * block, block), :]
        turned.append(fetch(source, acts_t.at[pl.ds(k * block, block), pl.ds(rows, rows)]))

    def wait(copies):
        for copy in copies:
            copy.wait()

    for half in range(2):
        at = slice(half * rows, (half + 1) * rows)
        wait(second if half else first + [gate_in])
        gate = dot(acts[at, :], wg[...].reshape(plain, half_ff))
        if not half:
            wait([up_in])
        up = dot(acts[at, :], wu[...].reshape(plain, half_ff))
        sg = 1.0 / (1.0 + jnp.exp(-gate))
        silu = gate * sg
        hidden[at, :] = (silu * up).astype(BF16)
        if not half:
            wait(cots_in + down_in)
        d_hidden = dot(cots[at, :], wd[...], NT)
        d_gate[at, :] = (d_hidden * up * sg * (1.0 + gate * (1.0 - sg))).astype(BF16)
        d_up[at, :] = (d_hidden * silu).astype(BF16)
    wait(turned)

    going = []

    def put(source, target):
        copy = pltpu.make_async_copy(source, target, out_sems.at[len(going)])
        copy.start()
        going.append(copy)

    for targets, first_row in ((sends, 2 * n), (keeps, 0)):
        for i, d in ((0, d_gate), (1, d_up)):
            grad = dot(acts_t[first_row : first_row + 2 * n, :], d[...])
            for k in range(2):
                slot = len(going) % chunks.shape[0]
                if len(going) >= chunks.shape[0]:
                    going[len(going) - chunks.shape[0]].wait()
                chunks[slot] = grad[k * n : (k + 1) * n].astype(BF16)
                put(chunks.at[slot], targets[k].at[i])
    count = len(going)
    down[...] = dot(hidden[...], cots[:, :features], TN).astype(BF16)
    chips = shards // 2
    for k, flip in enumerate(chip_flips(chips)):
        source = pl.multiple_of((place_ref[2] ^ flip) * fr, fr)
        put(down.at[pl.ds(source, fr), :], downs[1 - 2 * k // chips].at[k % (chips // 2)])

    def back(at):
        return dot(d_gate[at, :], wg[...].reshape(plain, half_ff), NT) + dot(
            d_up[at, :], wu[...].reshape(plain, half_ff), NT
        )

    d_two[...] = back(slice(0, rows))
    put(d_two, d_two_ref)
    out[...] = dot(hidden[:rows, :], wd[:, :features])
    put(out, out_ref)
    d_two_oth[...] = back(slice(rows, 2 * rows)).astype(BF16)
    put(d_two_oth, d_two_oth_ref)
    out_oth[...] = dot(hidden[rows:, :], wd[...]).astype(BF16)
    put(out_oth, out_oth_ref)
    wait(going[count - chunks.shape[0] :])


def on_device(
    tokens, cotangent, attn_gain, w_query, w_key, w_value, w_out, mlp_gain, w_gate, w_up, w_down
):
    shards = lax.axis_size("shard")
    chips = shards // 2
    zs = chips // 2
    me, rep = lax.axis_index("shard"), lax.axis_index("rep")
    core = me % 2
    micro, batch, length, features = tokens.shape
    seqs = micro * batch
    rows = seqs * length
    dr = features // shards
    quarter = -(-dr // 4)
    qr = -(-quarter // 8) * 8
    pr = -(-dr // 16) * 16
    plain = shards * pr
    width = shards * 4 * qr
    half = width // 2
    block = zs * qr
    fr = w_down.shape[0]
    half_ff = chips * fr
    nq, nk = HQ * HD, KV * HD
    nqkv = nq + 2 * nk
    wide = -(-(nqkv + 2) // LANES) * LANES
    padded = -(-features // LANES) * LANES
    full = wide + padded
    cosine, sine = (jnp.asarray(t) for t in tables(length))
    place = jnp.stack([core, rep, me // 2]).astype(jnp.int32)
    in_smem = pl.BlockSpec(memory_space=pltpu.SMEM)
    in_vmem = pl.BlockSpec(memory_space=pltpu.VMEM)
    anywhere = pl.BlockSpec(memory_space=pl.ANY)
    z_bits = zs.bit_length() - 1
    z_flip = np.array([sum(((i >> b) & 1) << (z_bits - 1 - b) for b in range(z_bits)) for i in range(zs)])

    def over(array, flip):
        return lax.ppermute(array, "shard", [(s, s ^ flip) for s in range(shards)])

    def over_core(array):
        return over(array, 1)

    def over_y(array):
        return over(array, 2)

    def over_rep(array):
        return lax.ppermute(array, "rep", [(0, 1), (1, 0)])

    def tie(arrays, *deps):
        return call(
            tie_kernel, [shape(a.shape, a.dtype) for a in arrays],
            in_specs=[anywhere] * (len(arrays) + len(deps)), out_specs=[anywhere] * len(arrays),
            input_output_aliases={i: i for i in range(len(arrays))},
        )(*arrays, *deps)

    def small(kernel, outs, arrays, deps=()):
        return call(
            kernel, outs, in_specs=[in_vmem] * len(arrays) + [anywhere] * len(deps), vmem=16 << 20
        )(*arrays, *deps)


    def feature_of(dims):
        sizes = {"core": 2, "split": 2, "f1": 2, "f2": 2, "z": zs, "row": qr}
        grid = np.meshgrid(*[np.arange(sizes[d]) for d in dims], indexing="ij")
        at = {d: g.reshape(-1) for d, g in zip(dims, grid)}
        x_flip = np.where(at["split"] == 0, at["f1"], at["f2"])
        y_flip = np.where(at["split"] == 0, at["f2"], at["f1"])
        shard = me ^ jnp.asarray(at["core"] + 2 * (y_flip + 2 * z_flip[at["z"]]), jnp.int32)
        part = 2 * (rep ^ jnp.asarray(x_flip, jnp.int32)) + jnp.asarray(at["split"], jnp.int32)
        inside = part * quarter + jnp.asarray(at["row"], jnp.int32)
        real = jnp.asarray(at["row"] < quarter) & (inside < dr)
        return jnp.where(real, shard * dr + inside, -1)[:, None]

    feats = [feature_of(("core", "f1", "split", "f2", "z", "row")), feature_of(("f1", "split", "core", "f2", "z", "row"))]
    shard, row = np.repeat(np.arange(shards), pr), np.tile(np.arange(pr), shards)
    feats.append(jnp.asarray(np.where(row < dr, shard * dr + row, -1)[:, None], jnp.int32))
    attn_order, mlp_order, plain_order = call(
        order_kernel, [shape((f.shape[0], padded)) for f in feats], grid=(1,), in_specs=[in_vmem] * 3,
        out_specs=[whole(f.shape[0], padded) for f in feats],
    )(*feats)

    floor = (16 << 20) // (2 * half_ff * shards) + 1
    depth = -(-max(4 * pr + fr, floor) // 16) * 16
    attn_piece, mlp_piece = call(
        functools.partial(pieces_kernel, quarter=quarter, qr=qr, pr=pr, fr=fr, wide=wide),
        [shape((2, qr, full)), shape((depth, half_ff))],
        grid=(1,),
        in_specs=[in_smem] + [
            whole(*w.shape)
            for w in (w_query, w_key, w_value, w_out, attn_gain[None], mlp_gain[None], w_gate, w_up, w_down)
        ],
        out_specs=[in_vmem, whole(depth, half_ff)],
    )(place, w_query, w_key, w_value, w_out, attn_gain[None], mlp_gain[None], w_gate, w_up, w_down)
    mlp = lax.all_gather(mlp_piece, "shard", axis=0, tiled=True).reshape(shards, depth, half_ff)
    parts = [attn_piece if z == 0 else over(attn_piece, 4 * z) for z in z_flip]
    x = tokens.reshape(rows, features)
    cot = cotangent.reshape(rows, features)
    cot_wide = small(copy_kernel, shape((rows, padded)), [cot], [attn_piece])
    cot_oth = over_core(cot_wide)
    attn_near = small(
        functools.partial(split_attn_kernel, count=zs), shape((2, block, full)), parts, [cot_oth, x, attn_order]
    )
    attn_y, attn_x = over_y(attn_near), over_rep(attn_near)
    attn_blocks = [attn_near, attn_y, attn_x, over_rep(attn_y)]
    attn_blocks += [over_core(b) for b in attn_blocks]

    by_rows = lambda cols: pl.BlockSpec((length, cols), lambda i: (i, 0))
    by_cols = lambda n: pl.BlockSpec((n, length), lambda i: (0, i))
    by_once = lambda *arrays: [once(*a.shape) for a in arrays]
    by_probs = pl.BlockSpec((1, HQ, length, length), lambda i: (i, 0, 0, 0))
    rows_at = lambda i, cols: pl.BlockSpec((length, cols), lambda _: (i, 0))
    shared = (*attn_blocks, attn_order, mlp_order, plain_order, cosine, sine)
    two, two_t, keep_t, send_t, qkv, probs, mixed, gain_rows, attn_all = call(
        functools.partial(attention_forward, wide=wide),
        [
            shape((rows, plain)), shape((width, rows)), shape((width, rows)), shape((width, rows)),
            shape((rows, wide)), shape((seqs, HQ, length, length)), shape((rows, features), F32),
            shape((8, features), F32), shape((width, full)),
        ],
        grid=(seqs,),
        in_specs=[by_rows(features)] + by_once(*shared),
        out_specs=[by_rows(plain)] + [by_cols(width)] * 3
        + [by_rows(wide), by_probs, by_rows(features), once(8, features), once(width, full)],
    )(x, *shared)

    n = width // 4
    (
        alpha_send, beta_send, alpha_keep, beta_keep, down_send, down_keep, out_part, out_other, d_two_mine,
        d_two_other,
    ) = call(
        mlp_kernel,
        [shape((2, n, half_ff))] * 4 + [shape((chips // 2, fr, features))] * 2
        + [shape((rows, features), F32), shape((rows, padded)), shape((rows, plain), F32), shape((rows, plain))],
        in_specs=[in_smem] + [anywhere] * 7,
        out_specs=[anywhere] * 10,
        scratch_shapes=[
            pltpu.VMEM((2 * rows, plain), BF16), pltpu.VMEM((width, 2 * rows), BF16), pltpu.VMEM((2 * rows, padded), BF16),
            pltpu.VMEM((shards, pr, half_ff), BF16), pltpu.VMEM((shards, pr, half_ff), BF16),
            pltpu.VMEM((half_ff, padded), BF16),
            pltpu.VMEM((2 * rows, half_ff), BF16), pltpu.VMEM((2 * rows, half_ff), BF16), pltpu.VMEM((2 * rows, half_ff), BF16),
            pltpu.VMEM((4, n, half_ff), BF16), pltpu.VMEM((half_ff, features), BF16), pltpu.VMEM((rows, features), F32),
            pltpu.VMEM((rows, padded), BF16), pltpu.VMEM((rows, plain), F32), pltpu.VMEM((rows, plain), BF16),
            pltpu.SemaphoreType.DMA((15 + chips,)), pltpu.SemaphoreType.DMA((12 + chips,)),
        ],
    )(place, two, over_core(two), two_t, over_core(two_t), cot_wide, cot_oth, mlp)
    def fold(parts, n, at, deps=()):
        spec = pl.BlockSpec((n, fr, features), lambda _: (at, 0, 0))
        return call(
            functools.partial(fold_kernel, count=len(parts)), shape((n, fr, features)), grid=(1,),
            in_specs=[spec] * len(parts) + [anywhere] * len(deps), out_specs=whole(n, fr, features), vmem=ADD_VMEM,
        )(*parts, *deps)

    down_parts = [down_keep, over(down_send, 4)]

    def down_stages():
        n = chips // 2
        for flip in [4 << b for b in range(1, z_bits)] + [2]:
            n //= 2
            yield n, flip

    def down_stage(n, flip, *deps):
        sent = fold(down_parts, n, 1, deps)
        down_parts.append(over(sent, flip))
        return [sent]

    def add(alpha, beta, at, size, form, deps):
        arrays = [p[0] for p in alpha + beta]
        j, cores, _, _, n = arrays[0].shape
        one = shape((j, cores, 1, size, n))
        outs = {"apart": [one, one], "stack": shape((2,) + one.shape), "last": shape((cores, j, 2, size, n))}[form]
        specs = []
        for _, lead, f in alpha + beta:
            spot = ((0, 0, f, at // size, 0), (j, cores, None, size, n))
            if lead is not None:
                spot = ((lead,) + spot[0], (None,) + spot[1])
            specs.append(pl.BlockSpec(spot[1], functools.partial(lambda where, _: where, spot[0])))
        return call(
            functools.partial(add_kernel, n_alpha=len(alpha), count=len(arrays), form=form), outs, grid=(1,),
            in_specs=specs + [anywhere] * len(deps),
            out_specs=[whole(*o.shape) for o in outs] if form == "apart" else whole(*outs.shape),
            vmem=ADD_VMEM,
        )(*arrays, *deps)

    class Reduction:
        def __init__(self, alpha_keep, beta_keep, alpha_send, beta_send):
            self.early = [[alpha_keep, over_rep(alpha_send)], [beta_keep, over_y(beta_send)]]
            self.late = []
            self.both = []
            self.size = block

        def parts(self, f):
            return [
                [(a, None, f) for a in self.early[s]]
                + [(pair[s], None, 0) for pair in self.late] + [(a, s, 0) for a in self.both]
                for s in range(2)
            ]

        def second(self, *deps):
            alpha_sent, beta_sent = add(*self.parts(1), 0, block, "apart", deps)
            self.late.append((over_y(alpha_sent), over_rep(beta_sent)))
            return [alpha_sent, beta_sent]

        def z(self, *deps):
            self.size //= 2
            sent = add(*self.parts(0), self.size, self.size, "stack", deps)
            self.both.append(over(sent, 4 << (len(self.both))))
            return [sent]

        def last(self, *deps):
            mine = add(*self.parts(0), 0, qr, "last", deps)
            return mine, over_rep(mine)

    mlp_sum = Reduction(
        *[a.reshape(2, 2, 2, block, half_ff) for a in (alpha_keep, beta_keep, alpha_send, beta_send)]
    )

    low = wide // LANES // 8 * 8 * LANES
    arrays = (gain_rows, attn_all, attn_order)
    d_low, d_high, d_attn, grad_tokens, grad_gains = call(
        functools.partial(attention_backward, wide=wide),
        [
            shape((rows, low)), shape((rows, wide - low)), shape((rows, padded)), shape((rows, features)),
            shape((8, features), F32),
        ],
        grid=(seqs,),
        in_specs=[by_rows(plain), by_rows(plain)] + by_once(plain_order) + [by_rows(features)] * 2
        + by_once(*arrays) + [by_rows(wide), by_probs] + by_once(cosine, sine) + [by_rows(features)],
        out_specs=[by_rows(low), by_rows(wide - low), by_rows(padded), by_rows(features), whole(8, features)],
        vmem=44 << 20,
    )(d_two_mine, over_core(d_two_other), plain_order, mixed, cot, *arrays, qkv, probs, cosine, sine, x)
    down_left = list(down_stages())
    out_oth, got_t = over_core(out_other), over_core(send_t)
    sent = down_stage(*down_left.pop(0), d_low, out_oth, got_t)
    sent += mlp_sum.second(*sent)
    n = half // 4
    arrays = [d_low, d_high, d_attn]
    arrays = [
        keep_t, got_t, *arrays, *[over_core(a) for a in arrays], grad_gains, over_core(grad_gains), attn_order
    ]
    attn_grads = call(
        functools.partial(attn_grad_kernel, wide=wide, gain_at=nqkv),
        [shape((n, full))] * 4,
        grid=(1,),
        in_specs=by_once(*arrays) + [anywhere] * len(sent),
        out_specs=[whole(n, full)] * 4,
        vmem=32 << 20,
    )(*arrays, *sent)
    attn_sum = Reduction(*[a.reshape(1, 1, 2, block, full) for a in attn_grads])
    for i in range(seqs):
        output = call(
            sum_kernel, shape((rows, features)), grid=(1,),
            in_specs=[rows_at(i, features), rows_at(i, features), rows_at(i, padded)]
            + [anywhere] * (2 if i else 1),
            out_specs=rows_at(i, features), input_output_aliases={4: 0} if i else {},
        )(out_part, mixed, out_oth, attn_grads[0], *([output] if i else []))
    sent = mlp_sum.z(attn_grads[0], output)
    sent = attn_sum.second(*sent)
    for step in range(z_bits):
        if step:
            sent = mlp_sum.z(*sent)
        if down_left:
            sent = down_stage(*down_left.pop(0), *sent)
        sent = attn_sum.z(*sent)
    while down_left:
        sent = down_stage(*down_left.pop(0), *sent)
    down_mine = fold(down_parts, 1, 0, sent)
    down_from = over_rep(down_mine)
    mlp_mine, mlp_from = mlp_sum.last(down_mine)
    attn_mine, attn_from = attn_sum.last(mlp_mine)

    grad_gate, grad_up = call(
        functools.partial(shards_kernel, quarter=quarter, fr=fr),
        [shape((dr, 2 * half_ff), F32)] * 2,
        grid=(1,),
        in_specs=[in_smem] + by_once(*[mlp_mine] * 4), out_specs=[whole(dr, 2 * half_ff)] * 2,
    )(place, mlp_mine, mlp_from, over_core(mlp_mine), over_core(mlp_from))
    grad_down = call(
        functools.partial(fold_kernel, count=2), shape((1, fr, features), F32), grid=(1,),
        in_specs=by_once(down_mine, down_mine) + [anywhere], out_specs=whole(1, fr, features), vmem=ADD_VMEM,
    )(down_mine, down_from, grad_gate)
    attn_dims = ((dr, nq), (dr, nk), (dr, nk), (1, dr), (1, dr), (dr, features))
    grad_query, grad_key, grad_value, grad_gain_one, grad_gain_two, grad_out = call(
        functools.partial(attn_shards_kernel, quarter=quarter, wide=wide),
        [shape(dims, F32) for dims in attn_dims],
        grid=(1,),
        in_specs=[in_smem] + by_once(attn_mine, attn_mine) + [anywhere] * 2,
        out_specs=[whole(*dims) for dims in attn_dims],
    )(place, attn_mine, attn_from, grad_down, grad_gate)
    dims = tokens.shape
    return (
        output.reshape(dims), grad_tokens.reshape(dims), grad_gain_one.reshape(dr), grad_query, grad_key, grad_value,
        grad_out, grad_gain_two.reshape(dr), grad_gate, grad_up, grad_down[0],
    )


def solution(mesh):
    data = P(None, ("rep", "shard"), None, None)
    vector, matrix = P("shard"), P("shard", None)
    weights = (vector, matrix, matrix, matrix, matrix, vector, matrix, matrix, matrix)
    return jax.shard_map(
        on_device,
        mesh=mesh,
        in_specs=(data, data) + weights,
        out_specs=(data, data) + weights,
        check_vma=False,
    )
```
